32 devices in a mesh: dp: 8 (over z, y), head: 4 (over x, core).
Axes of the slice: x: 2, y: 2, z: 4, core: 2. Of those that a mesh axis runs over, the one named last changes fastest.
Arguments:
- tokens: bfloat16 [16, 1024, 512], P('dp', 'head'), may hold values from -6 to 6
- seq_counts: int32 [16], P('dp'), may hold values from 1 to 4, as said below
- seq_lengths: int32 [16, 4], P('dp'), may hold values from 0 to 1024, as said below
- query_key_value_weight: bfloat16 [2, 512, 1536], replicated, may hold values from -0.25 to 0.25
- output_weight: bfloat16 [2, 512, 512], replicated, may hold values from -3 to 3
- up_weight: bfloat16 [2, 512, 2048], replicated, may hold values from -0.25 to 0.25
- down_weight: bfloat16 [2, 2048, 512], replicated, may hold values from -0.125 to 0.125
- norm_gain: float32 [5, 512], replicated, may hold values from 0.5 to 1.5
- norm_bias: float32 [5, 512], replicated, may hold values from -1.5 to 1.5
- cotangent: bfloat16 [16, 1024, 512], P('dp', 'head'), may hold values from -6 to 6
Outputs:
- result: float32 [16, 1024, 512], P('dp', 'head')
- grad_tokens: float32 [16, 1024, 512], P('dp', 'head')
- grad_qkv: float32 [2, 512, 1536], P(None, 'dp')
- grad_out: float32 [2, 512, 512], P(None, 'dp')
- grad_up: float32 [2, 512, 2048], P(None, 'dp')
- grad_down: float32 [2, 2048, 512], P(None, 'dp')
- grad_gain: float32 [5, 512], P(None, 'dp')
- grad_bias: float32 [5, 512], P(None, 'dp')
The draws below stay inside these ranges and needn't reach their ends.
Inputs may be any that keep to these rules, and one draw needn't show every extreme that they name: `seq_counts`: each entry is 1 or 4, the number of sequences in that slot of 1024 tokens; among the slots of one index of dp at least one holds a single sequence. `seq_lengths`: A slot with one sequence has its length in entry 0, from 512 to 1024, and zeros beside it; a slot with four has lengths of 1 to 256. Among the slots of one index of dp one holds a single sequence of 1024 tokens.
All inputs are finite; a program needn't handle non-finite values.
Results may differ from the reference program's by a relative error of at most 0.018.
Values may be sent and summed in bfloat16 or wider, within the bound.
A program may use at most 128 MiB of HBM per device.

```python
import math
import jax
import jax.numpy as jnp
from jax import lax

D = 512
HEADS = 8
DH = 64
FF = 2048
LAYERS = 2
SLOT_LEN = 1024
SLOTS_DP = 2
SEG = 256
NORMS = 5
SLOTS = 16


def slot_plan(key):
    base_key = jax.random.fold_in(key, 11)
    key_many, key_pick, key_long, key_short = jax.random.split(base_key, 4)
    several = jax.random.randint(key_many, (SLOTS,), 0, 2)
    chosen = jax.random.randint(key_pick, (SLOTS // SLOTS_DP,), 0, SLOTS_DP)
    slot_ids = jnp.arange(SLOTS, dtype=jnp.int32)
    forced = slot_ids % SLOTS_DP == jnp.repeat(chosen, SLOTS_DP)
    several = jnp.where(forced, 0, several)
    counts = (1 + 3 * several).astype(jnp.int32)
    long_len = jax.random.randint(key_long, (SLOTS,), SLOT_LEN // 2, SLOT_LEN + 1)
    long_len = jnp.where(forced, SLOT_LEN, long_len)
    short_len = jax.random.randint(key_short, (SLOTS, 4), 1, SEG + 1)
    column = jnp.arange(4, dtype=jnp.int32)[None, :]
    single = jnp.where(column == 0, long_len[:, None], 0)
    lengths = jnp.where(several[:, None] == 1, short_len, single).astype(jnp.int32)
    return (counts, lengths)


def draw_seq_counts(key, part):
    counts, lengths = slot_plan(key)
    return counts


def draw_seq_lengths(key, part):
    counts, lengths = slot_plan(key)
    return lengths


def level_of(stream_key, shape, shards, low, largest):
    loudness, own = 1.0, jax.random.fold_in(stream_key, 6)
    for dim, shards_of in shards:
        steps = jnp.exp(jax.random.uniform(jax.random.fold_in(own, dim), (shards_of,), jnp.float32, low / len(shards), largest / len(shards)))
        loudness = loudness * jnp.repeat(steps, shape[dim] // shards_of).reshape([-1 if axis == dim else 1 for axis in range(len(shape))])
    return loudness


def bell_draw(own_key, extent, deviation, most, pieces=(), kind=jnp.bfloat16):
    entries = deviation * jax.random.normal(own_key, extent, jnp.float32)
    if pieces:
        entries = entries * level_of(own_key, extent, pieces, -0.22, 0.18)
    return jnp.clip(entries, -most, most).astype(kind)


def setup_inputs(seed: int = 0) -> dict:
    arg_keys = jax.random.split(jax.random.key(seed), 11)
    return {
        "tokens": bell_draw(arg_keys[0], (SLOTS, SLOT_LEN, D), 1.0, 6.0, ((0, 8), (1, 4))),
        "seq_counts": draw_seq_counts(jax.random.fold_in(arg_keys[10], 71), 0),
        "seq_lengths": draw_seq_lengths(jax.random.fold_in(arg_keys[10], 71), 0),
        "query_key_value_weight": bell_draw(arg_keys[3], (LAYERS, D, 3 * D), D ** -0.5, 0.25),
        "output_weight": bell_draw(arg_keys[4], (LAYERS, D, D), (max(1, D // 128)) ** -0.5, 3.0),
        "up_weight": bell_draw(arg_keys[5], (LAYERS, D, FF), D ** -0.5, 0.25),
        "down_weight": bell_draw(arg_keys[6], (LAYERS, FF, D), FF ** -0.5, 0.125),
        "norm_gain": jnp.clip(1.0 + 0.1 * jax.random.normal(arg_keys[7], (NORMS, D), jnp.float32), 0.5, 1.5),
        "norm_bias": bell_draw(arg_keys[8], (NORMS, D), 0.3, 1.5, (), jnp.float32),
        "cotangent": bell_draw(arg_keys[9], (SLOTS, SLOT_LEN, D), 1.0, 6.0, ((0, 8), (1, 4))),
    }


EPS = 1e-05
NEG = -1e+30
HIGH_PRECISION = lax.Precision.HIGHEST

@jax.custom_vjp
def low(v):
    return lax.optimization_barrier(v.astype(jnp.bfloat16)).astype(jnp.float32)

@jax.custom_vjp
def lowered_backward(v):
    return v

def low_keep(v):
    return (low(v), None)

def low_pass(kept, grad):
    return (grad,)

def back_keep(v):
    return (v, None)

def back_low(kept, grad):
    return (low(grad),)
low.defvjp(low_keep, low_pass)
lowered_backward.defvjp(back_keep, back_low)

def norm_apply(values, gain_row, bias_row):
    centred = values - lax.optimization_barrier(jnp.mean(values, axis=-1, keepdims=True))
    spread = lax.optimization_barrier(jnp.mean(centred * centred, axis=-1, keepdims=True))
    return centred * lax.rsqrt(spread + EPS) * gain_row + bias_row

def smooth(values):
    return jax.nn.gelu(values, approximate=False)

def slot_masks(counts, lengths, full_len, quarter):
    positions = jnp.arange(full_len, dtype=jnp.int32)
    several = counts[:, None] == 4
    segment = jnp.where(several, positions[None, :] // quarter, 0)
    within = jnp.where(several, positions[None, :] % quarter, positions[None, :])
    choose = segment[:, :, None] == jnp.arange(4, dtype=jnp.int32)[None, None, :]
    limits = lax.optimization_barrier(jnp.sum(jnp.where(choose, lengths[:, None, :], 0), axis=2))
    return (segment, within < limits)

def attend_slot(packed_tokens, segment, usable):
    shaped = packed_tokens.reshape(SLOT_LEN, HEADS, 3, DH)
    query_rows = shaped[:, :, 0]
    key_rows = shaped[:, :, 1]
    value_rows = shaped[:, :, 2]
    scores = jnp.einsum('qhd,khd->hqk', query_rows, key_rows, precision=HIGH_PRECISION) * (1.0 / math.sqrt(DH))
    scores = lowered_backward(scores)
    allowed = (segment[:, None] == segment[None, :]) & usable[None, :]
    scores = jnp.where(allowed[None], scores, NEG)
    top_score = lax.optimization_barrier(jnp.max(scores, axis=2, keepdims=True))
    weights = jnp.exp(scores - top_score)
    probs = weights / lax.optimization_barrier(jnp.sum(weights, axis=2, keepdims=True))
    output = jnp.einsum('hqk,khd->qhd', low(probs), value_rows, precision=HIGH_PRECISION)
    return output.reshape(SLOT_LEN, D)

def attend_packet(packet):
    return attend_slot(packet[0], packet[1], packet[2])

def forward(tokens, query_key_value_weight, output_weight, up_weight, down_weight, norm_gain, norm_bias, segment, usable):
    normed = tokens
    dual_sum = tokens
    for layer_index in range(LAYERS):
        lowered_input = low(normed)
        packed_tokens = jnp.einsum('tog,gr->tor', lowered_input, query_key_value_weight[layer_index], precision=HIGH_PRECISION)
        packed_tokens = low(lowered_backward(packed_tokens))
        attended_rows = lax.map(jax.checkpoint(attend_packet), (packed_tokens, segment, usable))
        attended_rows = low(lowered_backward(attended_rows))
        branch_output = lowered_backward(jnp.einsum('mki,ib->mkb', attended_rows, output_weight[layer_index], precision=HIGH_PRECISION))
        dual_sum = dual_sum + branch_output
        normed = norm_apply(normed + branch_output, norm_gain[2 * layer_index], norm_bias[2 * layer_index])
        lowered_middle = low(normed)
        hidden_state = lowered_backward(jnp.einsum('irj,jc->irc', lowered_middle, up_weight[layer_index], precision=HIGH_PRECISION))
        active_tokens = low(smooth(hidden_state))
        branch_output = lowered_backward(jnp.einsum('uqi,ip->uqp', active_tokens, down_weight[layer_index], precision=HIGH_PRECISION))
        dual_sum = dual_sum + branch_output
        normed = norm_apply(normed + branch_output, norm_gain[2 * layer_index + 1], norm_bias[2 * layer_index + 1])
    return normed + norm_apply(dual_sum, norm_gain[2 * LAYERS], norm_bias[2 * LAYERS])

def reference(tokens, seq_counts, seq_lengths, query_key_value_weight, output_weight, up_weight, down_weight, norm_gain, norm_bias, cotangent):
    segment, usable = slot_masks(seq_counts, seq_lengths, SLOT_LEN, SEG)

    def wrapped(tokens_in, qkv_in, out_in, up_in, down_in, gain_in, bias_in):
        return forward(tokens_in, qkv_in, out_in, up_in, down_in, gain_in, bias_in, segment, usable)
    result, pullback = jax.vjp(wrapped, tokens.astype(jnp.float32), query_key_value_weight.astype(jnp.float32), output_weight.astype(jnp.float32), up_weight.astype(jnp.float32), down_weight.astype(jnp.float32), norm_gain.astype(jnp.float32), norm_bias.astype(jnp.float32))
    gradients = pullback(cotangent.astype(jnp.float32))
    return (result, gradients[0], gradients[1], gradients[2], gradients[3], gradients[4], gradients[5], gradients[6])
```

```python
import math
from functools import partial
from types import SimpleNamespace

import jax
import jax.numpy as jnp
import numpy as np
from jax import lax
from jax.experimental import pallas as pl
from jax.experimental.pallas import tpu as pltpu
from jax.sharding import PartitionSpec as P

HEADS = 8
EPS = 1e-05
NEG = -1e30
LOG2E = 1.4426950408889634
BF = jnp.bfloat16
F32 = jnp.float32
MESH = pl.DeviceIdType.MESH


EVENTS = {
    ("up", 1): [("D", 1)],
    ("out", 1): [("U", 1)],
    (1, 1): [("O", 1)],
    (2, 1): [("D", 1)],
    (3, 1): [("U", 1), ("O", 1)],
    ("down", 0): [("Q", 1), ("D", 1)],
    ("up", 0): [("D", 0), ("U", 1), ("O", 1)],
    ("out", 0): [("U", 0), ("Q", 1)],
    (0, 0): [("O", 0)],
    (1, 0): [("D", 0), ("Q", 1)],
    (2, 0): [("U", 0), ("O", 0)],
    (3, 0): [("D", 0)],
}


def dot(a, b):
    return jnp.dot(a, b, preferred_element_type=F32)


def dot_t(a, b):
    return lax.dot_general(a, b, (((1,), (1,)), ((), ())), preferred_element_type=F32)


def dot_lt(a, b):
    return lax.dot_general(a, b, (((0,), (0,)), ((), ())), preferred_element_type=F32)


def gelu_parts(h):
    t = 1.0 / (1.0 + (0.3275911 * math.sqrt(0.5)) * jnp.abs(h))
    e = jnp.exp2(h * h * (-0.5 * LOG2E))
    poly = 0.5 * 1.061405429
    for a in (-1.453152027, 1.421413741, -0.284496736, 0.254829592):
        poly = poly * t + 0.5 * a
    q = poly * t * e
    phi = jnp.where(h >= 0.0, 1.0 - q, q)
    return h * phi, phi + h * (e * (1.0 / math.sqrt(2.0 * math.pi)))


def split3(v):
    hi = v.astype(BF).astype(F32)
    rest = v - hi
    mid = rest.astype(BF).astype(F32)
    return hi, mid, rest - mid


class Plan:
    def __init__(self, layers, tl, width, ff, nd):
        self.L, self.TL, self.D, self.FF, self.nd = layers, tl, width, ff, nd
        self.T = 2 * tl
        self.nb = nd.bit_length() - 1
        self.r = width // nd // 4
        self.scratch = {}
        self.n_sem = 0

    def add(self, name, shape, dtype):
        self.scratch[name] = pltpu.VMEM(tuple(shape), dtype)

    def sem(self):
        self.n_sem += 1
        return self.n_sem - 1


def axes_of(nb):
    return [("head", 1), ("head", 2)] + [("dp", 1 << b) for b in reversed(range(nb))]


def stages_of(kind, layer, nb):
    d = [("dp", 1 << b) for b in range(nb)]
    c, x = ("head", 1), ("head", 2)
    y, z = d[:1], d[1:]
    return [s for s in ([c], [x] + y, z) if s]


class Chunk:
    def __init__(self, plan, kind, layer):
        self.kind, self.layer, self.plan = kind, layer, plan
        self.name = f"{kind}{layer}"
        nb, r = plan.nb, plan.r
        rows, cols = {
            "U": (r, plan.FF),
            "O": (r, plan.D),
            "Q": (r, 3 * plan.D),
            "D": (plan.D // 4, plan.FF // plan.nd),
        }[kind]
        self.rows, self.cols = rows, cols
        self.axes = axes_of(nb)
        self.stages = stages_of(kind, layer, nb)
        plan.add("G" + self.name, [2] * len(self.axes) + [rows, cols], BF)
        self.out_shape = (cols, rows) if kind == "D" else (rows, cols)
        plan.add("P" + self.name, self.out_shape, BF)
        self.patterns, self.sems = [], []
        left = len(self.axes)
        for s, dims in enumerate(self.stages):
            left -= len(dims)
            pats = [
                [dims[i] for i in range(len(dims)) if m >> i & 1] for m in range(1, 1 << len(dims))
            ]
            self.patterns.append(pats)
            plan.add(f"R{self.name}_{s}", [len(pats)] + [2] * left + [rows, cols], BF)
            self.sems.append([(plan.sem(), plan.sem()) for _ in pats])
        self.last_sems = [(plan.sem(), plan.sem()) for _ in range(3)]
        self.local_sem = plan.sem()
        self.at = 0

    def index(self, env, stage, flipped):
        done = [a for s in self.stages[:stage] for a in s]
        out = []
        for a in self.axes:
            bit = env.bits[a]
            if a in done:
                out.append(bit)
            elif stage < len(self.stages) and a in self.stages[stage]:
                out.append(1 - bit if a in flipped else bit)
            else:
                out.append(slice(None))
        return tuple(out)

    def copies(self, env, stage):
        for i, (pat, (ss, rs)) in enumerate(zip(self.patterns[stage], self.sems[stage])):
            yield pltpu.make_async_remote_copy(
                src_ref=env.ref["G" + self.name].at[self.index(env, stage, pat)],
                dst_ref=env.ref[f"R{self.name}_{stage}"].at[i],
                send_sem=env.sems.at[ss],
                recv_sem=env.sems.at[rs],
                device_id=env.partner(pat),
                device_id_type=MESH,
            )

    def start(self, env, stage):
        for c in self.copies(env, stage):
            c.start()

    def finish(self, env, stage):
        for c in self.copies(env, stage):
            c.wait()
        own = self.index(env, stage, ())
        g = env.ref["G" + self.name]
        got = env.ref[f"R{self.name}_{stage}"]

        def summed(at):
            piece = iter(at)
            here = tuple(next(piece) if isinstance(o, slice) else o for o in own)
            total = g[here].astype(F32)
            for i in range(len(self.patterns[stage])):
                total = total + got[(i, *at)].astype(F32)
            return total

        if stage < len(self.stages) - 1:
            left = sum(isinstance(o, slice) for o in own)
            for at in np.ndindex(*[2] * left):
                piece = iter(at)
                here = tuple(next(piece) if isinstance(o, slice) else o for o in own)
                g[here] = summed(at).astype(BF)
            return
        total = summed(())
        if self.kind == "D":
            total = total.T
        if self.kind == "Q":
            d = self.plan.D
            lo = lax.broadcasted_iota(jnp.int32, (self.rows, 128), 1) < 64
            tiles = []
            for p in range(HEADS // 2):
                q = total[:, 128 * p : 128 * p + 128]
                k0 = pltpu.roll(total[:, d + 256 * p : d + 256 * p + 128], 64, 1)
                k1 = pltpu.roll(total[:, d + 256 * p + 128 : d + 256 * p + 256], 64, 1)
                tiles += [jnp.where(lo, q, k0), jnp.where(lo, k0, q), k1]
            total = jnp.concatenate(tiles, axis=1)
        env.ref["P" + self.name][...] = total.astype(BF)

    def place(self, env):
        out = env.out[self.kind]
        quarter = env.head
        if self.kind == "D":
            return out.at[self.layer, :, pl.ds(pl.multiple_of(quarter * self.rows, self.rows), self.rows)]
        return out.at[self.layer, quarter]

    def spread(self, env):
        src = env.ref["P" + self.name]
        yield pltpu.make_async_copy(src, self.place(env), env.sems.at[self.local_sem])
        pats = ([("head", 1)], [("head", 2)], [("head", 1), ("head", 2)])
        for pat, (ss, rs) in zip(pats, self.last_sems):
            yield pltpu.make_async_remote_copy(
                src_ref=src,
                dst_ref=self.place(env),
                send_sem=env.sems.at[ss],
                recv_sem=env.sems.at[rs],
                device_id=env.partner(pat),
                device_id_type=MESH,
            )

    def advance(self, env):
        n = len(self.stages)
        if self.at > n:
            return
        if self.at > 0:
            self.finish(env, self.at - 1)
        if self.at < n:
            self.start(env, self.at)
        else:
            for c in self.spread(env):
                c.start()
        self.at += 1

    def complete(self, env):
        while self.at <= len(self.stages):
            self.advance(env)
        for c in self.spread(env):
            c.wait()


def make_plan(layers, tl, width, ff, nd):
    plan = Plan(layers, tl, width, ff, nd)
    t, n = plan.T, HEADS
    add = plan.add
    add("x", (t, width), F32)
    add("dual", (t, width), F32)
    add("br", (t, width), F32)
    add("cot", (2, tl, width), BF)
    add("E", (4 * tl, 128), BF)
    add("EQ", (t, 128), BF)
    add("wq", (layers, width, width), BF)
    add("wkv", (layers, width, 2 * width), BF)
    add("wo", (layers, n // 2, 2, 64, width), BF)
    add("wup", (width, ff), BF)
    add("wdown", (ff, width), BF)
    add("low_in", (layers, 2, tl, width), BF)
    add("KV", (layers, n, 4 * tl, 128), BF)
    add("Q", (layers, n // 2, t, 128), BF)
    add("QX", (layers, t, 128), BF)
    add("att", (layers, t, width), BF)
    add("n_attn", (layers, t, width), BF)
    add("RS", (t, 128), F32)
    add("low_mid", (layers, t, width), BF)
    add("n_ffn", (layers, t, width), BF)
    add("act", (t, ff), BF)
    add("gp", (t, ff), BF)
    add("gb", (t, width), BF)
    add("ksend", (n, t, 128), BF)
    add("krecv", (n, t, 128), BF)
    add("gpk", (t, 3 * width), BF)
    add("GB", (16, width), F32)
    nbits = 2 + plan.nb
    add("GBR", (nbits, 16, width), F32)
    plan.chunks = {}
    for layer in reversed(range(layers)):
        for kind in "DUOQ":
            plan.chunks[kind, layer] = Chunk(plan, kind, layer)
    plan.misc = {}
    for name in (
        ["tok_l", "cot_l", "res_l", "gtok_l", "act_s", "gp_s", "act_b", "gp_b", "gb_out"]
        + [f"{w}{l}{i}" for l in range(layers) for w in ("wqkv", "wo0", "wo1", "wup", "wdown") for i in "ab"]
    ):
        plan.misc[name] = plan.sem()
    for name in (
        ["tok_r", "cot_r", "res_r", "gtok_r"]
        + [f"kv{l}{i}" for l in range(layers) for i in range(2)]
        + [f"dkv{l}{h}" for l in range(layers) for h in range(n)]
        + [f"GB{i}" for i in range(nbits)]
    ):
        plan.misc[name] = (plan.sem(), plan.sem())
    return plan


def kernel(plan, names, *refs):
    (tokens, counts, lengths, wqkv, wo, wup, wdown, gain, bias, cot) = refs[:10]
    (o_res, o_gtok, o_q, o_o, o_u, o_d, o_gb, s_act, s_gp) = refs[10:19]
    ref = dict(zip(names, refs[19:-1]))
    sems = refs[-1]
    r = SimpleNamespace(**{k: v for k, v in ref.items()})
    L, T, TL, D, FF, nb = plan.L, plan.T, plan.TL, plan.D, plan.FF, plan.nb
    n_heads = HEADS
    dp, head = lax.axis_index("dp"), lax.axis_index("head")
    core, xc = head % 2, head // 2
    bits = {("head", 1): core, ("head", 2): xc}
    for b in range(nb):
        bits["dp", 1 << b] = (dp // (1 << b)) % 2

    def partner(pat):
        d, h = dp, head
        for axis, bit in pat:
            v = bits[axis, bit]
            if axis == "dp":
                d = d + bit * (1 - 2 * v)
            else:
                h = h + bit * (1 - 2 * v)
        return (d, h)

    env = SimpleNamespace(
        ref=ref,
        sems=sems,
        bits=bits,
        partner=partner,
        head=head,
        out={"Q": o_q, "O": o_o, "U": o_u, "D": o_d},
    )
    CORE, XP = [("head", 1)], [("head", 2)]

    greet = [CORE, XP, CORE + XP]
    for ch in plan.chunks.values():
        for pats in ch.patterns:
            for pat in pats:
                if pat not in greet:
                    greet.append(pat)
    for b in range(nb):
        if [("dp", 1 << b)] not in greet:
            greet.append([("dp", 1 << b)])
    barrier = pltpu.get_barrier_semaphore()
    for pat in greet:
        pl.semaphore_signal(barrier, inc=1, device_id=partner(pat), device_id_type=MESH)

    def local(src, dst, name):
        return pltpu.make_async_copy(src, dst, sems.at[plan.misc[name]])

    def remote(src, dst, name, pat):
        ss, rs = plan.misc[name]
        return pltpu.make_async_remote_copy(
            src_ref=src,
            dst_ref=dst,
            send_sem=sems.at[ss],
            recv_sem=sems.at[rs],
            device_id=partner(pat),
            device_id_type=MESH,
        )

    stage_ref = [r.act, r.gp]
    raw = [
        local(wqkv.at[l], stage_ref[l].at[:, pl.ds(0, 3 * D)], f"wqkv{l}a") for l in range(L)
    ]
    raw[0].start()
    tok_l = local(tokens.at[xc], r.low_in.at[0, xc], "tok_l")
    tok_l.start()
    cot_l = local(cot.at[xc], r.cot.at[xc], "cot_l")
    wos = []
    for l in range(L):
        wos.append(
            [
                local(wo.at[l, :, e], r.wo.at[l, :, 1 - e], f"wo{e}{l}a")
                for e in range(2)
            ]
        )
    ups = [[local(wup.at[l], r.wup, f"wup{l}{i}") for i in "ab"[: L - l]] for l in range(L)]
    downs = [[local(wdown.at[l], r.wdown, f"wdown{l}{i}") for i in "ab"[: L - l]] for l in range(L)]
    pl.semaphore_wait(barrier, len(greet))
    tok_r = remote(tokens.at[1 - xc], r.low_in.at[0, xc], "tok_r", XP)
    tok_r.start()
    for c in raw[1:] + wos[0] + [ups[0][0], downs[0][0]] + sum(wos[1:], []) + [cot_l]:
        c.start()
    cot_r = remote(cot.at[1 - xc], r.cot.at[xc], "cot_r", XP)
    cot_r.start()

    lane = lax.broadcasted_iota(jnp.int32, (TL, 128), 1)
    row = lax.broadcasted_iota(jnp.int32, (TL, 128), 0)
    count = counts[xc]
    several = count == 4
    for j in range(4):
        quarter = core + 2 * j if j < 2 else (1 - core) + 2 * (j - 2)
        limit_one = lengths[xc, 0] - TL * quarter
        limit = jnp.where(several, lengths[xc, quarter], limit_one)
        usable = row < limit
        same = jnp.logical_or(lane == quarter, jnp.logical_not(several))
        ok = jnp.logical_and(usable, same)
        tile = jnp.where(lane < 4, jnp.where(ok, 0.0, NEG), jnp.where(lane < 32, 1.0, 0.0))
        r.E[pl.ds(TL * j, TL), :] = tile.astype(BF)
    for b in range(2):
        tile = jnp.where(lane == core + 2 * b, 1.0, 0.0).astype(BF)
        r.EQ[pl.ds(TL * b, TL), :] = tile
        for l in range(L):
            r.QX[l, pl.ds(TL * b, TL), :] = tile

    low_half = lax.broadcasted_iota(jnp.int32, (D, 128), 1) < 64
    for l in range(L):
        raw[l].wait()

        def sort_pair(p, _, l=l):
            cols = lambda i: pl.ds(pl.multiple_of(p * 384 + 128 * i, 128), 128)
            t0 = stage_ref[l][:, cols(0)].astype(F32)
            t1 = stage_ref[l][:, cols(1)].astype(F32)
            t2 = stage_ref[l][:, cols(2)].astype(F32)
            r0, r1, r2 = (pltpu.roll(t, 64, 1) for t in (t0, t1, t2))
            r.wq[l, :, pl.ds(pl.multiple_of(p * 128, 128), 128)] = jnp.where(low_half, t0, t1).astype(BF)
            r.wkv[l, :, pl.ds(pl.multiple_of(p * 256, 128), 128)] = jnp.where(low_half, r0, r1).astype(BF)
            r.wkv[l, :, pl.ds(pl.multiple_of(p * 256 + 128, 128), 128)] = r2.astype(BF)
            return 0

        lax.fori_loop(0, n_heads // 2, sort_pair, 0)

    lane1 = lax.broadcasted_iota(jnp.int32, (1, 128), 1)
    m_lo = jnp.where(lane1 < 64, 1.0, 0.0).astype(BF)
    m_hi = jnp.where(lane1 < 64, 0.0, 1.0).astype(BF)
    m_of = [m_lo, m_hi]
    CH = 64

    def rows_of(i):
        return pl.ds(pl.multiple_of(i * CH, CH), CH)

    def normalise(v):
        mu = jnp.mean(v, axis=1, keepdims=True)
        cen = v - mu
        var = jnp.mean(cen * cen, axis=1, keepdims=True)
        rs = lax.rsqrt(var + EPS)
        return cen * rs, rs

    def norm_back(g, n, rs, gain_row):
        h = g * gain_row
        return rs * (
            h - jnp.mean(h, axis=1, keepdims=True) - n * jnp.mean(h * n, axis=1, keepdims=True)
        )

    def keep_rs(col, rows, rs):
        lanes = lax.broadcasted_iota(jnp.int32, (CH, 128), 1)
        r.RS[rows, :] = jnp.where(lanes == col, rs, r.RS[rows, :])

    def fold(v):
        return jnp.sum(v.reshape(CH // 8, 8, D), axis=0)

    r.RS[...] = jnp.zeros((T, 128), F32)
    tok_l.wait()
    tok_r.wait()
    for b in range(2):
        v = r.low_in[0, b].astype(F32)
        r.x[pl.ds(TL * b, TL), :] = v
        r.dual[pl.ds(TL * b, TL), :] = v

    hold = {}

    def forward(l):
        if l > 0:
            r.low_in[l] = r.x[...].astype(BF).reshape(2, TL, D)
        low = r.low_in[l].reshape(T, D)
        sends = []
        hh = n_heads // 2
        for half in range(2):
            kv = dot(low, r.wkv[l, :, D * half : D * half + D]).astype(BF)
            for i in range(hh):
                r.KV[l, half * hh + i, 0:T, :] = kv[:, 128 * i : 128 * i + 128]
            c = remote(
                r.KV.at[l, pl.ds(half * hh, hh), pl.ds(0, T)],
                r.KV.at[l, pl.ds(half * hh, hh), pl.ds(T, T)],
                f"kv{l}{half}",
                CORE,
            )
            c.start()
            sends.append(c)
        q = (dot(low, r.wq[l]) * (LOG2E / 8.0)).astype(BF)
        for p in range(n_heads // 2):
            r.Q[l, p] = q[:, 128 * p : 128 * p + 128]
        sends[0].wait()
        sends[1].wait()
        lane_t = lax.broadcasted_iota(jnp.int32, (TL, 128), 1)

        def attend(p, _):
            outs = []
            for e in range(2):
                h = 2 * p + e
                kve = jnp.concatenate([r.KV[l, h], r.E[...]], axis=1)
                for b in range(2):
                    rows = pl.ds(TL * b, TL)
                    eq = r.EQ[rows, :]
                    qe = jnp.concatenate([r.Q[l, p, rows, :] * m_of[e], eq], axis=1)
                    s = dot_t(qe, kve)
                    top = jnp.max(s, axis=1, keepdims=True)
                    pe = jnp.exp2(s - top).astype(BF)
                    o = dot(pe, kve)
                    total = o[:, 132:133]
                    lse = top + jnp.log(total) * LOG2E
                    outs.append(o[:, :128] * (1.0 / total))
                    hi, mid, lo = split3(-lse)
                    at = lane_t - (8 + 3 * h)
                    old = r.QX[l, rows, :].astype(F32)
                    tile = jnp.where(at == 0, hi, jnp.where(at == 1, mid, jnp.where(at == 2, lo, old)))
                    r.QX[l, rows, :] = tile.astype(BF)
            sel = lane_t < 64
            for b in range(2):
                r.att[l, pl.ds(TL * b, TL), pl.ds(pl.multiple_of(p * 128, 128), 128)] = jnp.where(
                    sel, outs[2 + b], outs[b]
                ).astype(BF)
            return 0

        lax.fori_loop(0, n_heads // 2, attend, 0)
        if l == 0:
            for l2 in range(L):
                for c in wos[l2]:
                    c.wait()
        r.br[...] = dot(r.att[l], r.wo[l].reshape(D, D))

        def after_attn(i, _):
            rows = rows_of(i)
            br = r.br[rows, :]
            r.dual[rows, :] = r.dual[rows, :] + br
            n, rs = normalise(r.x[rows, :] + br)
            r.n_attn[l, rows, :] = n.astype(BF)
            keep_rs(2 * l, rows, rs)
            y = n * gain[2 * l : 2 * l + 1, :] + bias[2 * l : 2 * l + 1, :]
            r.x[rows, :] = y
            r.low_mid[l, rows, :] = y.astype(BF)
            return 0

        lax.fori_loop(0, T // CH, after_attn, 0)
        ups[l][0].wait()
        downs[l][0].wait()
        if l > 0:
            hold["act_s"].wait()
            hold["gp_s"].wait()
        low = r.low_mid[l]
        fb = 512

        def ffn_cols(j, _):
            cols = pl.ds(pl.multiple_of(j * fb, fb), fb)
            a, gp = gelu_parts(dot(r.low_mid[l], r.wup[:, cols]))
            r.act[:, cols] = a.astype(BF)
            r.gp[:, cols] = gp.astype(BF)
            return 0

        lax.fori_loop(0, FF // fb, ffn_cols, 0)
        r.br[...] = dot(r.act[...], r.wdown[...])
        if l < L - 1:
            hold["act_s"] = local(r.act, s_act.at[l], "act_s")
            hold["gp_s"] = local(r.gp, s_gp.at[l], "gp_s")
            hold["act_s"].start()
            hold["gp_s"].start()
            ups[l + 1][0].start()
            downs[l + 1][0].start()

        def after_ffn(i, _):
            rows = rows_of(i)
            br = r.br[rows, :]
            r.dual[rows, :] = r.dual[rows, :] + br
            n, rs = normalise(r.x[rows, :] + br)
            r.n_ffn[l, rows, :] = n.astype(BF)
            keep_rs(2 * l + 1, rows, rs)
            r.x[rows, :] = n * gain[2 * l + 1 : 2 * l + 2, :] + bias[2 * l + 1 : 2 * l + 2, :]
            return 0

        lax.fori_loop(0, T // CH, after_ffn, 0)

    for l in range(L):
        forward(l)

    cot_l.wait()
    cot_r.wait()
    k = 2 * L
    zero = jnp.zeros((8, D), F32)
    r.GB[...] = jnp.zeros((16, D), F32)

    def put_gb(row, acc):
        r.GB[row : row + 1, :] = jnp.sum(acc[0], axis=0, keepdims=True)
        r.GB[8 + row : 9 + row, :] = jnp.sum(acc[1], axis=0, keepdims=True)

    for b in range(2):

        def ending(i, acc, b=b):
            rows = pl.ds(pl.multiple_of(TL * b + i * CH, CH), CH)
            part = pl.ds(pl.multiple_of(i * CH, CH), CH)
            n, rs = normalise(r.dual[rows, :])
            res = r.x[rows, :] + n * gain[k : k + 1, :] + bias[k : k + 1, :]
            g = r.cot[b, part, :].astype(F32)
            r.cot[b, part, :] = res.astype(BF)
            r.x[rows, :] = g
            r.dual[rows, :] = norm_back(g, n, rs, gain[k : k + 1, :])
            return acc[0] + fold(g * n), acc[1] + fold(g)

        acc = lax.fori_loop(0, TL // CH, ending, (zero, zero) if b == 0 else acc)
    put_gb(k, acc)
    res_l = local(r.cot.at[xc], o_res.at[xc], "res_l")
    res_r = remote(r.cot.at[1 - xc], o_res.at[xc], "res_r", XP)
    res_l.start()
    res_r.start()

    def norm_pull(row, n_ref, l):
        def step(i, acc):
            rows = rows_of(i)
            g, n = r.x[rows, :], n_ref[l, rows, :].astype(F32)
            pre = norm_back(g, n, r.RS[rows, row : row + 1], gain[row : row + 1, :])
            r.x[rows, :] = pre
            r.gb[rows, :] = (pre + r.dual[rows, :]).astype(BF)
            return acc[0] + fold(g * n), acc[1] + fold(g)

        put_gb(row, lax.fori_loop(0, T // CH, step, (zero, zero)))

    def store_rows(ch, res, cols, swap=False):
        g = ref["G" + ch.name]
        rr = plan.r
        piece = min(rr, 64)
        for d in range(plan.nd):
            for q in range(4):
                for s in range(0, rr, piece):
                    src = (4 * d + q) * rr + s
                    if swap:
                        src = src ^ 64
                    idx = (q % 2, q // 2) + tuple((d >> b) & 1 for b in reversed(range(nb)))
                    g[idx + (slice(s, s + piece), cols)] = res[src : src + piece].astype(BF)

    def exchange_gb(i):
        pat = ([CORE, XP] + [[("dp", 1 << b)] for b in range(nb)])[i]
        return remote(r.GB, r.GBR.at[i], f"GB{i}", pat)

    order = list(plan.chunks.values())

    def step_chunks(point, l):
        for c in EVENTS.get((point, l), ()):
            plan.chunks[c].advance(env)

    def backward_ffn(l):
        norm_pull(2 * l + 1, r.n_ffn, l)
        if l < L - 1:
            for c in (hold["act_b"], hold["gp_b"], ups[l][1], downs[l][1]):
                c.wait()
        ch = plan.chunks["D", l]
        gbt = r.gb[...].astype(F32).T.astype(BF)
        dcols = ch.cols
        g = ref["G" + ch.name]
        for d in range(plan.nd):
            idx = tuple((d >> b) & 1 for b in reversed(range(nb)))
            step = min(dcols, 512)
            for s in range(0, dcols, step):
                res = dot(gbt, r.act[:, d * dcols + s : d * dcols + s + step])
                for q in range(4):
                    g[(q % 2, q // 2) + idx + (slice(None), slice(s, s + step))] = res[
                        q * ch.rows : (q + 1) * ch.rows
                    ].astype(BF)
        ch.advance(env)
        step_chunks("down", l)
        fb = 512

        def hidden_cols(j, _):
            cols = pl.ds(pl.multiple_of(j * fb, fb), fb)
            gact = dot_t(r.gb[...], r.wdown[cols, :])
            r.gp[:, cols] = (gact * r.gp[:, cols].astype(F32)).astype(BF)
            return 0

        lax.fori_loop(0, FF // fb, hidden_cols, 0)
        ch = plan.chunks["U", l]
        lmt = r.low_mid[l].astype(F32).T.astype(BF)
        for j in range(FF // fb):
            res = dot(lmt, r.gp[:, j * fb : (j + 1) * fb])
            store_rows(ch, res, slice(j * fb, (j + 1) * fb))
        ch.advance(env)
        step_chunks("up", l)
        r.br[...] = dot_t(r.gp[...], r.wup[...])
        r.x[...] = r.x[...] + r.br[...]
        if l > 0:
            hold["act_b"] = local(s_act.at[l - 1], r.act, "act_b")
            hold["gp_b"] = local(s_gp.at[l - 1], r.gp, "gp_b")
            for c in (hold["act_b"], hold["gp_b"], ups[l - 1][1], downs[l - 1][1]):
                c.start()

    def backward_attn(l):
        norm_pull(2 * l, r.n_attn, l)
        ch = plan.chunks["O", l]
        res = dot(r.att[l].astype(F32).T.astype(BF), r.gb[...])
        store_rows(ch, res, slice(None), swap=True)
        ch.advance(env)
        step_chunks("out", l)
        r.gb[...] = dot_t(r.gb[...], r.wo[l].reshape(D, D)).astype(BF)
        lane_t = lax.broadcasted_iota(jnp.int32, (T, 128), 1)
        scale = [
            jnp.where(lane1 < 64, 1.0 / LOG2E, 1.0),
            jnp.where(lane1 < 64, 1.0, 1.0 / LOG2E),
        ]

        def dkv_copy(h, name_h):
            ss, rs = plan.misc[f"dkv{l}0"]
            return pltpu.make_async_remote_copy(
                src_ref=r.ksend.at[h],
                dst_ref=r.krecv.at[h],
                send_sem=sems.at[ss + 2 * h],
                recv_sem=sems.at[rs + 2 * h],
                device_id=partner(CORE),
                device_id_type=MESH,
            )

        def pair(p, _):
            tile = pl.ds(pl.multiple_of(p * 128, 128), 128)
            att = r.att[l, :, tile].astype(F32)
            dqts = []
            for e in range(2):
                h = 2 * p + e
                q = r.Q[l, p] * m_of[e]
                at = lane1 - (8 + 3 * h)
                mine = jnp.where(
                    jnp.logical_or(lane1 < 4, jnp.logical_and(at >= 0, at < 3)), 1.0, 0.0
                ).astype(BF)
                do = r.gb[:, tile] * m_of[1 - e]
                centre = jnp.sum(att * do.astype(F32), axis=1, keepdims=True)
                hi, mid, lo = split3(-centre)
                ed = jnp.where(
                    lane_t == 4, hi, jnp.where(lane_t == 5, mid, jnp.where(lane_t == 6, lo, 0.0))
                ).astype(BF)
                qd = jnp.concatenate(
                    [
                        jnp.concatenate([q, r.QX[l] * mine], axis=1),
                        jnp.concatenate([do, ed], axis=1),
                    ],
                    axis=0,
                )
                dq_in = jnp.concatenate([do, q], axis=0)
                dqt = None
                for j in (2, 3, 0, 1):
                    rows = pl.ds(TL * j, TL)
                    kv = r.KV[l, h, rows, :]
                    ss = dot_t(jnp.concatenate([kv, r.E[rows, :]], axis=1), qd)
                    pr = jnp.exp2(ss[:, :T])
                    ds = (pr * ss[:, T:]).astype(BF)
                    dkv = dot(jnp.concatenate([pr.astype(BF), ds], axis=1), dq_in) * scale[e]
                    part = dot_lt(kv, ds)
                    dqt = part if dqt is None else dqt + part
                    if j >= 2:
                        r.ksend[h, pl.ds(TL * (j - 2), TL), :] = dkv.astype(BF)
                    else:
                        r.gpk[rows, pl.ds(pl.multiple_of(D + h * 128, 128), 128)] = dkv.astype(BF)
                    if j == 3:
                        dkv_copy(h, None).start()
                dqts.append(dqt)
            dq = jnp.concatenate([dqts[0][:64], dqts[1][64:]], axis=0).T * (1.0 / 8.0)
            r.gpk[:, tile] = dq.astype(BF)
            for at in range(n_heads // 2):
                if (at, l) in EVENTS:

                    @pl.when(p == at)
                    def _(at=at):
                        step_chunks(at, l)

            return 0

        lax.fori_loop(0, n_heads // 2, pair, 0)
        for h in range(n_heads):
            dkv_copy(h, None).wait()
            cols = slice(D + 128 * h, D + 128 * h + 128)
            r.gpk[:, cols] = (r.gpk[:, cols].astype(F32) + r.krecv[h].astype(F32)).astype(BF)
        ch = plan.chunks["Q", l]
        lit = r.low_in[l].reshape(T, D).astype(F32).T.astype(BF)
        for j in range(3):
            cols = slice(j * D, (j + 1) * D)
            store_rows(ch, dot(lit, r.gpk[:, cols]), cols)
        ch.advance(env)
        r.br[...] = dot_t(r.gpk[:, :D], r.wq[l]) + dot_t(r.gpk[:, D:], r.wkv[l])
        r.x[...] = r.x[...] + r.br[...]

    for l in reversed(range(L)):
        backward_ffn(l)
        backward_attn(l)

    res_l.wait()
    res_r.wait()
    for b in range(2):
        rows = pl.ds(TL * b, TL)
        r.cot[b] = (r.x[rows, :] + r.dual[rows, :]).astype(BF)
    gt_l = local(r.cot.at[xc], o_gtok.at[xc], "gtok_l")
    gt_r = remote(r.cot.at[1 - xc], o_gtok.at[xc], "gtok_r", XP)
    gt_l.start()
    gt_r.start()
    for i in range(2 + nb):
        c = exchange_gb(i)
        c.start()
        c.wait()
        r.GB[...] = r.GB[...] + r.GBR[i]
    gb_out = local(r.GB, o_gb, "gb_out")
    gb_out.start()
    for ch in order:
        ch.complete(env)
    gb_out.wait()
    gt_l.wait()
    gt_r.wait()


def body(nd, tokens, counts, lengths, wqkv, wo, wup, wdown, gain, bias, cot):
    layers, width = wo.shape[0], wo.shape[2]
    ff = wup.shape[2]
    tl = tokens.shape[1]
    plan = make_plan(layers, tl, width, ff, nd)
    names = list(plan.scratch)
    any_spec = pl.BlockSpec(memory_space=pl.ANY)
    vmem = pl.BlockSpec(memory_space=pltpu.VMEM)
    smem = pl.BlockSpec(memory_space=pltpu.SMEM)
    rr = plan.r
    sd = jax.ShapeDtypeStruct
    outs = pl.pallas_call(
        partial(kernel, plan, names),
        out_shape=(
            sd(tokens.shape, BF),
            sd(tokens.shape, BF),
            sd((layers, 4, rr, 3 * width), BF),
            sd((layers, 4, rr, width), BF),
            sd((layers, 4, rr, ff), BF),
            sd((layers, ff // nd, width), BF),
            sd((16, width), F32),
            sd((max(layers - 1, 1), 2 * tl, ff), BF),
            sd((max(layers - 1, 1), 2 * tl, ff), BF),
        ),
        in_specs=[any_spec, smem, smem, any_spec, any_spec, any_spec, any_spec, vmem, vmem, any_spec],
        out_specs=[any_spec] * 9,
        scratch_shapes=[plan.scratch[k] for k in names] + [pltpu.SemaphoreType.DMA((plan.n_sem,))],
        compiler_params=pltpu.CompilerParams(
            collective_id=0, has_side_effects=True, vmem_limit_bytes=60 * 2**20
        ),
    )(
        tokens,
        counts,
        lengths,
        wqkv,
        wo.reshape(layers, HEADS // 2, 2, 64, width),
        wup,
        wdown,
        gain,
        bias,
        cot,
    )
    res, gtok, gq, go, gu, gd, gb = outs[:7]
    result = res.astype(F32)
    grad_tokens = gtok.astype(F32)
    grads = [
        gq.astype(F32).reshape(layers, 4 * rr, 3 * width),
        go.astype(F32).reshape(layers, 4 * rr, width),
        gu.astype(F32).reshape(layers, 4 * rr, ff),
        gd.astype(F32),
    ]
    norms = gain.shape[0]
    gains = [gb[:norms], gb[8 : 8 + norms]]
    size = lax.axis_size("dp")
    if nd == size:
        piece = width // size
        start = lax.axis_index("dp") * piece
        gains = [lax.dynamic_slice(g, (0, start), (norms, piece)) for g in gains]
    else:
        grads = [lax.psum_scatter(g, "dp", scatter_dimension=1, tiled=True) for g in grads]
        gains = [lax.psum_scatter(g, "dp", scatter_dimension=1, tiled=True) for g in gains]
    return (result, grad_tokens, *grads, *gains)


def solution(mesh):
    dp = mesh.shape["dp"]
    nd = dp if dp & (dp - 1) == 0 and 512 % (64 * dp) == 0 else 1
    return jax.shard_map(
        partial(body, nd),
        mesh=mesh,
        in_specs=(
            P("dp", "head", None),
            P("dp"),
            P("dp", None),
            P(),
            P(),
            P(),
            P(),
            P(),
            P(),
            P("dp", "head", None),
        ),
        out_specs=(
            P("dp", "head", None),
            P("dp", "head", None),
            P(None, "dp", None),
            P(None, "dp", None),
            P(None, "dp", None),
            P(None, "dp", None),
            P(None, "dp"),
            P(None, "dp"),
        ),
        check_vma=False,
    )
```

```python
import math
from functools import partial
from types import SimpleNamespace

import jax
import jax.numpy as jnp
import numpy as np
from jax import lax
from jax.experimental import pallas as pl
from jax.experimental.pallas import tpu as pltpu
from jax.sharding import PartitionSpec as P

HEADS = 8
EPS = 1e-05
NEG = -1e30
LOG2E = 1.4426950408889634
BF = jnp.bfloat16
F32 = jnp.float32
MESH = pl.DeviceIdType.MESH


DOWN, HID, UP, GN, NORM_A, OUT, HEAD = range(7)
QKV, GN2 = HEAD + HEADS, HEAD + HEADS + 1
TAIL = (GN2 + 1, -1)

EVENTS = {
    (GN, 1): (10, 11, 12),
    (HEAD, 1): (110, 111, 112),
    (HEAD + 1, 1): (210,),
    (HEAD + 3, 1): (10, 11, 12),
    (HEAD + 5, 1): (112,),
    (HEAD + 6, 1): (110, 111, 210),
    (HEAD + 7, 1): (10, 12),
    (QKV, 1): (11,),
    (GN2, 1): (112,),
    (DOWN, 0): (110, 111, 310, 311, 312),
    (HID, 0): (10, 210, 11, 12),
    (UP, 0): (112,),
    (GN, 0): (0, 1, 2),
    (NORM_A, 0): (110, 111),
    (HEAD, 0): (210, 310, 100, 101, 102),
    (HEAD + 1, 0): (10, 312, 200),
    (HEAD + 2, 0): (11, 12, 311),
    (HEAD + 3, 0): (112, 0),
    (HEAD + 4, 0): (310, 1, 2),
    (HEAD + 5, 0): (110, 111, 210),
    (HEAD + 7, 0): (312, 100, 101, 102),
    (QKV, 0): (0, 2, 200),
    (GN2, 0): (311,),
    TAIL: (
        310, 312, 300, 301, 302, 1, 100, 102, 2, 311, 101, 200,
        0, 312, 300, 302, 100, 2, 301, 311, 102, 0, 1, 101,
        302, 200, 100, 301, 300, 102, 1, 302, 101, 301, 200, 300,
        302, 301,
    ),
}


GB_STEPS = [(p, 0) for p in (NORM_A, HEAD + 1, HEAD + 3, HEAD + 5, HEAD + 7, GN2)]


def dot(a, b):
    return jnp.dot(a, b, preferred_element_type=F32)


def dot_t(a, b):
    return lax.dot_general(a, b, (((1,), (1,)), ((), ())), preferred_element_type=F32)


def dot_lt(a, b):
    return lax.dot_general(a, b, (((0,), (0,)), ((), ())), preferred_element_type=F32)


def gelu_parts(h):
    t = 1.0 / (1.0 + (0.3275911 * math.sqrt(0.5)) * jnp.abs(h))
    e = jnp.exp2(h * h * (-0.5 * LOG2E))
    poly = 0.5 * 1.061405429
    for a in (-1.453152027, 1.421413741, -0.284496736, 0.254829592):
        poly = poly * t + 0.5 * a
    q = poly * t * e
    phi = jnp.where(h >= 0.0, 1.0 - q, q)
    return h * phi, phi + h * (e * (1.0 / math.sqrt(2.0 * math.pi)))


def split3(v):
    hi = v.astype(BF).astype(F32)
    rest = v - hi
    mid = rest.astype(BF).astype(F32)
    return hi, mid, rest - mid


class Plan:
    def __init__(self, layers, tl, width, ff, nd):
        self.L, self.TL, self.D, self.FF, self.nd = layers, tl, width, ff, nd
        self.T = 2 * tl
        self.nb = nd.bit_length() - 1
        self.r = width // nd // 4
        self.scratch = {}
        self.n_sem = 0

    def add(self, name, shape, dtype):
        self.scratch[name] = pltpu.VMEM(tuple(shape), dtype)

    def sem(self):
        self.n_sem += 1
        return self.n_sem - 1


def axes_of(nb):
    return [("head", 1), ("head", 2)] + [("dp", 1 << b) for b in reversed(range(nb))]


X, Y, Z1, Z2 = ("head", 2), ("dp", 1), ("dp", 2), ("dp", 4)
ORDER_X = [[X], [Y], [Z1], [Z2]]
ORDER_Y = [[Y], [Z1], [X], [Z2]]
ORDER_Z = [[Z1], [X], [Y], [Z2]]
ORDERS = {
    "D": [ORDER_X, ORDER_Y, ORDER_Z],
    "U": [ORDER_X, ORDER_Y, ORDER_Z],
    "O": [[[Z1], [Y], [X], [Z2]]],
    "Q": [[[Y], [X], [Z1, Z2]], ORDER_Y, [[Z1], [Y], [X], [Z2]]],
}
SHARES = {"D": (3, 3, 2), "U": (6, 6, 4), "O": (1,), "Q": (4, 4, 4)}


class Part:
    def __init__(self, chunk, number, rows, cols):
        plan, nb = chunk.plan, chunk.plan.nb
        self.chunk, self.rows, self.cols = chunk, rows, cols
        self.name = f"{chunk.name}{number}"
        self.axes = axes_of(nb)
        known = [[a for a in s if a in self.axes] for s in ORDERS[chunk.kind][number]]
        self.stages = [[("head", 1)]] + [s for s in known if s]
        rest = [a for a in self.axes if not any(a in s for s in self.stages)]
        self.stages += [[a] for a in rest]
        self.patterns, self.sems = [], []
        left = len(self.axes)
        for s, dims in enumerate(self.stages):
            left -= len(dims)
            pats = [
                [dims[i] for i in range(len(dims)) if m >> i & 1] for m in range(1, 1 << len(dims))
            ]
            self.patterns.append(pats)
            size = [rows.stop - rows.start, cols.stop - cols.start]
            plan.add(f"R{self.name}_{s}", [len(pats)] + [2] * left + size, BF)
            self.sems.append([(plan.sem(), plan.sem()) for _ in pats])
        self.at = 0

    def index(self, env, stage, flipped):
        done = [a for s in self.stages[:stage] for a in s]
        out = []
        for a in self.axes:
            bit = env.bits[a]
            if a in done:
                out.append(bit)
            elif a in self.stages[stage]:
                out.append(1 - bit if a in flipped else bit)
            else:
                out.append(slice(None))
        return tuple(out)

    def copies(self, env, stage):
        for i, (pat, (ss, rs)) in enumerate(zip(self.patterns[stage], self.sems[stage])):
            yield pltpu.make_async_remote_copy(
                src_ref=env.ref["G" + self.chunk.name].at[
                    self.index(env, stage, pat) + (self.rows, self.cols)
                ],
                dst_ref=env.ref[f"R{self.name}_{stage}"].at[i],
                send_sem=env.sems.at[ss],
                recv_sem=env.sems.at[rs],
                device_id=env.partner(pat),
                device_id_type=MESH,
            )

    def finish(self, env, stage):
        for c in self.copies(env, stage):
            c.wait()
        own = self.index(env, stage, ())
        g = env.ref["G" + self.chunk.name]
        got = env.ref[f"R{self.name}_{stage}"]
        left = sum(isinstance(o, slice) for o in own)
        for at in np.ndindex(*[2] * left):
            piece = iter(at)
            here = tuple(next(piece) if isinstance(o, slice) else o for o in own)
            here = here + (self.rows, self.cols)
            total = g[here].astype(F32)
            for i in range(len(self.patterns[stage])):
                total = total + got[(i, *at)].astype(F32)
            g[here] = total.astype(BF)

    def step(self, env, at):
        if at > 0:
            self.finish(env, at - 1)
        if at < len(self.stages):
            for c in self.copies(env, at):
                c.start()


class Chunk:
    def __init__(self, plan, kind, layer):
        self.kind, self.layer, self.plan = kind, layer, plan
        self.name = f"{kind}{layer}"
        nb, r = plan.nb, plan.r
        rows, cols = {
            "U": (r, plan.FF),
            "O": (r, plan.D),
            "Q": (r, 3 * plan.D),
            "D": (plan.D // 4, plan.FF // plan.nd),
        }[kind]
        self.rows, self.cols = rows, cols
        plan.add("G" + self.name, [2] * (2 + nb) + [rows, cols], BF)
        out_shape = (cols, rows) if kind == "D" else (rows, cols)
        plan.add("P" + self.name, out_shape, BF)
        self.parts, start, shares = [], 0, SHARES[kind]
        for number, share in enumerate(shares):
            whole = rows if kind == "D" else cols
            stop = start + whole * share // sum(shares)
            span = slice(start, stop)
            if kind == "D":
                self.parts.append(Part(self, number, span, slice(0, cols)))
            else:
                self.parts.append(Part(self, number, slice(0, rows), span))
            start = stop
        self.last_sems = [(plan.sem(), plan.sem()) for _ in range(3)]
        self.local_sem = plan.sem()
        self.to_do = len(self.parts)

    def parts_done(self, env):
        own = tuple(env.bits[a] for a in axes_of(self.plan.nb))
        total = env.ref["G" + self.name][own]
        if self.kind == "D":
            total = total.astype(F32).T
        if self.kind == "Q":
            total = total.astype(F32)
            d = self.plan.D
            lo = lax.broadcasted_iota(jnp.int32, (self.rows, 128), 1) < 64
            tiles = []
            for p in range(HEADS // 2):
                q = total[:, 128 * p : 128 * p + 128]
                k0 = pltpu.roll(total[:, d + 256 * p : d + 256 * p + 128], 64, 1)
                k1 = pltpu.roll(total[:, d + 256 * p + 128 : d + 256 * p + 256], 64, 1)
                tiles += [jnp.where(lo, q, k0), jnp.where(lo, k0, q), k1]
            total = jnp.concatenate(tiles, axis=1)
        env.ref["P" + self.name][...] = total.astype(BF)
        for c in self.spread(env)[:3]:
            c.start()

    def place(self, env, quarter):
        out = env.out[self.kind]
        if self.kind == "D":
            cols = pl.ds(pl.multiple_of(quarter * self.rows, self.rows), self.rows)
            return out.at[self.layer, :, cols]
        return out.at[self.layer, quarter]

    def spread(self, env):
        core, x = ("head", 1), ("head", 2)
        src, here = env.ref["P" + self.name], self.place(env, env.head)
        there = self.place(env, env.partner([x])[1])
        copies = [pltpu.make_async_copy(src, here, env.sems.at[self.local_sem])]
        for (a, b, pat), (ss, rs) in zip(
            ((src, here, [x]), (src, here, [core]), (there, there, [core])), self.last_sems
        ):
            copies.append(
                pltpu.make_async_remote_copy(
                    src_ref=a,
                    dst_ref=b,
                    send_sem=env.sems.at[ss],
                    recv_sem=env.sems.at[rs],
                    device_id=env.partner(pat),
                    device_id_type=MESH,
                )
            )
        return copies

    def pass_on(self, env):
        copies = self.spread(env)
        copies[1].wait_recv()
        copies[3].start()

    def complete(self, env):
        copies = self.spread(env)
        copies[0].wait()
        copies[1].wait_send()
        copies[2].wait()
        copies[3].wait()


def schedule(plan):
    layers = sorted({l for _, l in plan.chunks}, reverse=True)
    ready = {DOWN: "D", UP: "U", OUT: "O", QKV: "Q"}
    todo = {}

    def advance(acts, ch, number):
        part = ch.parts[number]
        if part.at > len(part.stages):
            return
        acts.append((part.step, part.at))
        part.at += 1
        if part.at > len(part.stages):
            ch.to_do -= 1
            if ch.to_do == 0:
                acts.append((ch.parts_done,))

    for point in [(n, l) for l in layers for n in range(GN2 + 1)] + [TAIL]:
        acts = todo.setdefault(point, [])
        ch = plan.chunks.get((ready.get(point[0]), point[1]))
        if ch is not None:
            for i in range(len(ch.parts)):
                advance(acts, ch, i)
        for c in EVENTS.get(point, ()):
            ch = plan.chunks.get(("DUOQ"[c // 100], c // 10 % 10))
            if ch is None:
                continue
            advance(acts, ch, c % 10)
    for ch in plan.chunks.values():
        for i, part in enumerate(ch.parts):
            while part.at <= len(part.stages):
                advance(acts, ch, i)
    for ch in plan.chunks.values():
        acts.append((ch.pass_on,))
    return todo


def make_plan(layers, tl, width, ff, nd):
    plan = Plan(layers, tl, width, ff, nd)
    t, n = plan.T, HEADS
    add = plan.add
    add("x", (t, width), F32)
    add("dual", (t, width), F32)
    add("cot", (2, tl, width), BF)
    add("E", (4 * tl, 128), BF)
    add("EQ", (t, 128), BF)
    add("wq", (layers, width, width), BF)
    add("wkv", (layers, width, 2 * width), BF)
    add("wo", (layers, n // 2, 2, 64, width), BF)
    add("wup", (width, ff), BF)
    add("wdown", (ff, width), BF)
    add("low_in", (layers, 2, tl, width), BF)
    add("KV", (layers, n, 4 * tl, 128), BF)
    add("Q", (layers, n // 2, t, 128), BF)
    add("QX", (layers, t, 128), BF)
    add("att", (layers, t, width), BF)
    add("n_attn", (layers, t, width), BF)
    add("RS", (t, 128), F32)
    add("low_mid", (layers, t, width), BF)
    add("n_ffn", (layers, t, width), BF)
    add("act", (t, ff), BF)
    add("gp", (t, ff), BF)
    add("gb", (t, width), BF)
    add("ksend", (n, t, 128), BF)
    add("krecv", (n, t, 128), BF)
    add("GB", (16, width), F32)
    nbits = 2 + plan.nb
    add("GBR", (nbits, 16, width), F32)
    plan.chunks = {}
    for layer in reversed(range(layers)):
        for kind in "DUOQ":
            plan.chunks[kind, layer] = Chunk(plan, kind, layer)
    plan.misc = {}
    for name in (
        ["tok_l", "cot_l", "res_l", "gtok_l", "act_s", "gp_s", "act_b", "gp_b", "gb_out"]
        + [f"{w}{l}{i}" for l in range(layers) for w in ("wqkv", "wo0", "wo1", "wup", "wdown") for i in "ab"]
    ):
        plan.misc[name] = plan.sem()
    for name in (
        ["tok_r", "cot_r", "res_r", "gtok_r"]
        + [f"kv{l}{i}" for l in range(layers) for i in range(2)]
        + [f"dkv{l}{h}" for l in range(layers) for h in range(n)]
        + [f"GB{i}" for i in range(nbits)]
    ):
        plan.misc[name] = (plan.sem(), plan.sem())
    return plan


def kernel(plan, names, *refs):
    (tokens, counts, lengths, wqkv, wo, wup, wdown, gain, bias, cot) = refs[:10]
    (o_res, o_gtok, o_q, o_o, o_u, o_d, o_gb, s_act, s_gp) = refs[10:19]
    ref = dict(zip(names, refs[19:-1]))
    sems = refs[-1]
    r = SimpleNamespace(**{k: v for k, v in ref.items()})
    L, T, TL, D, FF, nb = plan.L, plan.T, plan.TL, plan.D, plan.FF, plan.nb
    n_heads = HEADS
    dp, head = lax.axis_index("dp"), lax.axis_index("head")
    core, xc = head % 2, head // 2
    bits = {("head", 1): core, ("head", 2): xc}
    for b in range(nb):
        bits["dp", 1 << b] = (dp // (1 << b)) % 2

    def partner(pat):
        d, h = dp, head
        for axis, bit in pat:
            v = bits[axis, bit]
            if axis == "dp":
                d = d + bit * (1 - 2 * v)
            else:
                h = h + bit * (1 - 2 * v)
        return (d, h)

    env = SimpleNamespace(
        ref=ref,
        sems=sems,
        bits=bits,
        partner=partner,
        head=head,
        out={"Q": o_q, "O": o_o, "U": o_u, "D": o_d},
    )
    CORE, XP = [("head", 1)], [("head", 2)]

    greet = [CORE, XP]
    for ch in plan.chunks.values():
        for part in ch.parts:
            for pats in part.patterns:
                for pat in pats:
                    if set(pat) not in [set(g) for g in greet]:
                        greet.append(pat)
    for b in range(nb):
        if [("dp", 1 << b)] not in greet:
            greet.append([("dp", 1 << b)])
    barrier = pltpu.get_barrier_semaphore()
    for pat in greet:
        pl.semaphore_signal(barrier, inc=1, device_id=partner(pat), device_id_type=MESH)

    def local(src, dst, name):
        return pltpu.make_async_copy(src, dst, sems.at[plan.misc[name]])

    def remote(src, dst, name, pat):
        ss, rs = plan.misc[name]
        return pltpu.make_async_remote_copy(
            src_ref=src,
            dst_ref=dst,
            send_sem=sems.at[ss],
            recv_sem=sems.at[rs],
            device_id=partner(pat),
            device_id_type=MESH,
        )

    stage_ref = [r.act, r.gp]
    raw = [
        local(wqkv.at[l], stage_ref[l].at[:, pl.ds(0, 3 * D)], f"wqkv{l}a") for l in range(L)
    ]
    raw[0].start()
    tok_l = local(tokens.at[xc], r.low_in.at[0, xc], "tok_l")
    tok_l.start()
    cot_l = local(cot.at[xc], r.cot.at[xc], "cot_l")
    wos = []
    for l in range(L):
        wos.append(
            [
                local(wo.at[l, :, e], r.wo.at[l, :, 1 - e], f"wo{e}{l}a")
                for e in range(2)
            ]
        )
    ups = [[local(wup.at[l], r.wup, f"wup{l}{i}") for i in "ab"[: L - l]] for l in range(L)]
    downs = [[local(wdown.at[l], r.wdown, f"wdown{l}{i}") for i in "ab"[: L - l]] for l in range(L)]
    pl.semaphore_wait(barrier, len(greet))
    tok_r = remote(tokens.at[1 - xc], r.low_in.at[0, xc], "tok_r", XP)
    tok_r.start()
    for c in raw[1:] + wos[0] + [ups[0][0], downs[0][0]] + sum(wos[1:], []) + [cot_l]:
        c.start()
    cot_r = remote(cot.at[1 - xc], r.cot.at[xc], "cot_r", XP)

    lane = lax.broadcasted_iota(jnp.int32, (TL, 128), 1)
    row = lax.broadcasted_iota(jnp.int32, (TL, 128), 0)
    count = counts[xc]
    several = count == 4
    for j in range(4):
        quarter = core + 2 * j if j < 2 else (1 - core) + 2 * (j - 2)
        limit_one = lengths[xc, 0] - TL * quarter
        limit = jnp.where(several, lengths[xc, quarter], limit_one)
        usable = row < limit
        same = jnp.logical_or(lane == quarter, jnp.logical_not(several))
        ok = jnp.logical_and(usable, same)
        tile = jnp.where(lane < 4, jnp.where(ok, 0.0, NEG), jnp.where(lane < 32, 1.0, 0.0))
        r.E[pl.ds(TL * j, TL), :] = tile.astype(BF)
    for b in range(2):
        tile = jnp.where(lane == core + 2 * b, 1.0, 0.0).astype(BF)
        r.EQ[pl.ds(TL * b, TL), :] = tile
        for l in range(L):
            r.QX[l, pl.ds(TL * b, TL), :] = tile

    low_half = lax.broadcasted_iota(jnp.int32, (D, 128), 1) < 64
    for l in range(L):
        raw[l].wait()

        def sort_pair(p, _, l=l):
            cols = lambda i: pl.ds(pl.multiple_of(p * 384 + 128 * i, 128), 128)
            t0 = stage_ref[l][:, cols(0)].astype(F32)
            t1 = stage_ref[l][:, cols(1)].astype(F32)
            t2 = stage_ref[l][:, cols(2)].astype(F32)
            r0, r1, r2 = (pltpu.roll(t, 64, 1) for t in (t0, t1, t2))
            r.wq[l, :, pl.ds(pl.multiple_of(p * 128, 128), 128)] = jnp.where(low_half, t0, t1).astype(BF)
            r.wkv[l, :, pl.ds(pl.multiple_of(p * 256, 128), 128)] = jnp.where(low_half, r0, r1).astype(BF)
            r.wkv[l, :, pl.ds(pl.multiple_of(p * 256 + 128, 128), 128)] = r2.astype(BF)
            return 0

        lax.fori_loop(0, n_heads // 2, sort_pair, 0)

    lane1 = lax.broadcasted_iota(jnp.int32, (1, 128), 1)
    m_lo = jnp.where(lane1 < 64, 1.0, 0.0).astype(BF)
    m_hi = jnp.where(lane1 < 64, 0.0, 1.0).astype(BF)
    m_of = [m_lo, m_hi]
    CH = T

    def rows_of(i):
        return pl.ds(i * CH, CH)

    def normalise(v):
        mu = jnp.mean(v, axis=1, keepdims=True)
        cen = v - mu
        var = jnp.mean(cen * cen, axis=1, keepdims=True)
        rs = lax.rsqrt(var + EPS)
        return cen * rs, rs

    def norm_back(g, n, rs, gain_row):
        h = g * gain_row
        return rs * (
            h - jnp.mean(h, axis=1, keepdims=True) - n * jnp.mean(h * n, axis=1, keepdims=True)
        )

    def keep_rs(col, rows, rs):
        lanes = lax.broadcasted_iota(jnp.int32, (CH, 128), 1)
        r.RS[rows, :] = jnp.where(lanes == col, rs, r.RS[rows, :])

    def fold(v):
        return jnp.sum(v.reshape(v.shape[0] // 8, 8, D), axis=0)

    r.RS[...] = jnp.zeros((T, 128), F32)
    tok_l.wait()
    tok_r.wait()
    cot_r.start()
    for b in range(2):
        v = r.low_in[0, b].astype(F32)
        r.x[pl.ds(TL * b, TL), :] = v
        r.dual[pl.ds(TL * b, TL), :] = v

    hold = {}

    def forward(l):
        if l > 0:
            r.low_in[l] = r.x[...].astype(BF).reshape(2, TL, D)
        low = r.low_in[l].reshape(T, D)
        sends = []
        hh = n_heads // 2
        for half in range(2):
            kv = dot(low, r.wkv[l, :, D * half : D * half + D]).astype(BF)
            for i in range(hh):
                r.KV[l, half * hh + i, 0:T, :] = kv[:, 128 * i : 128 * i + 128]
            c = remote(
                r.KV.at[l, pl.ds(half * hh, hh), pl.ds(0, T)],
                r.KV.at[l, pl.ds(half * hh, hh), pl.ds(T, T)],
                f"kv{l}{half}",
                CORE,
            )
            c.start()
            sends.append(c)
        q = (dot(low, r.wq[l]) * (LOG2E / 8.0)).astype(BF)
        for p in range(n_heads // 2):
            r.Q[l, p] = q[:, 128 * p : 128 * p + 128]
        lane_t = lax.broadcasted_iota(jnp.int32, (TL, 128), 1)

        pairs = 1
        tasks = [(u, e, b) for u in range(pairs) for e in range(2) for b in range(2)]

        def scores(p, e, b):
            rows = pl.ds(TL * b, TL)
            kve = jnp.concatenate([r.KV[l, 2 * p + e], r.E[...]], axis=1)
            qe = jnp.concatenate([r.Q[l, p, rows, :] * m_of[e], r.EQ[rows, :]], axis=1)
            return dot_t(qe, kve)

        def attend(i, _):
            outs, lses = {}, {}
            first = i * pairs
            ahead = scores(first, *tasks[0][1:])
            for k, (u, e, b) in enumerate(tasks):
                p, s, ahead = first + u, ahead, None
                if k + 1 < len(tasks):
                    ahead = scores(first + tasks[k + 1][0], *tasks[k + 1][1:])
                top = jnp.max(s, axis=1, keepdims=True)
                pe = jnp.exp2(s - top)
                total = jnp.sum(pe, axis=1, keepdims=True)
                o = dot(pe.astype(BF), r.KV[l, 2 * p + e])
                outs[e, b] = o * (1.0 / total)
                lses[e, b] = top + jnp.log(total) * LOG2E
                if e == 1:
                    rows = pl.ds(TL * b, TL)
                    tile = r.QX[l, rows, :].astype(F32)
                    for e2 in range(2):
                        hi, mid, lo = split3(-lses[e2, b])
                        at = lane_t - (8 + 3 * (2 * p + e2))
                        tile = jnp.where(at == 0, hi, jnp.where(at == 1, mid, jnp.where(at == 2, lo, tile)))
                    r.QX[l, rows, :] = tile.astype(BF)
                    both = jnp.where(lane_t < 64, outs[1, b], outs[0, b])
                    r.att[l, rows, pl.ds(pl.multiple_of(p * 128, 128), 128)] = both.astype(BF)
            return 0

        steps = n_heads // 4 // pairs
        for half in range(2):
            sends[half].wait()
            lax.fori_loop(half * steps, half * steps + steps, attend, 0)
        if l == 0:
            for l2 in range(L):
                for c in wos[l2]:
                    c.wait()
        branch = dot(r.att[l], r.wo[l].reshape(D, D))

        def after_attn(i, _):
            rows = rows_of(i)
            br = branch
            r.dual[rows, :] = r.dual[rows, :] + br
            n, rs = normalise(r.x[rows, :] + br)
            r.n_attn[l, rows, :] = n.astype(BF)
            keep_rs(2 * l, rows, rs)
            y = n * gain[2 * l : 2 * l + 1, :] + bias[2 * l : 2 * l + 1, :]
            r.x[rows, :] = y
            r.low_mid[l, rows, :] = y.astype(BF)
            return 0

        after_attn(0, 0)
        ups[l][0].wait()
        downs[l][0].wait()
        if l > 0:
            hold["act_s"].wait()
            hold["gp_s"].wait()
        fb = 256

        def up(j):
            return dot(r.low_mid[l], r.wup[:, j * fb : (j + 1) * fb])

        ahead = up(0)
        for j in range(FF // fb):
            hidden, ahead = ahead, up(j + 1) if j + 1 < FF // fb else None
            cols = slice(j * fb, (j + 1) * fb)
            a, gp = gelu_parts(hidden)
            r.act[:, cols] = a.astype(BF)
            r.gp[:, cols] = gp.astype(BF)
        branch = dot(r.act[...], r.wdown[...])
        if l < L - 1:
            hold["act_s"] = local(r.act, s_act.at[l], "act_s")
            hold["gp_s"] = local(r.gp, s_gp.at[l], "gp_s")
            hold["act_s"].start()
            hold["gp_s"].start()
            ups[l + 1][0].start()
            downs[l + 1][0].start()

        def after_ffn(i, _):
            rows = rows_of(i)
            br = branch
            r.dual[rows, :] = r.dual[rows, :] + br
            n, rs = normalise(r.x[rows, :] + br)
            r.n_ffn[l, rows, :] = n.astype(BF)
            keep_rs(2 * l + 1, rows, rs)
            r.x[rows, :] = n * gain[2 * l + 1 : 2 * l + 2, :] + bias[2 * l + 1 : 2 * l + 2, :]
            return 0

        after_ffn(0, 0)

    for l in range(L):
        forward(l)

    cot_l.wait()
    cot_r.wait()
    k = 2 * L
    zero = jnp.zeros((8, D), F32)
    r.GB[...] = jnp.zeros((16, D), F32)

    def put_gb(row, acc):
        r.GB[row : row + 1, :] = jnp.sum(acc[0], axis=0, keepdims=True)
        r.GB[8 + row : 9 + row, :] = jnp.sum(acc[1], axis=0, keepdims=True)

    for b in range(2):

        def ending(i, acc, b=b):
            rows = pl.ds(TL * b, TL)
            part = pl.ds(0, TL)
            n, rs = normalise(r.dual[rows, :])
            res = r.x[rows, :] + n * gain[k : k + 1, :] + bias[k : k + 1, :]
            g = r.cot[b, part, :].astype(F32)
            r.cot[b, part, :] = res.astype(BF)
            r.x[rows, :] = g
            r.dual[rows, :] = norm_back(g, n, rs, gain[k : k + 1, :])
            return acc[0] + fold(g * n), acc[1] + fold(g)

        acc = ending(0, (zero, zero) if b == 0 else acc)
    put_gb(k, acc)
    res_l = local(r.cot.at[xc], o_res.at[xc], "res_l")
    res_r = remote(r.cot.at[1 - xc], o_res.at[xc], "res_r", XP)
    res_l.start()
    res_r.start()

    def norm_pull(row, n_ref, l):
        def step(i, acc):
            rows = rows_of(i)
            g, n = r.x[rows, :], n_ref[l, rows, :].astype(F32)
            pre = norm_back(g, n, r.RS[rows, row : row + 1], gain[row : row + 1, :])
            r.x[rows, :] = pre
            r.gb[rows, :] = (pre + r.dual[rows, :]).astype(BF)
            return acc[0] + fold(g * n), acc[1] + fold(g)

        put_gb(row, step(0, (zero, zero)))

    def store_rows(ch, res, cols, swap=False):
        g = ref["G" + ch.name]
        rr = plan.r
        piece = min(rr, 64)
        for d in range(plan.nd):
            for q in range(4):
                for s in range(0, rr, piece):
                    src = (4 * d + q) * rr + s
                    if swap:
                        src = src ^ 64
                    idx = (q % 2, q // 2) + tuple((d >> b) & 1 for b in reversed(range(nb)))
                    g[idx + (slice(s, s + piece), cols)] = res[src : src + piece].astype(BF)

    def exchange_gb(i):
        pat = ([CORE, XP] + [[("dp", 1 << b)] for b in range(nb)])[i]
        return remote(r.GB, r.GBR.at[i], f"GB{i}", pat)

    order = list(plan.chunks.values())

    todo = schedule(plan)

    def step_chunks(point, l):
        for act, *at in todo.get((point, l), ()):
            act(env, *at)
        if (point, l) in GB_STEPS:
            i = GB_STEPS.index((point, l))
            if 0 < i <= 2 + nb:
                exchange_gb(i - 1).wait()
                r.GB[...] = r.GB[...] + r.GBR[i - 1]
            if i < 2 + nb:
                exchange_gb(i).start()

    def backward_ffn(l):
        norm_pull(2 * l + 1, r.n_ffn, l)
        if l < L - 1:
            for c in (hold["act_b"], hold["gp_b"], ups[l][1], downs[l][1]):
                c.wait()
        ch = plan.chunks["D", l]
        gbt = r.gb[...].astype(F32).T.astype(BF)
        dcols = ch.cols
        g = ref["G" + ch.name]
        for d in range(plan.nd):
            idx = tuple((d >> b) & 1 for b in reversed(range(nb)))
            step = min(dcols, 512)
            for s in range(0, dcols, step):
                res = dot(gbt, r.act[:, d * dcols + s : d * dcols + s + step])
                for q in range(4):
                    g[(q % 2, q // 2) + idx + (slice(None), slice(s, s + step))] = res[
                        q * ch.rows : (q + 1) * ch.rows
                    ].astype(BF)
        step_chunks(DOWN, l)
        fb = 512

        def down_back(j):
            return dot_t(r.gb[...], r.wdown[j * fb : (j + 1) * fb, :])

        ahead = down_back(0)
        for j in range(FF // fb):
            gact, ahead = ahead, down_back(j + 1) if j + 1 < FF // fb else None
            cols = slice(j * fb, (j + 1) * fb)
            r.gp[:, cols] = (gact * r.gp[:, cols].astype(F32)).astype(BF)
        step_chunks(HID, l)
        ch = plan.chunks["U", l]
        lmt = r.low_mid[l].astype(F32).T.astype(BF)
        for j in range(FF // fb):
            res = dot(lmt, r.gp[:, j * fb : (j + 1) * fb])
            store_rows(ch, res, slice(j * fb, (j + 1) * fb))
        step_chunks(UP, l)
        r.x[...] = r.x[...] + dot_t(r.gp[...], r.wup[...])
        step_chunks(GN, l)
        if l > 0:
            hold["act_b"] = local(s_act.at[l - 1], r.act, "act_b")
            hold["gp_b"] = local(s_gp.at[l - 1], r.gp, "gp_b")
            for c in (hold["gp_b"], ups[l - 1][1], downs[l - 1][1]):
                c.start()

    def backward_attn(l):
        norm_pull(2 * l, r.n_attn, l)
        step_chunks(NORM_A, l)
        ch = plan.chunks["O", l]
        res = dot(r.att[l].astype(F32).T.astype(BF), r.gb[...])
        store_rows(ch, res, slice(None), swap=True)
        step_chunks(OUT, l)
        r.gb[...] = dot_t(r.gb[...], r.wo[l].reshape(D, D)).astype(BF)
        lane_t = lax.broadcasted_iota(jnp.int32, (T, 128), 1)
        scale = [
            jnp.where(lane1 < 64, 1.0 / LOG2E, 1.0),
            jnp.where(lane1 < 64, 1.0, 1.0 / LOG2E),
        ]

        def dkv_copy(h, name_h):
            ss, rs = plan.misc[f"dkv{l}0"]
            return pltpu.make_async_remote_copy(
                src_ref=r.ksend.at[h],
                dst_ref=r.krecv.at[h],
                send_sem=sems.at[ss + 2 * h],
                recv_sem=sems.at[rs + 2 * h],
                device_id=partner(CORE),
                device_id_type=MESH,
            )

        def pair(p, _):
            tile = pl.ds(pl.multiple_of(p * 128, 128), 128)
            att = r.att[l, :, tile].astype(F32)
            given = []
            for e in range(2):
                h = 2 * p + e
                q = r.Q[l, p] * m_of[e]
                at = lane1 - (8 + 3 * h)
                mine = jnp.where(
                    jnp.logical_or(lane1 < 4, jnp.logical_and(at >= 0, at < 3)), 1.0, 0.0
                ).astype(BF)
                do = r.gb[:, tile] * m_of[1 - e]
                centre = jnp.sum(att * do.astype(F32), axis=1, keepdims=True)
                hi, mid, lo = split3(-centre)
                ed = jnp.where(
                    lane_t == 4, hi, jnp.where(lane_t == 5, mid, jnp.where(lane_t == 6, lo, 0.0))
                ).astype(BF)
                qd = jnp.concatenate(
                    [
                        jnp.concatenate([q, r.QX[l] * mine], axis=1),
                        jnp.concatenate([do, ed], axis=1),
                    ],
                    axis=0,
                )
                given.append((h, qd, jnp.concatenate([do, q], axis=0)))

            def scores(e, j):
                h, qd, _ = given[e]
                rows = pl.ds(T * j, T)
                return dot_t(jnp.concatenate([r.KV[l, h, rows, :], r.E[rows, :]], axis=1), qd)

            dqts = [0.0, 0.0]

            def products(e, j, pr, ds):
                h, _, dq_in = given[e]
                dkv = dot(jnp.concatenate([pr, ds], axis=1), dq_in) * scale[e]
                dqts[e] = dqts[e] + dot_lt(r.KV[l, h, pl.ds(T * j, T), :], ds)
                if j == 1:
                    r.ksend[h] = dkv.astype(BF)
                    dkv_copy(h, None).start()
                else:
                    r.act[:, pl.ds(pl.multiple_of(D + h * 128, 128), 128)] = dkv.astype(BF)
                    for at in range(n_heads // 2):
                        point = HEAD + 2 * at + e
                        if todo.get((point, l)) or (point, l) in GB_STEPS:

                            @pl.when(p == at)
                            def _(point=point):
                                step_chunks(point, l)

            tasks = [(e, j) for e in range(2) for j in (1, 0)]
            ahead, behind = scores(*tasks[0]), None
            for k, (e, j) in enumerate(tasks):
                ss, ahead = ahead, scores(*tasks[k + 1]) if k + 1 < len(tasks) else None
                pr = jnp.exp2(ss[:, :T])
                ds = (pr * ss[:, T:]).astype(BF)
                if behind is not None:
                    products(*behind)
                behind = (e, j, pr.astype(BF), ds)
            products(*behind)
            dq = jnp.concatenate([dqts[0][:64], dqts[1][64:]], axis=0).T * (1.0 / 8.0)
            r.act[:, tile] = dq.astype(BF)
            return 0

        lax.fori_loop(0, n_heads // 2, pair, 0)
        for h in range(n_heads):
            dkv_copy(h, None).wait()
            cols = slice(D + 128 * h, D + 128 * h + 128)
            r.act[:, cols] = (r.act[:, cols].astype(F32) + r.krecv[h].astype(F32)).astype(BF)
        ch = plan.chunks["Q", l]
        lit = r.low_in[l].reshape(T, D).astype(F32).T.astype(BF)
        for j in range(3):
            cols = slice(j * D, (j + 1) * D)
            store_rows(ch, dot(lit, r.act[:, cols]), cols)
        step_chunks(QKV, l)
        back = dot_t(r.act[:, :D], r.wq[l]) + dot_t(r.act[:, D : 3 * D], r.wkv[l])
        r.x[...] = r.x[...] + back
        step_chunks(GN2, l)
        if l > 0:
            hold["act_b"].start()

    for l in reversed(range(L)):
        backward_ffn(l)
        backward_attn(l)

    res_l.wait()
    res_r.wait()
    for b in range(2):
        rows = pl.ds(TL * b, TL)
        r.cot[b] = (r.x[rows, :] + r.dual[rows, :]).astype(BF)
    gt_l = local(r.cot.at[xc], o_gtok.at[xc], "gtok_l")
    gt_r = remote(r.cot.at[1 - xc], o_gtok.at[xc], "gtok_r", XP)
    gt_l.start()
    gt_r.start()
    for i in range(2 + nb):
        if i + 1 >= len(GB_STEPS):
            exchange_gb(i).start()
            exchange_gb(i).wait()
            r.GB[...] = r.GB[...] + r.GBR[i]
    gb_out = local(r.GB, o_gb, "gb_out")
    gb_out.start()
    step_chunks(*TAIL)
    for ch in order:
        ch.complete(env)
    gb_out.wait()
    gt_l.wait()
    gt_r.wait()


def body(nd, tokens, counts, lengths, wqkv, wo, wup, wdown, gain, bias, cot):
    layers, width = wo.shape[0], wo.shape[2]
    ff = wup.shape[2]
    tl = tokens.shape[1]
    plan = make_plan(layers, tl, width, ff, nd)
    names = list(plan.scratch)
    any_spec = pl.BlockSpec(memory_space=pl.ANY)
    vmem = pl.BlockSpec(memory_space=pltpu.VMEM)
    smem = pl.BlockSpec(memory_space=pltpu.SMEM)
    rr = plan.r
    sd = jax.ShapeDtypeStruct
    outs = pl.pallas_call(
        partial(kernel, plan, names),
        out_shape=(
            sd(tokens.shape, BF),
            sd(tokens.shape, BF),
            sd((layers, 4, rr, 3 * width), BF),
            sd((layers, 4, rr, width), BF),
            sd((layers, 4, rr, ff), BF),
            sd((layers, ff // nd, width), BF),
            sd((16, width), F32),
            sd((max(layers - 1, 1), 2 * tl, ff), BF),
            sd((max(layers - 1, 1), 2 * tl, ff), BF),
        ),
        in_specs=[any_spec, smem, smem, any_spec, any_spec, any_spec, any_spec, vmem, vmem, any_spec],
        out_specs=[any_spec] * 9,
        scratch_shapes=[plan.scratch[k] for k in names] + [pltpu.SemaphoreType.DMA((plan.n_sem,))],
        compiler_params=pltpu.CompilerParams(
            collective_id=0, has_side_effects=True, vmem_limit_bytes=60 * 2**20
        ),
    )(
        tokens,
        counts,
        lengths,
        wqkv,
        wo.reshape(layers, HEADS // 2, 2, 64, width),
        wup,
        wdown,
        gain,
        bias,
        cot,
    )
    wide = list(outs[:6])
    for i, cols in ((2, 3 * width), (3, width), (4, ff)):
        wide[i] = wide[i].reshape(layers, 4 * rr, cols)
    norms = gain.shape[0]
    size = lax.axis_size("dp")
    piece = width // size
    summed_here = nd == size

    def widen(*refs):
        src, dst, narrow, full = refs[:7], refs[7:15], refs[15:22], refs[22:28]
        sems = refs[28]
        into = [pltpu.make_async_copy(a, b, sems.at[i]) for i, (a, b) in enumerate(zip(src, narrow))]
        away = [pltpu.make_async_copy(a, b, sems.at[7 + i]) for i, (a, b) in enumerate(zip(full, dst))]
        for c in into:
            c.start()
        for i in range(6):
            into[i].wait()
            full[i][...] = narrow[i][...].astype(F32)
            away[i].start()
        into[6].wait()
        gb = narrow[6][...]
        if summed_here:
            start = lax.axis_index("dp") * piece
            gb = pltpu.roll(gb, lax.rem(width - start, width), 1)[:, :piece]
        dst[6][...] = gb[:norms]
        dst[7][...] = gb[8 : 8 + norms]
        for c in away:
            c.wait()

    gcols = piece if summed_here else width
    result, grad_tokens, *grads, gain_rows, bias_rows = pl.pallas_call(
        widen,
        out_shape=[sd(w.shape, F32) for w in wide] + [sd((norms, gcols), F32)] * 2,
        in_specs=[any_spec] * 7,
        out_specs=[any_spec] * 6 + [vmem] * 2,
        scratch_shapes=[pltpu.VMEM(w.shape, BF) for w in wide]
        + [pltpu.VMEM(outs[6].shape, F32)]
        + [pltpu.VMEM(w.shape, F32) for w in wide]
        + [pltpu.SemaphoreType.DMA((13,))],
        compiler_params=pltpu.CompilerParams(vmem_limit_bytes=56 * 2**20),
    )(*wide, outs[6])
    gains = [gain_rows, bias_rows]
    if not summed_here:
        grads = [lax.psum_scatter(g, "dp", scatter_dimension=1, tiled=True) for g in grads]
        gains = [lax.psum_scatter(g, "dp", scatter_dimension=1, tiled=True) for g in gains]
    return (result, grad_tokens, *grads, *gains)


def solution(mesh):
    dp = mesh.shape["dp"]
    nd = dp if dp & (dp - 1) == 0 and 512 % (64 * dp) == 0 else 1
    return jax.shard_map(
        partial(body, nd),
        mesh=mesh,
        in_specs=(
            P("dp", "head", None),
            P("dp"),
            P("dp", None),
            P(),
            P(),
            P(),
            P(),
            P(),
            P(),
            P("dp", "head", None),
        ),
        out_specs=(
            P("dp", "head", None),
            P("dp", "head", None),
            P(None, "dp", None),
            P(None, "dp", None),
            P(None, "dp", None),
            P(None, "dp", None),
            P(None, "dp"),
            P(None, "dp"),
        ),
        check_vma=False,
    )
```

```python
import math
from functools import partial
from types import SimpleNamespace

import jax
import jax.numpy as jnp
import numpy as np
from jax import lax
from jax.experimental import pallas as pl
from jax.experimental.pallas import tpu as pltpu
from jax.sharding import PartitionSpec as P

HEADS = 8
EPS = 1e-05
NEG = -1e30
LOG2E = 1.4426950408889634
BF = jnp.bfloat16
F32 = jnp.float32
MESH = pl.DeviceIdType.MESH


DOWN, HID, UP, GN, NORM_A, OUT, HEAD = range(7)
QKV, GN2 = HEAD + HEADS, HEAD + HEADS + 1
TAIL = (GN2 + 1, -1)

EVENTS = {
    (GN, 1): (10, 11, 12),
    (HEAD, 1): (110, 111, 112),
    (HEAD + 1, 1): (210,),
    (HEAD + 3, 1): (10, 11, 12),
    (HEAD + 5, 1): (112,),
    (HEAD + 6, 1): (110, 111, 210),
    (HEAD + 7, 1): (10, 12),
    (QKV, 1): (11,),
    (GN2, 1): (112,),
    (DOWN, 0): (110, 111, 310, 311, 312),
    (HID, 0): (10, 210, 11, 12),
    (UP, 0): (112,),
    (GN, 0): (0, 1, 2),
    (NORM_A, 0): (110, 111),
    (HEAD, 0): (210, 310, 100, 101, 102),
    (HEAD + 1, 0): (10, 312, 200),
    (HEAD + 2, 0): (11, 12, 311),
    (HEAD + 3, 0): (112, 0),
    (HEAD + 4, 0): (310, 1, 2),
    (HEAD + 5, 0): (110, 111, 210),
    (HEAD + 7, 0): (312, 100, 101, 102),
    (QKV, 0): (0, 2, 200),
    (GN2, 0): (311,),
    TAIL: (
        310, 312, 300, 301, 302, 1, 100, 102, 2, 311, 101, 200,
        0, 312, 300, 302, 100, 2, 301, 311, 102, 0, 1, 101,
        302, 200, 100, 301, 300, 102, 1, 302, 101, 301, 200, 300,
        302, 301,
    ),
}


GB_STEPS = [(p, 0) for p in (NORM_A, HEAD + 1, HEAD + 3, HEAD + 5, HEAD + 7, GN2)]


def dot(a, b):
    return jnp.dot(a, b, preferred_element_type=F32)


def dot_t(a, b):
    return lax.dot_general(a, b, (((1,), (1,)), ((), ())), preferred_element_type=F32)


def dot_lt(a, b):
    return lax.dot_general(a, b, (((0,), (0,)), ((), ())), preferred_element_type=F32)


def gelu_parts(h):
    t = 1.0 / (1.0 + (0.3275911 * math.sqrt(0.5)) * jnp.abs(h))
    e = jnp.exp2(h * h * (-0.5 * LOG2E))
    poly = 0.5 * 1.061405429
    for a in (-1.453152027, 1.421413741, -0.284496736, 0.254829592):
        poly = poly * t + 0.5 * a
    q = poly * t * e
    phi = jnp.where(h >= 0.0, 1.0 - q, q)
    return h * phi, phi + h * (e * (1.0 / math.sqrt(2.0 * math.pi)))


def split3(v):
    hi = v.astype(BF).astype(F32)
    rest = v - hi
    mid = rest.astype(BF).astype(F32)
    return hi, mid, rest - mid


class Plan:
    def __init__(self, layers, tl, width, ff, nd):
        self.L, self.TL, self.D, self.FF, self.nd = layers, tl, width, ff, nd
        self.T = 2 * tl
        self.nb = nd.bit_length() - 1
        self.r = width // nd // 4
        self.scratch = {}
        self.n_sem = 0

    def add(self, name, shape, dtype):
        self.scratch[name] = pltpu.VMEM(tuple(shape), dtype)

    def sem(self):
        self.n_sem += 1
        return self.n_sem - 1


def axes_of(nb):
    return [("head", 1), ("head", 2)] + [("dp", 1 << b) for b in reversed(range(nb))]


X, Y, Z1, Z2 = ("head", 2), ("dp", 1), ("dp", 2), ("dp", 4)
ORDER_X = [[X], [Y], [Z1], [Z2]]
ORDER_Y = [[Y], [Z1], [X], [Z2]]
ORDER_Z = [[Z1], [X], [Y], [Z2]]
ORDERS = {
    "D": [ORDER_X, ORDER_Y, ORDER_Z],
    "U": [ORDER_X, ORDER_Y, ORDER_Z],
    "O": [[[Z1], [Y], [X], [Z2]]],
    "Q": [[[Y], [X], [Z1, Z2]], ORDER_Y, [[Z1], [Y], [X], [Z2]]],
}
SHARES = {"D": (3, 3, 2), "U": (6, 6, 4), "O": (1,), "Q": (4, 4, 4)}


class Part:
    def __init__(self, chunk, number, rows, cols):
        plan, nb = chunk.plan, chunk.plan.nb
        self.chunk, self.rows, self.cols = chunk, rows, cols
        self.name = f"{chunk.name}{number}"
        self.axes = axes_of(nb)
        known = [[a for a in s if a in self.axes] for s in ORDERS[chunk.kind][number]]
        self.stages = [[("head", 1)]] + [s for s in known if s]
        rest = [a for a in self.axes if not any(a in s for s in self.stages)]
        self.stages += [[a] for a in rest]
        self.patterns, self.sems = [], []
        left = len(self.axes)
        for s, dims in enumerate(self.stages):
            left -= len(dims)
            pats = [
                [dims[i] for i in range(len(dims)) if m >> i & 1] for m in range(1, 1 << len(dims))
            ]
            self.patterns.append(pats)
            size = [rows.stop - rows.start, cols.stop - cols.start]
            plan.add(f"R{self.name}_{s}", [len(pats)] + [2] * left + size, BF)
            self.sems.append([(plan.sem(), plan.sem()) for _ in pats])
        self.at = 0

    def index(self, env, stage, flipped):
        done = [a for s in self.stages[:stage] for a in s]
        out = []
        for a in self.axes:
            bit = env.bits[a]
            if a in done:
                out.append(bit)
            elif a in self.stages[stage]:
                out.append(1 - bit if a in flipped else bit)
            else:
                out.append(slice(None))
        return tuple(out)

    def copies(self, env, stage):
        for i, (pat, (ss, rs)) in enumerate(zip(self.patterns[stage], self.sems[stage])):
            yield pltpu.make_async_remote_copy(
                src_ref=env.ref["G" + self.chunk.name].at[
                    self.index(env, stage, pat) + (self.rows, self.cols)
                ],
                dst_ref=env.ref[f"R{self.name}_{stage}"].at[i],
                send_sem=env.sems.at[ss],
                recv_sem=env.sems.at[rs],
                device_id=env.partner(pat),
                device_id_type=MESH,
            )

    def finish(self, env, stage):
        for c in self.copies(env, stage):
            c.wait()
        own = self.index(env, stage, ())
        g = env.ref["G" + self.chunk.name]
        got = env.ref[f"R{self.name}_{stage}"]
        left = sum(isinstance(o, slice) for o in own)
        for at in np.ndindex(*[2] * left):
            piece = iter(at)
            here = tuple(next(piece) if isinstance(o, slice) else o for o in own)
            here = here + (self.rows, self.cols)
            total = g[here].astype(F32)
            for i in range(len(self.patterns[stage])):
                total = total + got[(i, *at)].astype(F32)
            g[here] = total.astype(BF)

    def step(self, env, at):
        if at > 0:
            self.finish(env, at - 1)
        if at < len(self.stages):
            for c in self.copies(env, at):
                c.start()


class Chunk:
    def __init__(self, plan, kind, layer):
        self.kind, self.layer, self.plan = kind, layer, plan
        self.name = f"{kind}{layer}"
        nb, r = plan.nb, plan.r
        rows, cols = {
            "U": (r, plan.FF),
            "O": (r, plan.D),
            "Q": (r, 3 * plan.D),
            "D": (plan.D // 4, plan.FF // plan.nd),
        }[kind]
        self.rows, self.cols = rows, cols
        plan.add("G" + self.name, [2] * (2 + nb) + [rows, cols], BF)
        out_shape = (cols, rows) if kind == "D" else (rows, cols)
        plan.add("P" + self.name, out_shape, BF)
        self.parts, start, shares = [], 0, SHARES[kind]
        for number, share in enumerate(shares):
            whole = rows if kind == "D" else cols
            stop = start + whole * share // sum(shares)
            span = slice(start, stop)
            if kind == "D":
                self.parts.append(Part(self, number, span, slice(0, cols)))
            else:
                self.parts.append(Part(self, number, slice(0, rows), span))
            start = stop
        self.last_sems = [(plan.sem(), plan.sem()) for _ in range(3)]
        self.local_sem = plan.sem()
        self.to_do = len(self.parts)

    def parts_done(self, env):
        own = tuple(env.bits[a] for a in axes_of(self.plan.nb))
        total = env.ref["G" + self.name][own]
        if self.kind == "D":
            total = total.astype(F32).T
        if self.kind == "Q":
            total = total.astype(F32)
            d = self.plan.D
            lo = lax.broadcasted_iota(jnp.int32, (self.rows, 128), 1) < 64
            tiles = []
            for p in range(HEADS // 2):
                q = total[:, 128 * p : 128 * p + 128]
                k0 = pltpu.roll(total[:, d + 256 * p : d + 256 * p + 128], 64, 1)
                k1 = pltpu.roll(total[:, d + 256 * p + 128 : d + 256 * p + 256], 64, 1)
                tiles += [jnp.where(lo, q, k0), jnp.where(lo, k0, q), k1]
            total = jnp.concatenate(tiles, axis=1)
        env.ref["P" + self.name][...] = total.astype(BF)
        for c in self.spread(env)[:3]:
            c.start()

    def place(self, env, quarter):
        out = env.out[self.kind]
        if self.kind == "D":
            cols = pl.ds(pl.multiple_of(quarter * self.rows, self.rows), self.rows)
            return out.at[self.layer, :, cols]
        return out.at[self.layer, quarter]

    def spread(self, env):
        core, x = ("head", 1), ("head", 2)
        src, here = env.ref["P" + self.name], self.place(env, env.head)
        there = self.place(env, env.partner([x])[1])
        copies = [pltpu.make_async_copy(src, here, env.sems.at[self.local_sem])]
        for (a, b, pat), (ss, rs) in zip(
            ((src, here, [x]), (src, here, [core]), (there, there, [core])), self.last_sems
        ):
            copies.append(
                pltpu.make_async_remote_copy(
                    src_ref=a,
                    dst_ref=b,
                    send_sem=env.sems.at[ss],
                    recv_sem=env.sems.at[rs],
                    device_id=env.partner(pat),
                    device_id_type=MESH,
                )
            )
        return copies

    def pass_on(self, env):
        copies = self.spread(env)
        copies[1].wait_recv()
        copies[3].start()

    def complete(self, env):
        copies = self.spread(env)
        copies[0].wait()
        copies[1].wait_send()
        copies[2].wait()
        copies[3].wait()


def schedule(plan):
    layers = sorted({l for _, l in plan.chunks}, reverse=True)
    ready = {DOWN: "D", UP: "U", OUT: "O", QKV: "Q"}
    todo = {}

    def advance(acts, ch, number):
        part = ch.parts[number]
        if part.at > len(part.stages):
            return
        acts.append((part.step, part.at))
        part.at += 1
        if part.at > len(part.stages):
            ch.to_do -= 1
            if ch.to_do == 0:
                acts.append((ch.parts_done,))

    for point in [(n, l) for l in layers for n in range(GN2 + 1)] + [TAIL]:
        acts = todo.setdefault(point, [])
        if point == TAIL:
            early = [ch for ch in plan.chunks.values() if ch.to_do == 0]
            acts += [(ch.pass_on,) for ch in early]
        ch = plan.chunks.get((ready.get(point[0]), point[1]))
        if ch is not None:
            for i in range(len(ch.parts)):
                advance(acts, ch, i)
        for c in EVENTS.get(point, ()):
            ch = plan.chunks.get(("DUOQ"[c // 100], c // 10 % 10))
            if ch is None:
                continue
            advance(acts, ch, c % 10)
    for ch in plan.chunks.values():
        for i, part in enumerate(ch.parts):
            while part.at <= len(part.stages):
                advance(acts, ch, i)
    acts += [(ch.pass_on,) for ch in plan.chunks.values() if ch not in early]
    return todo


def make_plan(layers, tl, width, ff, nd):
    plan = Plan(layers, tl, width, ff, nd)
    t, n = plan.T, HEADS
    add = plan.add
    add("x", (t, width), F32)
    add("dual", (t, width), F32)
    add("cot", (2, tl, width), BF)
    add("E", (4 * tl, 128), BF)
    add("EQ", (t, 128), BF)
    add("wq", (layers, width, width), BF)
    add("wkv", (layers, width, 2 * width), BF)
    add("wo", (layers, n // 2, 2, 64, width), BF)
    add("wup", (width, ff), BF)
    add("wdown", (ff, width), BF)
    add("low_in", (layers, 2, tl, width), BF)
    add("KV", (layers, n, 4 * tl, 128), BF)
    add("Q", (layers, n // 2, t, 128), BF)
    add("QX", (layers, t, 128), BF)
    add("att", (layers, t, width), BF)
    add("n_attn", (layers, t, width), BF)
    add("RS", (t, 128), F32)
    add("low_mid", (layers, t, width), BF)
    add("n_ffn", (layers, t, width), BF)
    add("act", (t, ff), BF)
    add("gp", (t, ff), BF)
    add("gb", (t, width), BF)
    add("ksend", (n, t, 128), BF)
    add("krecv", (n, t, 128), BF)
    add("GB", (16, width), F32)
    nbits = 2 + plan.nb
    add("GBR", (nbits, 16, width), F32)
    plan.chunks = {}
    for layer in reversed(range(layers)):
        for kind in "DUOQ":
            plan.chunks[kind, layer] = Chunk(plan, kind, layer)
    plan.misc = {}
    for name in (
        ["tok_l", "cot_l", "res_l", "gtok_l", "act_s", "gp_s", "act_b", "gp_b", "gb_out"]
        + [f"{w}{l}{i}" for l in range(layers) for w in ("wqkv", "wo0", "wo1", "wup", "wdown") for i in "ab"]
    ):
        plan.misc[name] = plan.sem()
    for name in (
        ["tok_r", "cot_r", "res_r", "gtok_r"]
        + [f"kv{l}{i}" for l in range(layers) for i in range(2)]
        + [f"dkv{l}{h}" for l in range(layers) for h in range(n)]
        + [f"GB{i}" for i in range(nbits)]
    ):
        plan.misc[name] = (plan.sem(), plan.sem())
    return plan


def kernel(plan, names, *refs):
    (tokens, counts, lengths, wqkv, wo, wup, wdown, gain, bias, cot) = refs[:10]
    (o_res, o_gtok, o_q, o_o, o_u, o_d, o_gb, s_act, s_gp) = refs[10:19]
    ref = dict(zip(names, refs[19:-1]))
    sems = refs[-1]
    r = SimpleNamespace(**{k: v for k, v in ref.items()})
    L, T, TL, D, FF, nb = plan.L, plan.T, plan.TL, plan.D, plan.FF, plan.nb
    n_heads = HEADS
    dp, head = lax.axis_index("dp"), lax.axis_index("head")
    core, xc = head % 2, head // 2
    bits = {("head", 1): core, ("head", 2): xc}
    for b in range(nb):
        bits["dp", 1 << b] = (dp // (1 << b)) % 2

    def partner(pat):
        d, h = dp, head
        for axis, bit in pat:
            v = bits[axis, bit]
            if axis == "dp":
                d = d + bit * (1 - 2 * v)
            else:
                h = h + bit * (1 - 2 * v)
        return (d, h)

    env = SimpleNamespace(
        ref=ref,
        sems=sems,
        bits=bits,
        partner=partner,
        head=head,
        out={"Q": o_q, "O": o_o, "U": o_u, "D": o_d},
    )
    CORE, XP = [("head", 1)], [("head", 2)]

    greet = [CORE, XP]
    for ch in plan.chunks.values():
        for part in ch.parts:
            for pats in part.patterns:
                for pat in pats:
                    if set(pat) not in [set(g) for g in greet]:
                        greet.append(pat)
    for b in range(nb):
        if [("dp", 1 << b)] not in greet:
            greet.append([("dp", 1 << b)])
    barrier = pltpu.get_barrier_semaphore()
    for pat in greet:
        pl.semaphore_signal(barrier, inc=1, device_id=partner(pat), device_id_type=MESH)

    def local(src, dst, name):
        return pltpu.make_async_copy(src, dst, sems.at[plan.misc[name]])

    def remote(src, dst, name, pat):
        ss, rs = plan.misc[name]
        return pltpu.make_async_remote_copy(
            src_ref=src,
            dst_ref=dst,
            send_sem=sems.at[ss],
            recv_sem=sems.at[rs],
            device_id=partner(pat),
            device_id_type=MESH,
        )

    stage_ref = [r.act, r.gp]
    raw = [
        local(wqkv.at[l], stage_ref[l].at[:, pl.ds(0, 3 * D)], f"wqkv{l}a") for l in range(L)
    ]
    raw[0].start()
    tok_l = local(tokens.at[xc], r.low_in.at[0, xc], "tok_l")
    tok_l.start()
    cot_l = local(cot.at[xc], r.cot.at[xc], "cot_l")
    wos = []
    for l in range(L):
        wos.append(
            [
                local(wo.at[l, :, e], r.wo.at[l, :, 1 - e], f"wo{e}{l}a")
                for e in range(2)
            ]
        )
    ups = [[local(wup.at[l], r.wup, f"wup{l}{i}") for i in "ab"[: L - l]] for l in range(L)]
    downs = [[local(wdown.at[l], r.wdown, f"wdown{l}{i}") for i in "ab"[: L - l]] for l in range(L)]
    pl.semaphore_wait(barrier, len(greet))
    tok_r = remote(tokens.at[1 - xc], r.low_in.at[0, xc], "tok_r", XP)
    tok_r.start()
    for c in raw[1:] + wos[0] + [ups[0][0], downs[0][0]] + sum(wos[1:], []) + [cot_l]:
        c.start()
    cot_r = remote(cot.at[1 - xc], r.cot.at[xc], "cot_r", XP)

    lane = lax.broadcasted_iota(jnp.int32, (TL, 128), 1)
    row = lax.broadcasted_iota(jnp.int32, (TL, 128), 0)
    count = counts[xc]
    several = count == 4
    for j in range(4):
        quarter = core + 2 * j if j < 2 else (1 - core) + 2 * (j - 2)
        limit_one = lengths[xc, 0] - TL * quarter
        limit = jnp.where(several, lengths[xc, quarter], limit_one)
        usable = row < limit
        same = jnp.logical_or(lane == quarter, jnp.logical_not(several))
        ok = jnp.logical_and(usable, same)
        tile = jnp.where(lane < 4, jnp.where(ok, 0.0, NEG), jnp.where(lane < 32, 1.0, 0.0))
        r.E[pl.ds(TL * j, TL), :] = tile.astype(BF)
    for b in range(2):
        tile = jnp.where(lane == core + 2 * b, 1.0, 0.0).astype(BF)
        r.EQ[pl.ds(TL * b, TL), :] = tile
        for l in range(L):
            r.QX[l, pl.ds(TL * b, TL), :] = tile

    low_half = lax.broadcasted_iota(jnp.int32, (D, 128), 1) < 64
    for l in range(L):
        raw[l].wait()

        def sort_pair(p, _, l=l):
            cols = lambda i: pl.ds(pl.multiple_of(p * 384 + 128 * i, 128), 128)
            t0 = stage_ref[l][:, cols(0)].astype(F32)
            t1 = stage_ref[l][:, cols(1)].astype(F32)
            t2 = stage_ref[l][:, cols(2)].astype(F32)
            r0, r1, r2 = (pltpu.roll(t, 64, 1) for t in (t0, t1, t2))
            r.wq[l, :, pl.ds(pl.multiple_of(p * 128, 128), 128)] = jnp.where(low_half, t0, t1).astype(BF)
            r.wkv[l, :, pl.ds(pl.multiple_of(p * 256, 128), 128)] = jnp.where(low_half, r0, r1).astype(BF)
            r.wkv[l, :, pl.ds(pl.multiple_of(p * 256 + 128, 128), 128)] = r2.astype(BF)
            return 0

        lax.fori_loop(0, n_heads // 2, sort_pair, 0)

    lane1 = lax.broadcasted_iota(jnp.int32, (1, 128), 1)
    m_lo = jnp.where(lane1 < 64, 1.0, 0.0).astype(BF)
    m_hi = jnp.where(lane1 < 64, 0.0, 1.0).astype(BF)
    m_of = [m_lo, m_hi]
    CH = T

    def rows_of(i):
        return pl.ds(i * CH, CH)

    def normalise(v):
        mu = jnp.mean(v, axis=1, keepdims=True)
        cen = v - mu
        var = jnp.mean(cen * cen, axis=1, keepdims=True)
        rs = lax.rsqrt(var + EPS)
        return cen * rs, rs

    def norm_back(g, n, rs, gain_row):
        h = g * gain_row
        return rs * (
            h - jnp.mean(h, axis=1, keepdims=True) - n * jnp.mean(h * n, axis=1, keepdims=True)
        )

    def keep_rs(col, rows, rs):
        lanes = lax.broadcasted_iota(jnp.int32, (CH, 128), 1)
        r.RS[rows, :] = jnp.where(lanes == col, rs, r.RS[rows, :])

    def fold(v):
        return jnp.sum(v.reshape(v.shape[0] // 8, 8, D), axis=0)

    r.RS[...] = jnp.zeros((T, 128), F32)
    tok_l.wait()
    tok_r.wait()
    cot_r.start()
    for b in range(2):
        v = r.low_in[0, b].astype(F32)
        r.x[pl.ds(TL * b, TL), :] = v
        r.dual[pl.ds(TL * b, TL), :] = v

    hold = {}

    def forward(l):
        if l > 0:
            r.low_in[l] = r.x[...].astype(BF).reshape(2, TL, D)
        low = r.low_in[l].reshape(T, D)
        sends = []
        hh = n_heads // 2
        for half in range(2):
            kv = dot(low, r.wkv[l, :, D * half : D * half + D]).astype(BF)
            for i in range(hh):
                r.KV[l, half * hh + i, 0:T, :] = kv[:, 128 * i : 128 * i + 128]
            c = remote(
                r.KV.at[l, pl.ds(half * hh, hh), pl.ds(0, T)],
                r.KV.at[l, pl.ds(half * hh, hh), pl.ds(T, T)],
                f"kv{l}{half}",
                CORE,
            )
            c.start()
            sends.append(c)
        q = (dot(low, r.wq[l]) * (LOG2E / 8.0)).astype(BF)
        for p in range(n_heads // 2):
            r.Q[l, p] = q[:, 128 * p : 128 * p + 128]
        lane_t = lax.broadcasted_iota(jnp.int32, (TL, 128), 1)

        pairs = 1
        tasks = [(u, e, b) for u in range(pairs) for e in range(2) for b in range(2)]

        def scores(p, e, b):
            rows = pl.ds(TL * b, TL)
            kve = jnp.concatenate([r.KV[l, 2 * p + e], r.E[...]], axis=1)
            qe = jnp.concatenate([r.Q[l, p, rows, :] * m_of[e], r.EQ[rows, :]], axis=1)
            return dot_t(qe, kve)

        def attend(i, _):
            outs, lses = {}, {}
            first = i * pairs
            ahead = scores(first, *tasks[0][1:])
            for k, (u, e, b) in enumerate(tasks):
                p, s, ahead = first + u, ahead, None
                if k + 1 < len(tasks):
                    ahead = scores(first + tasks[k + 1][0], *tasks[k + 1][1:])
                top = jnp.max(s, axis=1, keepdims=True)
                pe = jnp.exp2(s - top)
                total = jnp.sum(pe, axis=1, keepdims=True)
                o = dot(pe.astype(BF), r.KV[l, 2 * p + e])
                outs[e, b] = o * (1.0 / total)
                lses[e, b] = top + jnp.log(total) * LOG2E
                if e == 1:
                    rows = pl.ds(TL * b, TL)
                    tile = r.QX[l, rows, :].astype(F32)
                    for e2 in range(2):
                        hi, mid, lo = split3(-lses[e2, b])
                        at = lane_t - (8 + 3 * (2 * p + e2))
                        tile = jnp.where(at == 0, hi, jnp.where(at == 1, mid, jnp.where(at == 2, lo, tile)))
                    r.QX[l, rows, :] = tile.astype(BF)
                    both = jnp.where(lane_t < 64, outs[1, b], outs[0, b])
                    r.att[l, rows, pl.ds(pl.multiple_of(p * 128, 128), 128)] = both.astype(BF)
            return 0

        steps = n_heads // 4 // pairs
        for half in range(2):
            sends[half].wait()
            lax.fori_loop(half * steps, half * steps + steps, attend, 0)
        if l == 0:
            for l2 in range(L):
                for c in wos[l2]:
                    c.wait()
        branch = dot(r.att[l], r.wo[l].reshape(D, D))

        def after_attn(i, _):
            rows = rows_of(i)
            br = branch
            r.dual[rows, :] = r.dual[rows, :] + br
            n, rs = normalise(r.x[rows, :] + br)
            r.n_attn[l, rows, :] = n.astype(BF)
            keep_rs(2 * l, rows, rs)
            y = n * gain[2 * l : 2 * l + 1, :] + bias[2 * l : 2 * l + 1, :]
            r.x[rows, :] = y
            r.low_mid[l, rows, :] = y.astype(BF)
            return 0

        after_attn(0, 0)
        ups[l][0].wait()
        downs[l][0].wait()
        if l > 0:
            hold["act_s"].wait()
            hold["gp_s"].wait()
        fb = 256

        def up(j):
            return dot(r.low_mid[l], r.wup[:, j * fb : (j + 1) * fb])

        ahead = up(0)
        for j in range(FF // fb):
            hidden, ahead = ahead, up(j + 1) if j + 1 < FF // fb else None
            cols = slice(j * fb, (j + 1) * fb)
            a, gp = gelu_parts(hidden)
            r.act[:, cols] = a.astype(BF)
            r.gp[:, cols] = gp.astype(BF)
        branch = dot(r.act[...], r.wdown[...])
        if l < L - 1:
            hold["act_s"] = local(r.act, s_act.at[l], "act_s")
            hold["gp_s"] = local(r.gp, s_gp.at[l], "gp_s")
            hold["act_s"].start()
            hold["gp_s"].start()
            ups[l + 1][0].start()
            downs[l + 1][0].start()

        def after_ffn(i, _):
            rows = rows_of(i)
            br = branch
            r.dual[rows, :] = r.dual[rows, :] + br
            n, rs = normalise(r.x[rows, :] + br)
            r.n_ffn[l, rows, :] = n.astype(BF)
            keep_rs(2 * l + 1, rows, rs)
            r.x[rows, :] = n * gain[2 * l + 1 : 2 * l + 2, :] + bias[2 * l + 1 : 2 * l + 2, :]
            return 0

        after_ffn(0, 0)

    for l in range(L):
        forward(l)

    cot_l.wait()
    cot_r.wait()
    k = 2 * L
    zero = jnp.zeros((8, D), F32)
    r.GB[...] = jnp.zeros((16, D), F32)

    def put_gb(row, acc):
        r.GB[row : row + 1, :] = jnp.sum(acc[0], axis=0, keepdims=True)
        r.GB[8 + row : 9 + row, :] = jnp.sum(acc[1], axis=0, keepdims=True)

    for b in range(2):

        def ending(i, acc, b=b):
            rows = pl.ds(TL * b, TL)
            part = pl.ds(0, TL)
            n, rs = normalise(r.dual[rows, :])
            res = r.x[rows, :] + n * gain[k : k + 1, :] + bias[k : k + 1, :]
            g = r.cot[b, part, :].astype(F32)
            r.cot[b, part, :] = res.astype(BF)
            r.x[rows, :] = g
            r.dual[rows, :] = norm_back(g, n, rs, gain[k : k + 1, :])
            return acc[0] + fold(g * n), acc[1] + fold(g)

        acc = ending(0, (zero, zero) if b == 0 else acc)
    put_gb(k, acc)
    res_l = local(r.cot.at[xc], o_res.at[xc], "res_l")
    res_r = remote(r.cot.at[1 - xc], o_res.at[xc], "res_r", XP)
    res_l.start()
    res_r.start()

    def norm_pull(row, n_ref, l):
        def step(i, acc):
            rows = rows_of(i)
            g, n = r.x[rows, :], n_ref[l, rows, :].astype(F32)
            pre = norm_back(g, n, r.RS[rows, row : row + 1], gain[row : row + 1, :])
            r.x[rows, :] = pre
            r.gb[rows, :] = (pre + r.dual[rows, :]).astype(BF)
            return acc[0] + fold(g * n), acc[1] + fold(g)

        put_gb(row, step(0, (zero, zero)))

    def store_rows(ch, res, cols, swap=False):
        g = ref["G" + ch.name]
        rr = plan.r
        piece = min(rr, 64)
        for d in range(plan.nd):
            for q in range(4):
                for s in range(0, rr, piece):
                    src = (4 * d + q) * rr + s
                    if swap:
                        src = src ^ 64
                    idx = (q % 2, q // 2) + tuple((d >> b) & 1 for b in reversed(range(nb)))
                    g[idx + (slice(s, s + piece), cols)] = res[src : src + piece].astype(BF)

    def exchange_gb(i):
        pat = ([CORE, XP] + [[("dp", 1 << b)] for b in range(nb)])[i]
        return remote(r.GB, r.GBR.at[i], f"GB{i}", pat)

    order = list(plan.chunks.values())

    todo = schedule(plan)

    def step_chunks(point, l):
        for act, *at in todo.get((point, l), ()):
            act(env, *at)
        if (point, l) in GB_STEPS:
            i = GB_STEPS.index((point, l))
            if 0 < i <= 2 + nb:
                exchange_gb(i - 1).wait()
                r.GB[...] = r.GB[...] + r.GBR[i - 1]
            if i < 2 + nb:
                exchange_gb(i).start()

    def backward_ffn(l):
        norm_pull(2 * l + 1, r.n_ffn, l)
        if l < L - 1:
            for c in (hold["act_b"], hold["gp_b"], ups[l][1], downs[l][1]):
                c.wait()
        ch = plan.chunks["D", l]
        gbt = r.gb[...].astype(F32).T.astype(BF)
        dcols = ch.cols
        g = ref["G" + ch.name]
        for d in range(plan.nd):
            idx = tuple((d >> b) & 1 for b in reversed(range(nb)))
            step = min(dcols, 512)
            for s in range(0, dcols, step):
                res = dot(gbt, r.act[:, d * dcols + s : d * dcols + s + step])
                for q in range(4):
                    g[(q % 2, q // 2) + idx + (slice(None), slice(s, s + step))] = res[
                        q * ch.rows : (q + 1) * ch.rows
                    ].astype(BF)
        step_chunks(DOWN, l)
        fb = 512

        def down_back(j):
            return dot_t(r.gb[...], r.wdown[j * fb : (j + 1) * fb, :])

        ahead = down_back(0)
        for j in range(FF // fb):
            gact, ahead = ahead, down_back(j + 1) if j + 1 < FF // fb else None
            cols = slice(j * fb, (j + 1) * fb)
            r.gp[:, cols] = (gact * r.gp[:, cols].astype(F32)).astype(BF)
        step_chunks(HID, l)
        ch = plan.chunks["U", l]
        lmt = r.low_mid[l].astype(F32).T.astype(BF)
        for j in range(FF // fb):
            res = dot(lmt, r.gp[:, j * fb : (j + 1) * fb])
            store_rows(ch, res, slice(j * fb, (j + 1) * fb))
        step_chunks(UP, l)
        r.x[...] = r.x[...] + dot_t(r.gp[...], r.wup[...])
        step_chunks(GN, l)
        if l > 0:
            hold["act_b"] = local(s_act.at[l - 1], r.act, "act_b")
            hold["gp_b"] = local(s_gp.at[l - 1], r.gp, "gp_b")
            for c in (hold["gp_b"], ups[l - 1][1], downs[l - 1][1]):
                c.start()

    def backward_attn(l):
        norm_pull(2 * l, r.n_attn, l)
        step_chunks(NORM_A, l)
        ch = plan.chunks["O", l]
        res = dot(r.att[l].astype(F32).T.astype(BF), r.gb[...])
        store_rows(ch, res, slice(None), swap=True)
        step_chunks(OUT, l)
        r.gb[...] = dot_t(r.gb[...], r.wo[l].reshape(D, D)).astype(BF)
        lane_t = lax.broadcasted_iota(jnp.int32, (T, 128), 1)
        scale = [
            jnp.where(lane1 < 64, 1.0 / LOG2E, 1.0),
            jnp.where(lane1 < 64, 1.0, 1.0 / LOG2E),
        ]

        def dkv_copy(h, name_h):
            ss, rs = plan.misc[f"dkv{l}0"]
            return pltpu.make_async_remote_copy(
                src_ref=r.ksend.at[h],
                dst_ref=r.krecv.at[h],
                send_sem=sems.at[ss + 2 * h],
                recv_sem=sems.at[rs + 2 * h],
                device_id=partner(CORE),
                device_id_type=MESH,
            )

        def pair(p, _):
            tile = pl.ds(pl.multiple_of(p * 128, 128), 128)
            att = r.att[l, :, tile].astype(F32)
            given = []
            for e in range(2):
                h = 2 * p + e
                q = r.Q[l, p] * m_of[e]
                at = lane1 - (8 + 3 * h)
                mine = jnp.where(
                    jnp.logical_or(lane1 < 4, jnp.logical_and(at >= 0, at < 3)), 1.0, 0.0
                ).astype(BF)
                do = r.gb[:, tile] * m_of[1 - e]
                centre = jnp.sum(att * do.astype(F32), axis=1, keepdims=True)
                hi, mid, lo = split3(-centre)
                ed = jnp.where(
                    lane_t == 4, hi, jnp.where(lane_t == 5, mid, jnp.where(lane_t == 6, lo, 0.0))
                ).astype(BF)
                qd = jnp.concatenate(
                    [
                        jnp.concatenate([q, r.QX[l] * mine], axis=1),
                        jnp.concatenate([do, ed], axis=1),
                    ],
                    axis=0,
                )
                given.append((h, qd, jnp.concatenate([do, q], axis=0)))

            def scores(e, j):
                h, qd, _ = given[e]
                rows = pl.ds(T * j, T)
                return dot_t(jnp.concatenate([r.KV[l, h, rows, :], r.E[rows, :]], axis=1), qd)

            dqts = [0.0, 0.0]

            def products(e, j, pr, ds):
                h, _, dq_in = given[e]
                dkv = dot(jnp.concatenate([pr, ds], axis=1), dq_in) * scale[e]
                dqts[e] = dqts[e] + dot_lt(r.KV[l, h, pl.ds(T * j, T), :], ds)
                if j == 1:
                    r.ksend[h] = dkv.astype(BF)
                    dkv_copy(h, None).start()
                else:
                    r.act[:, pl.ds(pl.multiple_of(D + h * 128, 128), 128)] = dkv.astype(BF)
                    for at in range(n_heads // 2):
                        point = HEAD + 2 * at + e
                        if todo.get((point, l)) or (point, l) in GB_STEPS:

                            @pl.when(p == at)
                            def _(point=point):
                                step_chunks(point, l)

            tasks = [(e, j) for e in range(2) for j in (1, 0)]
            ahead, behind = scores(*tasks[0]), None
            for k, (e, j) in enumerate(tasks):
                ss, ahead = ahead, scores(*tasks[k + 1]) if k + 1 < len(tasks) else None
                pr = jnp.exp2(ss[:, :T])
                ds = (pr * ss[:, T:]).astype(BF)
                if behind is not None:
                    products(*behind)
                behind = (e, j, pr.astype(BF), ds)
            products(*behind)
            dq = jnp.concatenate([dqts[0][:64], dqts[1][64:]], axis=0).T * (1.0 / 8.0)
            r.act[:, tile] = dq.astype(BF)
            return 0

        lax.fori_loop(0, n_heads // 2, pair, 0)
        for h in range(n_heads):
            dkv_copy(h, None).wait()
            cols = slice(D + 128 * h, D + 128 * h + 128)
            r.act[:, cols] = (r.act[:, cols].astype(F32) + r.krecv[h].astype(F32)).astype(BF)
        ch = plan.chunks["Q", l]
        lit = r.low_in[l].reshape(T, D).astype(F32).T.astype(BF)
        for j in range(3):
            cols = slice(j * D, (j + 1) * D)
            store_rows(ch, dot(lit, r.act[:, cols]), cols)
        step_chunks(QKV, l)
        back = dot_t(r.act[:, :D], r.wq[l]) + dot_t(r.act[:, D : 3 * D], r.wkv[l])
        r.x[...] = r.x[...] + back
        step_chunks(GN2, l)
        if l > 0:
            hold["act_b"].start()

    for l in reversed(range(L)):
        backward_ffn(l)
        backward_attn(l)

    res_l.wait()
    res_r.wait()
    for b in range(2):
        rows = pl.ds(TL * b, TL)
        r.cot[b] = (r.x[rows, :] + r.dual[rows, :]).astype(BF)
    gt_l = local(r.cot.at[xc], o_gtok.at[xc], "gtok_l")
    gt_r = remote(r.cot.at[1 - xc], o_gtok.at[xc], "gtok_r", XP)
    gt_l.start()
    gt_r.start()
    for i in range(2 + nb):
        if i + 1 >= len(GB_STEPS):
            exchange_gb(i).start()
            exchange_gb(i).wait()
            r.GB[...] = r.GB[...] + r.GBR[i]
    gb_out = local(r.GB, o_gb, "gb_out")
    gb_out.start()
    step_chunks(*TAIL)
    for ch in order:
        ch.complete(env)
    gb_out.wait()
    gt_l.wait()
    gt_r.wait()


def body(nd, tokens, counts, lengths, wqkv, wo, wup, wdown, gain, bias, cot):
    layers, width = wo.shape[0], wo.shape[2]
    ff = wup.shape[2]
    tl = tokens.shape[1]
    plan = make_plan(layers, tl, width, ff, nd)
    names = list(plan.scratch)
    any_spec = pl.BlockSpec(memory_space=pl.ANY)
    vmem = pl.BlockSpec(memory_space=pltpu.VMEM)
    smem = pl.BlockSpec(memory_space=pltpu.SMEM)
    rr = plan.r
    sd = jax.ShapeDtypeStruct
    outs = pl.pallas_call(
        partial(kernel, plan, names),
        out_shape=(
            sd(tokens.shape, BF),
            sd(tokens.shape, BF),
            sd((layers, 4, rr, 3 * width), BF),
            sd((layers, 4, rr, width), BF),
            sd((layers, 4, rr, ff), BF),
            sd((layers, ff // nd, width), BF),
            sd((16, width), F32),
            sd((max(layers - 1, 1), 2 * tl, ff), BF),
            sd((max(layers - 1, 1), 2 * tl, ff), BF),
        ),
        in_specs=[any_spec, smem, smem, any_spec, any_spec, any_spec, any_spec, vmem, vmem, any_spec],
        out_specs=[any_spec] * 9,
        scratch_shapes=[plan.scratch[k] for k in names] + [pltpu.SemaphoreType.DMA((plan.n_sem,))],
        compiler_params=pltpu.CompilerParams(
            collective_id=0, has_side_effects=True, vmem_limit_bytes=60 * 2**20
        ),
    )(
        tokens,
        counts,
        lengths,
        wqkv,
        wo.reshape(layers, HEADS // 2, 2, 64, width),
        wup,
        wdown,
        gain,
        bias,
        cot,
    )
    wide = list(outs[:6])
    for i, cols in ((2, 3 * width), (3, width), (4, ff)):
        wide[i] = wide[i].reshape(layers, 4 * rr, cols)
    norms = gain.shape[0]
    size = lax.axis_size("dp")
    piece = width // size
    summed_here = nd == size

    def widen(*refs):
        src, dst, narrow, full = refs[:7], refs[7:14], refs[14:21], refs[21:27]
        sems = refs[27]
        into = [pltpu.make_async_copy(a, b, sems.at[i]) for i, (a, b) in enumerate(zip(src, narrow))]
        away = [pltpu.make_async_copy(a, b, sems.at[7 + i]) for i, (a, b) in enumerate(zip(full, dst))]
        for c in into:
            c.start()
        for i in range(6):
            into[i].wait()
            full[i][...] = narrow[i][...].astype(F32)
            away[i].start()
        into[6].wait()
        gb = narrow[6][...]
        if summed_here:
            start = lax.axis_index("dp") * piece
            gb = pltpu.roll(gb, lax.rem(width - start, width), 1)
        dst[6][...] = gb
        for c in away:
            c.wait()

    gcols = piece if summed_here else width
    result, grad_tokens, *grads, rows = pl.pallas_call(
        widen,
        out_shape=[sd(w.shape, F32) for w in wide] + [sd(outs[6].shape, F32)],
        in_specs=[any_spec] * 7,
        out_specs=[any_spec] * 6 + [vmem],
        scratch_shapes=[pltpu.VMEM(w.shape, BF) for w in wide]
        + [pltpu.VMEM(outs[6].shape, F32)]
        + [pltpu.VMEM(w.shape, F32) for w in wide]
        + [pltpu.SemaphoreType.DMA((13,))],
        compiler_params=pltpu.CompilerParams(vmem_limit_bytes=56 * 2**20),
    )(*wide, outs[6])
    gains = [rows[:norms, :gcols], rows[8 : 8 + norms, :gcols]]
    if not summed_here:
        grads = [lax.psum_scatter(g, "dp", scatter_dimension=1, tiled=True) for g in grads]
        gains = [lax.psum_scatter(g, "dp", scatter_dimension=1, tiled=True) for g in gains]
    return (result, grad_tokens, *grads, *gains)


def solution(mesh):
    dp = mesh.shape["dp"]
    nd = dp if dp & (dp - 1) == 0 and 512 % (64 * dp) == 0 else 1
    return jax.shard_map(
        partial(body, nd),
        mesh=mesh,
        in_specs=(
            P("dp", "head", None),
            P("dp"),
            P("dp", None),
            P(),
            P(),
            P(),
            P(),
            P(),
            P(),
            P("dp", "head", None),
        ),
        out_specs=(
            P("dp", "head", None),
            P("dp", "head", None),
            P(None, "dp", None),
            P(None, "dp", None),
            P(None, "dp", None),
            P(None, "dp", None),
            P(None, "dp"),
            P(None, "dp"),
        ),
        check_vma=False,
    )
```

```python
import math
from functools import partial
from types import SimpleNamespace

import jax
import jax.numpy as jnp
import numpy as np
from jax import lax
from jax.experimental import pallas as pl
from jax.experimental.pallas import tpu as pltpu
from jax.sharding import PartitionSpec as P

HEADS = 8
EPS = 1e-05
NEG = -1e30
LOG2E = 1.4426950408889634
BF = jnp.bfloat16
F32 = jnp.float32
MESH = pl.DeviceIdType.MESH


DOWN, HID, UP, GN, NORM_A, OUT, HEAD = range(7)
QKV, GN2 = HEAD + HEADS, HEAD + HEADS + 1
TAIL = (GN2 + 1, -1)

EVENTS = {
    (GN, 1): (10, 11, 12),
    (HEAD, 1): (110, 111, 112),
    (HEAD + 1, 1): (210,),
    (HEAD + 3, 1): (10, 11, 12),
    (HEAD + 5, 1): (112,),
    (HEAD + 6, 1): (110, 111, 210),
    (HEAD + 7, 1): (10, 12),
    (QKV, 1): (11,),
    (GN2, 1): (112,),
    (DOWN, 0): (110, 111, 310, 311, 312),
    (HID, 0): (10, 210, 11, 12),
    (UP, 0): (112,),
    (GN, 0): (0, 1, 2),
    (NORM_A, 0): (110, 111),
    (HEAD, 0): (210, 310, 100, 101, 102),
    (HEAD + 1, 0): (10, 312, 200),
    (HEAD + 2, 0): (11, 12, 311),
    (HEAD + 3, 0): (112, 0),
    (HEAD + 4, 0): (310, 1, 2),
    (HEAD + 5, 0): (110, 111, 210),
    (HEAD + 7, 0): (312, 100, 101, 102),
    (QKV, 0): (0, 2, 200),
    (GN2, 0): (311,),
    TAIL: (
        310, 312, 300, 301, 302, 1, 100, 102, 2, 311, 101, 200,
        0, 312, 300, 302, 100, 2, 301, 311, 102, 0, 1, 101,
        302, 200, 100, 301, 300, 102, 1, 302, 101, 301, 200, 300,
        302, 301,
    ),
}


GB_STEPS = [(p, 0) for p in (NORM_A, HEAD + 1, HEAD + 3, HEAD + 5, HEAD + 7, GN2)]


def dot(a, b):
    return jnp.dot(a, b, preferred_element_type=F32)


def dot_t(a, b):
    return lax.dot_general(a, b, (((1,), (1,)), ((), ())), preferred_element_type=F32)


def dot_lt(a, b):
    return lax.dot_general(a, b, (((0,), (0,)), ((), ())), preferred_element_type=F32)


def gelu_parts(h):
    t = 1.0 / (1.0 + (0.3275911 * math.sqrt(0.5)) * jnp.abs(h))
    e = jnp.exp2(h * h * (-0.5 * LOG2E))
    poly = 0.5 * 1.061405429
    for a in (-1.453152027, 1.421413741, -0.284496736, 0.254829592):
        poly = poly * t + 0.5 * a
    q = poly * t * e
    phi = jnp.where(h >= 0.0, 1.0 - q, q)
    return h * phi, phi + h * (e * (1.0 / math.sqrt(2.0 * math.pi)))


def split3(v):
    hi = v.astype(BF).astype(F32)
    rest = v - hi
    mid = rest.astype(BF).astype(F32)
    return hi, mid, rest - mid


class Plan:
    def __init__(self, layers, tl, width, ff, nd):
        self.L, self.TL, self.D, self.FF, self.nd = layers, tl, width, ff, nd
        self.T = 2 * tl
        self.nb = nd.bit_length() - 1
        self.r = width // nd // 4
        self.scratch = {}
        self.n_sem = 0

    def add(self, name, shape, dtype):
        self.scratch[name] = pltpu.VMEM(tuple(shape), dtype)

    def sem(self):
        self.n_sem += 1
        return self.n_sem - 1


def axes_of(nb):
    return [("head", 1), ("head", 2)] + [("dp", 1 << b) for b in reversed(range(nb))]


X, Y, Z1, Z2 = ("head", 2), ("dp", 1), ("dp", 2), ("dp", 4)
ORDER_X = [[X], [Y], [Z1], [Z2]]
ORDER_Y = [[Y], [Z1], [X], [Z2]]
ORDER_Z = [[Z1], [X], [Y], [Z2]]
ORDERS = {
    "D": [ORDER_X, ORDER_Y, ORDER_Z],
    "U": [ORDER_X, ORDER_Y, ORDER_Z],
    "O": [[[Z1], [Y], [X], [Z2]]],
    "Q": [[[Y], [X], [Z1, Z2]], ORDER_Y, [[Z1], [Y], [X], [Z2]]],
}
SHARES = {"D": (3, 3, 2), "U": (6, 6, 4), "O": (1,), "Q": (4, 4, 4)}


class Part:
    def __init__(self, chunk, number, rows, cols):
        plan, nb = chunk.plan, chunk.plan.nb
        self.chunk, self.rows, self.cols = chunk, rows, cols
        self.name = f"{chunk.name}{number}"
        self.axes = axes_of(nb)
        known = [[a for a in s if a in self.axes] for s in ORDERS[chunk.kind][number]]
        self.stages = [[("head", 1)]] + [s for s in known if s]
        rest = [a for a in self.axes if not any(a in s for s in self.stages)]
        self.stages += [[a] for a in rest]
        self.patterns, self.sems = [], []
        left = len(self.axes)
        for s, dims in enumerate(self.stages):
            left -= len(dims)
            pats = [
                [dims[i] for i in range(len(dims)) if m >> i & 1] for m in range(1, 1 << len(dims))
            ]
            self.patterns.append(pats)
            size = [rows.stop - rows.start, cols.stop - cols.start]
            plan.add(f"R{self.name}_{s}", [len(pats)] + [2] * left + size, BF)
            self.sems.append([(plan.sem(), plan.sem()) for _ in pats])
        self.at = 0

    def index(self, env, stage, flipped):
        done = [a for s in self.stages[:stage] for a in s]
        out = []
        for a in self.axes:
            bit = env.bits[a]
            if a in done:
                out.append(bit)
            elif a in self.stages[stage]:
                out.append(1 - bit if a in flipped else bit)
            else:
                out.append(slice(None))
        return tuple(out)

    def copies(self, env, stage):
        for i, (pat, (ss, rs)) in enumerate(zip(self.patterns[stage], self.sems[stage])):
            yield pltpu.make_async_remote_copy(
                src_ref=env.ref["G" + self.chunk.name].at[
                    self.index(env, stage, pat) + (self.rows, self.cols)
                ],
                dst_ref=env.ref[f"R{self.name}_{stage}"].at[i],
                send_sem=env.sems.at[ss],
                recv_sem=env.sems.at[rs],
                device_id=env.partner(pat),
                device_id_type=MESH,
            )

    def finish(self, env, stage):
        for c in self.copies(env, stage):
            c.wait()
        own = self.index(env, stage, ())
        g = env.ref["G" + self.chunk.name]
        got = env.ref[f"R{self.name}_{stage}"]
        left = sum(isinstance(o, slice) for o in own)
        for at in np.ndindex(*[2] * left):
            piece = iter(at)
            here = tuple(next(piece) if isinstance(o, slice) else o for o in own)
            here = here + (self.rows, self.cols)
            total = g[here].astype(F32)
            for i in range(len(self.patterns[stage])):
                total = total + got[(i, *at)].astype(F32)
            g[here] = total.astype(BF)

    def step(self, env, at):
        if at > 0:
            self.finish(env, at - 1)
        if at < len(self.stages):
            for c in self.copies(env, at):
                c.start()


class Chunk:
    def __init__(self, plan, kind, layer):
        self.kind, self.layer, self.plan = kind, layer, plan
        self.name = f"{kind}{layer}"
        nb, r = plan.nb, plan.r
        rows, cols = {
            "U": (r, plan.FF),
            "O": (r, plan.D),
            "Q": (r, 3 * plan.D),
            "D": (plan.D // 4, plan.FF // plan.nd),
        }[kind]
        self.rows, self.cols = rows, cols
        plan.add("G" + self.name, [2] * (2 + nb) + [rows, cols], BF)
        out_shape = (cols, rows) if kind == "D" else (rows, cols)
        plan.add("P" + self.name, out_shape, BF)
        self.parts, start, shares = [], 0, SHARES[kind]
        for number, share in enumerate(shares):
            whole = rows if kind == "D" else cols
            stop = start + whole * share // sum(shares)
            span = slice(start, stop)
            if kind == "D":
                self.parts.append(Part(self, number, span, slice(0, cols)))
            else:
                self.parts.append(Part(self, number, slice(0, rows), span))
            start = stop
        self.last_sems = [(plan.sem(), plan.sem()) for _ in range(3)]
        self.local_sem = plan.sem()
        self.to_do = len(self.parts)

    def parts_done(self, env):
        own = tuple(env.bits[a] for a in axes_of(self.plan.nb))
        total = env.ref["G" + self.name][own]
        if self.kind == "D":
            total = total.astype(F32).T
        if self.kind == "Q":
            total = total.astype(F32)
            d = self.plan.D
            lo = lax.broadcasted_iota(jnp.int32, (self.rows, 128), 1) < 64
            tiles = []
            for p in range(HEADS // 2):
                q = total[:, 128 * p : 128 * p + 128]
                k0 = pltpu.roll(total[:, d + 256 * p : d + 256 * p + 128], 64, 1)
                k1 = pltpu.roll(total[:, d + 256 * p + 128 : d + 256 * p + 256], 64, 1)
                tiles += [jnp.where(lo, q, k0), jnp.where(lo, k0, q), k1]
            total = jnp.concatenate(tiles, axis=1)
        env.ref["P" + self.name][...] = total.astype(BF)
        for c in self.spread(env)[:3]:
            c.start()

    def place(self, env, quarter):
        out = env.out[self.kind]
        if self.kind == "D":
            cols = pl.ds(pl.multiple_of(quarter * self.rows, self.rows), self.rows)
            return out.at[self.layer, :, cols]
        return out.at[self.layer, quarter]

    def spread(self, env):
        core, x = ("head", 1), ("head", 2)
        src, here = env.ref["P" + self.name], self.place(env, env.head)
        there = self.place(env, env.partner([x])[1])
        copies = [pltpu.make_async_copy(src, here, env.sems.at[self.local_sem])]
        for (a, b, pat), (ss, rs) in zip(
            ((src, here, [x]), (src, here, [core]), (there, there, [core])), self.last_sems
        ):
            copies.append(
                pltpu.make_async_remote_copy(
                    src_ref=a,
                    dst_ref=b,
                    send_sem=env.sems.at[ss],
                    recv_sem=env.sems.at[rs],
                    device_id=env.partner(pat),
                    device_id_type=MESH,
                )
            )
        return copies

    def pass_on(self, env):
        copies = self.spread(env)
        copies[1].wait_recv()
        copies[3].start()

    def complete(self, env):
        copies = self.spread(env)
        copies[0].wait()
        copies[1].wait_send()
        copies[2].wait()
        copies[3].wait()


def schedule(plan):
    layers = sorted({l for _, l in plan.chunks}, reverse=True)
    ready = {DOWN: "D", UP: "U", OUT: "O", QKV: "Q"}
    todo = {}

    def advance(acts, ch, number):
        part = ch.parts[number]
        if part.at > len(part.stages):
            return
        acts.append((part.step, part.at))
        part.at += 1
        if part.at > len(part.stages):
            ch.to_do -= 1
            if ch.to_do == 0:
                acts.append((ch.parts_done,))

    for point in [(n, l) for l in layers for n in range(GN2 + 1)] + [TAIL]:
        acts = todo.setdefault(point, [])
        if point == TAIL:
            early = [ch for ch in plan.chunks.values() if ch.to_do == 0]
            acts += [(ch.pass_on,) for ch in early]
        ch = plan.chunks.get((ready.get(point[0]), point[1]))
        if ch is not None:
            for i in range(len(ch.parts)):
                advance(acts, ch, i)
        for c in EVENTS.get(point, ()):
            ch = plan.chunks.get(("DUOQ"[c // 100], c // 10 % 10))
            if ch is None:
                continue
            advance(acts, ch, c % 10)
    for ch in plan.chunks.values():
        for i, part in enumerate(ch.parts):
            while part.at <= len(part.stages):
                advance(acts, ch, i)
    acts += [(ch.pass_on,) for ch in plan.chunks.values() if ch not in early]
    return todo


def make_plan(layers, tl, width, ff, nd):
    plan = Plan(layers, tl, width, ff, nd)
    t, n = plan.T, HEADS
    add = plan.add
    add("x", (t, width), F32)
    add("dual", (t, width), F32)
    add("cot", (2, tl, width), BF)
    add("E", (4 * tl, 128), BF)
    add("EQ", (t, 128), BF)
    add("wq", (layers, width, width), BF)
    add("wkv", (layers, width, 2 * width), BF)
    add("wo", (layers, n // 2, 2, 64, width), BF)
    add("wup", (width, ff), BF)
    add("wdown", (ff, width), BF)
    add("low_in", (layers, 2, tl, width), BF)
    add("KV", (layers, n, 4 * tl, 128), BF)
    add("Q", (layers, n // 2, t, 128), BF)
    add("QX", (layers, t, 128), BF)
    add("att", (layers, t, width), BF)
    add("n_attn", (layers, t, width), BF)
    add("RS", (t, 128), F32)
    add("low_mid", (layers, t, width), BF)
    add("n_ffn", (layers, t, width), BF)
    add("act", (t, ff), BF)
    add("gp", (t, ff), BF)
    add("gb", (t, width), BF)
    add("ksend", (n, t, 128), BF)
    add("krecv", (n, t, 128), BF)
    add("GB", (16, width), F32)
    nbits = 2 + plan.nb
    add("GBR", (nbits, 16, width), F32)
    plan.chunks = {}
    for layer in reversed(range(layers)):
        for kind in "DUOQ":
            plan.chunks[kind, layer] = Chunk(plan, kind, layer)
    plan.misc = {}
    for name in (
        ["tok_l", "cot_l", "res_l", "gtok_l", "act_s", "gp_s", "act_b", "gp_b", "gb_out"]
        + [f"{w}{l}{i}" for l in range(layers) for w in ("wqkv", "wo0", "wo1", "wup", "wdown") for i in "ab"]
    ):
        plan.misc[name] = plan.sem()
    for name in (
        ["tok_r", "cot_r", "res_r", "gtok_r"]
        + [f"kv{l}{i}" for l in range(layers) for i in range(2)]
        + [f"dkv{l}{h}" for l in range(layers) for h in range(n)]
        + [f"GB{i}" for i in range(nbits)]
    ):
        plan.misc[name] = (plan.sem(), plan.sem())
    return plan


def kernel(plan, names, *refs):
    (tokens, counts, lengths, wqkv, wo, wup, wdown, gain, bias, cot) = refs[:10]
    (o_res, o_gtok, o_q, o_o, o_u, o_d, o_gb, s_act, s_gp) = refs[10:19]
    ref = dict(zip(names, refs[19:-1]))
    sems = refs[-1]
    r = SimpleNamespace(**{k: v for k, v in ref.items()})
    L, T, TL, D, FF, nb = plan.L, plan.T, plan.TL, plan.D, plan.FF, plan.nb
    n_heads = HEADS
    dp, head = lax.axis_index("dp"), lax.axis_index("head")
    core, xc = head % 2, head // 2
    bits = {("head", 1): core, ("head", 2): xc}
    for b in range(nb):
        bits["dp", 1 << b] = (dp // (1 << b)) % 2

    def partner(pat):
        d, h = dp, head
        for axis, bit in pat:
            v = bits[axis, bit]
            if axis == "dp":
                d = d + bit * (1 - 2 * v)
            else:
                h = h + bit * (1 - 2 * v)
        return (d, h)

    env = SimpleNamespace(
        ref=ref,
        sems=sems,
        bits=bits,
        partner=partner,
        head=head,
        out={"Q": o_q, "O": o_o, "U": o_u, "D": o_d},
    )
    CORE, XP = [("head", 1)], [("head", 2)]

    greet = [CORE, XP]
    for ch in plan.chunks.values():
        for part in ch.parts:
            for pats in part.patterns:
                for pat in pats:
                    if set(pat) not in [set(g) for g in greet]:
                        greet.append(pat)
    for b in range(nb):
        if [("dp", 1 << b)] not in greet:
            greet.append([("dp", 1 << b)])
    barrier = pltpu.get_barrier_semaphore()
    for pat in greet:
        pl.semaphore_signal(barrier, inc=1, device_id=partner(pat), device_id_type=MESH)

    def local(src, dst, name):
        return pltpu.make_async_copy(src, dst, sems.at[plan.misc[name]])

    def remote(src, dst, name, pat):
        ss, rs = plan.misc[name]
        return pltpu.make_async_remote_copy(
            src_ref=src,
            dst_ref=dst,
            send_sem=sems.at[ss],
            recv_sem=sems.at[rs],
            device_id=partner(pat),
            device_id_type=MESH,
        )

    stage_ref = [r.act, r.gp]
    raw = [
        local(wqkv.at[l], stage_ref[l].at[:, pl.ds(0, 3 * D)], f"wqkv{l}a") for l in range(L)
    ]
    raw[0].start()
    tok_l = local(tokens.at[xc], r.low_in.at[0, xc], "tok_l")
    tok_l.start()
    cot_l = local(cot.at[xc], r.cot.at[xc], "cot_l")
    wos = []
    for l in range(L):
        wos.append(
            [
                local(wo.at[l, :, e], r.wo.at[l, :, 1 - e], f"wo{e}{l}a")
                for e in range(2)
            ]
        )
    ups = [[local(wup.at[l], r.wup, f"wup{l}{i}") for i in "ab"[: L - l]] for l in range(L)]
    downs = [[local(wdown.at[l], r.wdown, f"wdown{l}{i}") for i in "ab"[: L - l]] for l in range(L)]
    pl.semaphore_wait(barrier, len(greet))
    tok_r = remote(tokens.at[1 - xc], r.low_in.at[0, xc], "tok_r", XP)
    tok_r.start()
    for c in raw[1:] + wos[0] + [ups[0][0], downs[0][0]] + sum(wos[1:], []) + [cot_l]:
        c.start()
    cot_r = remote(cot.at[1 - xc], r.cot.at[xc], "cot_r", XP)

    lane = lax.broadcasted_iota(jnp.int32, (TL, 128), 1)
    row = lax.broadcasted_iota(jnp.int32, (TL, 128), 0)
    count = counts[xc]
    several = count == 4
    for j in range(4):
        quarter = core + 2 * j if j < 2 else (1 - core) + 2 * (j - 2)
        limit_one = lengths[xc, 0] - TL * quarter
        limit = jnp.where(several, lengths[xc, quarter], limit_one)
        usable = row < limit
        same = jnp.logical_or(lane == quarter, jnp.logical_not(several))
        ok = jnp.logical_and(usable, same)
        tile = jnp.where(lane < 4, jnp.where(ok, 0.0, NEG), jnp.where(lane < 32, 1.0, 0.0))
        r.E[pl.ds(TL * j, TL), :] = tile.astype(BF)
    for b in range(2):
        tile = jnp.where(lane == core + 2 * b, 1.0, 0.0).astype(BF)
        r.EQ[pl.ds(TL * b, TL), :] = tile
        for l in range(L):
            r.QX[l, pl.ds(TL * b, TL), :] = tile

    low_half = lax.broadcasted_iota(jnp.int32, (D, 128), 1) < 64
    for l in range(L):
        raw[l].wait()

        def sort_pair(p, _, l=l):
            cols = lambda i: pl.ds(pl.multiple_of(p * 384 + 128 * i, 128), 128)
            t0 = stage_ref[l][:, cols(0)].astype(F32)
            t1 = stage_ref[l][:, cols(1)].astype(F32)
            t2 = stage_ref[l][:, cols(2)].astype(F32)
            r0, r1, r2 = (pltpu.roll(t, 64, 1) for t in (t0, t1, t2))
            r.wq[l, :, pl.ds(pl.multiple_of(p * 128, 128), 128)] = jnp.where(low_half, t0, t1).astype(BF)
            r.wkv[l, :, pl.ds(pl.multiple_of(p * 256, 128), 128)] = jnp.where(low_half, r0, r1).astype(BF)
            r.wkv[l, :, pl.ds(pl.multiple_of(p * 256 + 128, 128), 128)] = r2.astype(BF)
            return 0

        lax.fori_loop(0, n_heads // 2, sort_pair, 0)

    lane1 = lax.broadcasted_iota(jnp.int32, (1, 128), 1)
    m_lo = jnp.where(lane1 < 64, 1.0, 0.0).astype(BF)
    m_hi = jnp.where(lane1 < 64, 0.0, 1.0).astype(BF)
    m_of = [m_lo, m_hi]
    CH = T

    def rows_of(i):
        return pl.ds(i * CH, CH)

    def normalise(v):
        mu = jnp.mean(v, axis=1, keepdims=True)
        cen = v - mu
        var = jnp.mean(cen * cen, axis=1, keepdims=True)
        rs = lax.rsqrt(var + EPS)
        return cen * rs, rs

    def norm_back(g, n, rs, gain_row):
        h = g * gain_row
        return rs * (
            h - jnp.mean(h, axis=1, keepdims=True) - n * jnp.mean(h * n, axis=1, keepdims=True)
        )

    def keep_rs(col, rows, rs):
        lanes = lax.broadcasted_iota(jnp.int32, (CH, 128), 1)
        r.RS[rows, :] = jnp.where(lanes == col, rs, r.RS[rows, :])

    def fold(v):
        return jnp.sum(v.reshape(v.shape[0] // 8, 8, D), axis=0)

    r.RS[...] = jnp.zeros((T, 128), F32)
    tok_l.wait()
    tok_r.wait()
    cot_r.start()
    for b in range(2):
        v = r.low_in[0, b].astype(F32)
        r.x[pl.ds(TL * b, TL), :] = v
        r.dual[pl.ds(TL * b, TL), :] = v

    hold = {}

    def forward(l):
        if l > 0:
            r.low_in[l] = r.x[...].astype(BF).reshape(2, TL, D)
        low = r.low_in[l].reshape(T, D)
        sends = []
        hh = n_heads // 2
        for half in range(2):
            kv = dot(low, r.wkv[l, :, D * half : D * half + D]).astype(BF)
            for i in range(hh):
                r.KV[l, half * hh + i, 0:T, :] = kv[:, 128 * i : 128 * i + 128]
            c = remote(
                r.KV.at[l, pl.ds(half * hh, hh), pl.ds(0, T)],
                r.KV.at[l, pl.ds(half * hh, hh), pl.ds(T, T)],
                f"kv{l}{half}",
                CORE,
            )
            c.start()
            sends.append(c)
        q = (dot(low, r.wq[l]) * (LOG2E / 8.0)).astype(BF)
        for p in range(n_heads // 2):
            r.Q[l, p] = q[:, 128 * p : 128 * p + 128]
        lane_t = lax.broadcasted_iota(jnp.int32, (TL, 128), 1)

        pairs = 1
        tasks = [(u, e, b) for u in range(pairs) for e in range(2) for b in range(2)]

        def scores(p, e, b):
            rows = pl.ds(TL * b, TL)
            kve = jnp.concatenate([r.KV[l, 2 * p + e], r.E[...]], axis=1)
            qe = jnp.concatenate([r.Q[l, p, rows, :] * m_of[e], r.EQ[rows, :]], axis=1)
            return dot_t(qe, kve)

        def attend(i, _):
            outs, lses = {}, {}
            first = i * pairs
            ahead = scores(first, *tasks[0][1:])
            for k, (u, e, b) in enumerate(tasks):
                p, s, ahead = first + u, ahead, None
                if k + 1 < len(tasks):
                    ahead = scores(first + tasks[k + 1][0], *tasks[k + 1][1:])
                top = jnp.max(s, axis=1, keepdims=True)
                pe = jnp.exp2(s - top)
                total = jnp.sum(pe, axis=1, keepdims=True)
                o = dot(pe.astype(BF), r.KV[l, 2 * p + e])
                outs[e, b] = o * (1.0 / total)
                lses[e, b] = top + jnp.log(total) * LOG2E
                if e == 1:
                    rows = pl.ds(TL * b, TL)
                    tile = r.QX[l, rows, :].astype(F32)
                    for e2 in range(2):
                        hi, mid, lo = split3(-lses[e2, b])
                        at = lane_t - (8 + 3 * (2 * p + e2))
                        tile = jnp.where(at == 0, hi, jnp.where(at == 1, mid, jnp.where(at == 2, lo, tile)))
                    r.QX[l, rows, :] = tile.astype(BF)
                    both = jnp.where(lane_t < 64, outs[1, b], outs[0, b])
                    r.att[l, rows, pl.ds(pl.multiple_of(p * 128, 128), 128)] = both.astype(BF)
            return 0

        steps = n_heads // 4 // pairs
        for half in range(2):
            sends[half].wait()
            lax.fori_loop(half * steps, half * steps + steps, attend, 0)
        if l == 0:
            for l2 in range(L):
                for c in wos[l2]:
                    c.wait()
        branch = dot(r.att[l], r.wo[l].reshape(D, D))

        def after_attn(i, _):
            rows = rows_of(i)
            br = branch
            r.dual[rows, :] = r.dual[rows, :] + br
            n, rs = normalise(r.x[rows, :] + br)
            r.n_attn[l, rows, :] = n.astype(BF)
            keep_rs(2 * l, rows, rs)
            y = n * gain[2 * l : 2 * l + 1, :] + bias[2 * l : 2 * l + 1, :]
            r.x[rows, :] = y
            r.low_mid[l, rows, :] = y.astype(BF)
            return 0

        after_attn(0, 0)
        ups[l][0].wait()
        downs[l][0].wait()
        if l > 0:
            hold["act_s"].wait()
            hold["gp_s"].wait()
        fb = 256

        def up(j):
            return dot(r.low_mid[l], r.wup[:, j * fb : (j + 1) * fb])

        ahead = up(0)
        for j in range(FF // fb):
            hidden, ahead = ahead, up(j + 1) if j + 1 < FF // fb else None
            cols = slice(j * fb, (j + 1) * fb)
            a, gp = gelu_parts(hidden)
            r.act[:, cols] = a.astype(BF)
            r.gp[:, cols] = gp.astype(BF)
        branch = dot(r.act[...], r.wdown[...])
        if l < L - 1:
            hold["act_s"] = local(r.act, s_act.at[l], "act_s")
            hold["gp_s"] = local(r.gp, s_gp.at[l], "gp_s")
            hold["act_s"].start()
            hold["gp_s"].start()
            ups[l + 1][0].start()
            downs[l + 1][0].start()

        def after_ffn(i, _):
            rows = rows_of(i)
            br = branch
            r.dual[rows, :] = r.dual[rows, :] + br
            n, rs = normalise(r.x[rows, :] + br)
            r.n_ffn[l, rows, :] = n.astype(BF)
            keep_rs(2 * l + 1, rows, rs)
            r.x[rows, :] = n * gain[2 * l + 1 : 2 * l + 2, :] + bias[2 * l + 1 : 2 * l + 2, :]
            return 0

        after_ffn(0, 0)

    for l in range(L):
        forward(l)

    cot_l.wait()
    cot_r.wait()
    k = 2 * L
    zero = jnp.zeros((8, D), F32)
    r.GB[...] = jnp.zeros((16, D), F32)

    def put_gb(row, acc):
        r.GB[row : row + 1, :] = jnp.sum(acc[0], axis=0, keepdims=True)
        r.GB[8 + row : 9 + row, :] = jnp.sum(acc[1], axis=0, keepdims=True)

    for b in range(2):

        def ending(i, acc, b=b):
            rows = pl.ds(TL * b, TL)
            part = pl.ds(0, TL)
            n, rs = normalise(r.dual[rows, :])
            res = r.x[rows, :] + n * gain[k : k + 1, :] + bias[k : k + 1, :]
            g = r.cot[b, part, :].astype(F32)
            r.cot[b, part, :] = res.astype(BF)
            r.x[rows, :] = g
            r.dual[rows, :] = norm_back(g, n, rs, gain[k : k + 1, :])
            return acc[0] + fold(g * n), acc[1] + fold(g)

        acc = ending(0, (zero, zero) if b == 0 else acc)
    put_gb(k, acc)
    res_l = local(r.cot.at[xc], o_res.at[xc], "res_l")
    res_r = remote(r.cot.at[1 - xc], o_res.at[xc], "res_r", XP)
    res_l.start()
    res_r.start()

    def norm_pull(row, n_ref, l):
        def step(i, acc):
            rows = rows_of(i)
            g, n = r.x[rows, :], n_ref[l, rows, :].astype(F32)
            pre = norm_back(g, n, r.RS[rows, row : row + 1], gain[row : row + 1, :])
            r.x[rows, :] = pre
            r.gb[rows, :] = (pre + r.dual[rows, :]).astype(BF)
            return acc[0] + fold(g * n), acc[1] + fold(g)

        put_gb(row, step(0, (zero, zero)))

    def store_rows(ch, res, cols, swap=False):
        g = ref["G" + ch.name]
        rr = plan.r
        piece = min(rr, 64)
        for d in range(plan.nd):
            for q in range(4):
                for s in range(0, rr, piece):
                    src = (4 * d + q) * rr + s
                    if swap:
                        src = src ^ 64
                    idx = (q % 2, q // 2) + tuple((d >> b) & 1 for b in reversed(range(nb)))
                    g[idx + (slice(s, s + piece), cols)] = res[src : src + piece].astype(BF)

    def exchange_gb(i):
        pat = ([CORE, XP] + [[("dp", 1 << b)] for b in range(nb)])[i]
        return remote(r.GB, r.GBR.at[i], f"GB{i}", pat)

    order = list(plan.chunks.values())

    todo = schedule(plan)

    def step_chunks(point, l):
        for act, *at in todo.get((point, l), ()):
            act(env, *at)
        if (point, l) in GB_STEPS:
            i = GB_STEPS.index((point, l))
            if 0 < i <= 2 + nb:
                exchange_gb(i - 1).wait()
                r.GB[...] = r.GB[...] + r.GBR[i - 1]
            if i < 2 + nb:
                exchange_gb(i).start()

    def backward_ffn(l):
        norm_pull(2 * l + 1, r.n_ffn, l)
        if l < L - 1:
            for c in (hold["act_b"], hold["gp_b"], ups[l][1], downs[l][1]):
                c.wait()
        ch = plan.chunks["D", l]
        gbt = r.gb[...].astype(F32).T.astype(BF)
        dcols = ch.cols
        g = ref["G" + ch.name]
        for d in range(plan.nd):
            idx = tuple((d >> b) & 1 for b in reversed(range(nb)))
            step = min(dcols, 512)
            for s in range(0, dcols, step):
                res = dot(gbt, r.act[:, d * dcols + s : d * dcols + s + step])
                for q in range(4):
                    g[(q % 2, q // 2) + idx + (slice(None), slice(s, s + step))] = res[
                        q * ch.rows : (q + 1) * ch.rows
                    ].astype(BF)
        step_chunks(DOWN, l)
        fb = 512

        def down_back(j):
            return dot_t(r.gb[...], r.wdown[j * fb : (j + 1) * fb, :])

        ahead = down_back(0)
        for j in range(FF // fb):
            gact, ahead = ahead, down_back(j + 1) if j + 1 < FF // fb else None
            cols = slice(j * fb, (j + 1) * fb)
            r.gp[:, cols] = (gact * r.gp[:, cols].astype(F32)).astype(BF)
        step_chunks(HID, l)
        ch = plan.chunks["U", l]
        lmt = r.low_mid[l].astype(F32).T.astype(BF)
        for j in range(FF // fb):
            res = dot(lmt, r.gp[:, j * fb : (j + 1) * fb])
            store_rows(ch, res, slice(j * fb, (j + 1) * fb))
        step_chunks(UP, l)
        r.x[...] = r.x[...] + dot_t(r.gp[...], r.wup[...])
        step_chunks(GN, l)
        if l > 0:
            hold["act_b"] = local(s_act.at[l - 1], r.act, "act_b")
            hold["gp_b"] = local(s_gp.at[l - 1], r.gp, "gp_b")
            for c in (hold["gp_b"], ups[l - 1][1], downs[l - 1][1]):
                c.start()

    def backward_attn(l):
        norm_pull(2 * l, r.n_attn, l)
        step_chunks(NORM_A, l)
        ch = plan.chunks["O", l]
        res = dot(r.att[l].astype(F32).T.astype(BF), r.gb[...])
        store_rows(ch, res, slice(None), swap=True)
        step_chunks(OUT, l)
        r.gb[...] = dot_t(r.gb[...], r.wo[l].reshape(D, D)).astype(BF)
        lane_t = lax.broadcasted_iota(jnp.int32, (T, 128), 1)
        scale = [
            jnp.where(lane1 < 64, 1.0 / LOG2E, 1.0),
            jnp.where(lane1 < 64, 1.0, 1.0 / LOG2E),
        ]

        def dkv_copy(h, name_h):
            ss, rs = plan.misc[f"dkv{l}0"]
            return pltpu.make_async_remote_copy(
                src_ref=r.ksend.at[h],
                dst_ref=r.krecv.at[h],
                send_sem=sems.at[ss + 2 * h],
                recv_sem=sems.at[rs + 2 * h],
                device_id=partner(CORE),
                device_id_type=MESH,
            )

        def pair(p, _):
            tile = pl.ds(pl.multiple_of(p * 128, 128), 128)
            att = r.att[l, :, tile].astype(F32)
            given = []
            for e in range(2):
                h = 2 * p + e
                q = r.Q[l, p] * m_of[e]
                at = lane1 - (8 + 3 * h)
                mine = jnp.where(
                    jnp.logical_or(lane1 < 4, jnp.logical_and(at >= 0, at < 3)), 1.0, 0.0
                ).astype(BF)
                do = r.gb[:, tile] * m_of[1 - e]
                centre = jnp.sum(att * do.astype(F32), axis=1, keepdims=True)
                hi, mid, lo = split3(-centre)
                ed = jnp.where(
                    lane_t == 4, hi, jnp.where(lane_t == 5, mid, jnp.where(lane_t == 6, lo, 0.0))
                ).astype(BF)
                qd = jnp.concatenate(
                    [
                        jnp.concatenate([q, r.QX[l] * mine], axis=1),
                        jnp.concatenate([do, ed], axis=1),
                    ],
                    axis=0,
                )
                given.append((h, qd, jnp.concatenate([do, q], axis=0)))

            def scores(e, j):
                h, qd, _ = given[e]
                rows = pl.ds(T * j, T)
                return dot_t(jnp.concatenate([r.KV[l, h, rows, :], r.E[rows, :]], axis=1), qd)

            dqts = [0.0, 0.0]

            def products(e, j, pr, ds):
                h, _, dq_in = given[e]
                dkv = dot(jnp.concatenate([pr, ds], axis=1), dq_in) * scale[e]
                dqts[e] = dqts[e] + dot_lt(r.KV[l, h, pl.ds(T * j, T), :], ds)
                if j == 1:
                    r.ksend[h] = dkv.astype(BF)
                    dkv_copy(h, None).start()
                else:
                    r.act[:, pl.ds(pl.multiple_of(D + h * 128, 128), 128)] = dkv.astype(BF)
                    for at in range(n_heads // 2):
                        point = HEAD + 2 * at + e
                        if todo.get((point, l)) or (point, l) in GB_STEPS:

                            @pl.when(p == at)
                            def _(point=point):
                                step_chunks(point, l)

            tasks = [(e, j) for e in range(2) for j in (1, 0)]
            ahead, behind = scores(*tasks[0]), None
            for k, (e, j) in enumerate(tasks):
                ss, ahead = ahead, scores(*tasks[k + 1]) if k + 1 < len(tasks) else None
                pr = jnp.exp2(ss[:, :T])
                ds = (pr * ss[:, T:]).astype(BF)
                if behind is not None:
                    products(*behind)
                behind = (e, j, pr.astype(BF), ds)
            products(*behind)
            dq = jnp.concatenate([dqts[0][:64], dqts[1][64:]], axis=0).T * (1.0 / 8.0)
            r.act[:, tile] = dq.astype(BF)
            return 0

        lax.fori_loop(0, n_heads // 2, pair, 0)
        for h in range(n_heads):
            dkv_copy(h, None).wait()
            cols = slice(D + 128 * h, D + 128 * h + 128)
            r.act[:, cols] = (r.act[:, cols].astype(F32) + r.krecv[h].astype(F32)).astype(BF)
        ch = plan.chunks["Q", l]
        lit = r.low_in[l].reshape(T, D).astype(F32).T.astype(BF)
        for j in range(3):
            cols = slice(j * D, (j + 1) * D)
            store_rows(ch, dot(lit, r.act[:, cols]), cols)
        step_chunks(QKV, l)
        back = dot_t(r.act[:, :D], r.wq[l]) + dot_t(r.act[:, D : 3 * D], r.wkv[l])
        r.x[...] = r.x[...] + back
        step_chunks(GN2, l)
        if l > 0:
            hold["act_b"].start()

    for l in reversed(range(L)):
        backward_ffn(l)
        backward_attn(l)

    res_l.wait()
    res_r.wait()
    for b in range(2):
        rows = pl.ds(TL * b, TL)
        r.cot[b] = (r.x[rows, :] + r.dual[rows, :]).astype(BF)
    gt_l = local(r.cot.at[xc], o_gtok.at[xc], "gtok_l")
    gt_r = remote(r.cot.at[1 - xc], o_gtok.at[xc], "gtok_r", XP)
    gt_l.start()
    gt_r.start()
    for i in range(2 + nb):
        if i + 1 >= len(GB_STEPS):
            exchange_gb(i).start()
            exchange_gb(i).wait()
            r.GB[...] = r.GB[...] + r.GBR[i]
    gb_out = local(r.GB, o_gb, "gb_out")
    gb_out.start()
    step_chunks(*TAIL)
    for ch in order:
        ch.complete(env)
    gb_out.wait()
    gt_l.wait()
    gt_r.wait()


def body(nd, tokens, counts, lengths, wqkv, wo, wup, wdown, gain, bias, cot):
    layers, width = wo.shape[0], wo.shape[2]
    ff = wup.shape[2]
    tl = tokens.shape[1]
    plan = make_plan(layers, tl, width, ff, nd)
    names = list(plan.scratch)
    any_spec = pl.BlockSpec(memory_space=pl.ANY)
    vmem = pl.BlockSpec(memory_space=pltpu.VMEM)
    smem = pl.BlockSpec(memory_space=pltpu.SMEM)
    rr = plan.r
    sd = jax.ShapeDtypeStruct
    outs = pl.pallas_call(
        partial(kernel, plan, names),
        out_shape=(
            sd(tokens.shape, BF),
            sd(tokens.shape, BF),
            sd((layers, 4, rr, 3 * width), BF),
            sd((layers, 4, rr, width), BF),
            sd((layers, 4, rr, ff), BF),
            sd((layers, ff // nd, width), BF),
            sd((16, width), F32),
            sd((max(layers - 1, 1), 2 * tl, ff), BF),
            sd((max(layers - 1, 1), 2 * tl, ff), BF),
        ),
        in_specs=[any_spec, smem, smem, any_spec, any_spec, any_spec, any_spec, vmem, vmem, any_spec],
        out_specs=[any_spec] * 9,
        scratch_shapes=[plan.scratch[k] for k in names] + [pltpu.SemaphoreType.DMA((plan.n_sem,))],
        compiler_params=pltpu.CompilerParams(
            collective_id=0, has_side_effects=True, vmem_limit_bytes=60 * 2**20
        ),
    )(
        tokens,
        counts,
        lengths,
        wqkv,
        wo.reshape(layers, HEADS // 2, 2, 64, width),
        wup,
        wdown,
        gain,
        bias,
        cot,
    )
    res, gtok, gq, go, gu, gd, gb = outs[:7]
    result = res.astype(F32)
    grad_tokens = gtok.astype(F32)
    grads = [
        gq.astype(F32).reshape(layers, 4 * rr, 3 * width),
        go.astype(F32).reshape(layers, 4 * rr, width),
        gu.astype(F32).reshape(layers, 4 * rr, ff),
        gd.astype(F32),
    ]
    norms = gain.shape[0]
    gains = [gb[:norms], gb[8 : 8 + norms]]
    size = lax.axis_size("dp")
    summed_here = nd == size
    if summed_here:
        piece = width // size
        start = lax.axis_index("dp") * piece
        gains = [lax.dynamic_slice(g, (0, start), (norms, piece)) for g in gains]
    if not summed_here:
        grads = [lax.psum_scatter(g, "dp", scatter_dimension=1, tiled=True) for g in grads]
        gains = [lax.psum_scatter(g, "dp", scatter_dimension=1, tiled=True) for g in gains]
    return (result, grad_tokens, *grads, *gains)


def solution(mesh):
    dp = mesh.shape["dp"]
    nd = dp if dp & (dp - 1) == 0 and 512 % (64 * dp) == 0 else 1
    return jax.shard_map(
        partial(body, nd),
        mesh=mesh,
        in_specs=(
            P("dp", "head", None),
            P("dp"),
            P("dp", None),
            P(),
            P(),
            P(),
            P(),
            P(),
            P(),
            P("dp", "head", None),
        ),
        out_specs=(
            P("dp", "head", None),
            P("dp", "head", None),
            P(None, "dp", None),
            P(None, "dp", None),
            P(None, "dp", None),
            P(None, "dp", None),
            P(None, "dp"),
            P(None, "dp"),
        ),
        check_vma=False,
    )
```

```python
import math
from functools import partial
from types import SimpleNamespace

import jax
import jax.numpy as jnp
import numpy as np
from jax import lax
from jax.experimental import pallas as pl
from jax.experimental.pallas import tpu as pltpu
from jax.sharding import PartitionSpec as P

HEADS = 8
EPS = 1e-05
NEG = -1e30
LOG2E = 1.4426950408889634
BF = jnp.bfloat16
F32 = jnp.float32
MESH = pl.DeviceIdType.MESH


DOWN, HID, UP, GN, NORM_A, OUT, HEAD = range(7)
QKV, GN2 = HEAD + HEADS, HEAD + HEADS + 1
TAIL = (GN2 + 1, -1)

EVENTS = {
    (GN, 1): (10, 11, 12),
    (HEAD, 1): (110, 111, 112),
    (HEAD + 1, 1): (210,),
    (HEAD + 3, 1): (10, 11, 12),
    (HEAD + 5, 1): (112,),
    (HEAD + 6, 1): (110, 111, 210),
    (HEAD + 7, 1): (10, 12),
    (QKV, 1): (11,),
    (GN2, 1): (112,),
    (DOWN, 0): (110, 111, 310, 311, 312),
    (HID, 0): (10, 210, 11, 12),
    (UP, 0): (112,),
    (GN, 0): (0, 1, 2),
    (NORM_A, 0): (110, 111),
    (HEAD, 0): (210, 310, 100, 101, 102),
    (HEAD + 1, 0): (10, 312, 200),
    (HEAD + 2, 0): (11, 12, 311),
    (HEAD + 3, 0): (112, 0),
    (HEAD + 4, 0): (310, 1, 2),
    (HEAD + 5, 0): (110, 111, 210),
    (HEAD + 7, 0): (312, 100, 101, 102),
    (QKV, 0): (0, 2, 200),
    (GN2, 0): (311,),
    TAIL: (
        310, 312, 300, 301, 302, 1, 100, 102, 2, 311, 101, 200,
        0, 312, 300, 302, 100, 2, 301, 311, 102, 0, 1, 101,
        302, 200, 100, 301, 300, 102, 1, 302, 101, 301, 200, 300,
        302, 301,
    ),
}


GB_STEPS = [(p, 0) for p in (NORM_A, HEAD + 1, HEAD + 3, HEAD + 5, HEAD + 7, GN2)]


def dot(a, b):
    return jnp.dot(a, b, preferred_element_type=F32)


def dot_t(a, b):
    return lax.dot_general(a, b, (((1,), (1,)), ((), ())), preferred_element_type=F32)


def dot_lt(a, b):
    return lax.dot_general(a, b, (((0,), (0,)), ((), ())), preferred_element_type=F32)


def gelu_parts(h):
    t = 1.0 / (1.0 + (0.3275911 * math.sqrt(0.5)) * jnp.abs(h))
    e = jnp.exp2(h * h * (-0.5 * LOG2E))
    poly = 0.5 * 1.061405429
    for a in (-1.453152027, 1.421413741, -0.284496736, 0.254829592):
        poly = poly * t + 0.5 * a
    q = poly * t * e
    phi = jnp.where(h >= 0.0, 1.0 - q, q)
    return h * phi, phi + h * (e * (1.0 / math.sqrt(2.0 * math.pi)))


def split3(v):
    hi = v.astype(BF).astype(F32)
    rest = v - hi
    mid = rest.astype(BF).astype(F32)
    return hi, mid, rest - mid


class Plan:
    def __init__(self, layers, tl, width, ff, nd):
        self.L, self.TL, self.D, self.FF, self.nd = layers, tl, width, ff, nd
        self.T = 2 * tl
        self.nb = nd.bit_length() - 1
        self.r = width // nd // 4
        self.scratch = {}
        self.n_sem = 0

    def add(self, name, shape, dtype):
        self.scratch[name] = pltpu.VMEM(tuple(shape), dtype)

    def sem(self):
        self.n_sem += 1
        return self.n_sem - 1


def axes_of(nb):
    return [("head", 1), ("head", 2)] + [("dp", 1 << b) for b in reversed(range(nb))]


X, Y, Z1, Z2 = ("head", 2), ("dp", 1), ("dp", 2), ("dp", 4)
ORDER_X = [[X], [Y], [Z1], [Z2]]
ORDER_Y = [[Y], [Z1], [X], [Z2]]
ORDER_Z = [[Z1], [X], [Y], [Z2]]
ORDERS = {
    "D": [ORDER_X, ORDER_Y, ORDER_Z],
    "U": [ORDER_X, ORDER_Y, ORDER_Z],
    "O": [[[Z1], [Y], [X], [Z2]]],
    "Q": [[[Y], [X], [Z1, Z2]], ORDER_Y, [[Z1], [Y], [X], [Z2]]],
}
SHARES = {"D": (3, 3, 2), "U": (6, 6, 4), "O": (1,), "Q": (4, 4, 4)}


class Part:
    def __init__(self, chunk, number, rows, cols):
        plan, nb = chunk.plan, chunk.plan.nb
        self.chunk, self.rows, self.cols = chunk, rows, cols
        self.name = f"{chunk.name}{number}"
        self.axes = axes_of(nb)
        known = [[a for a in s if a in self.axes] for s in ORDERS[chunk.kind][number]]
        self.stages = [[("head", 1)]] + [s for s in known if s]
        rest = [a for a in self.axes if not any(a in s for s in self.stages)]
        self.stages += [[a] for a in rest]
        self.patterns, self.sems = [], []
        left = len(self.axes)
        for s, dims in enumerate(self.stages):
            left -= len(dims)
            pats = [
                [dims[i] for i in range(len(dims)) if m >> i & 1] for m in range(1, 1 << len(dims))
            ]
            self.patterns.append(pats)
            size = [rows.stop - rows.start, cols.stop - cols.start]
            plan.add(f"R{self.name}_{s}", [len(pats)] + [2] * left + size, BF)
            self.sems.append([(plan.sem(), plan.sem()) for _ in pats])
        self.at = 0

    def index(self, env, stage, flipped):
        done = [a for s in self.stages[:stage] for a in s]
        out = []
        for a in self.axes:
            bit = env.bits[a]
            if a in done:
                out.append(bit)
            elif a in self.stages[stage]:
                out.append(1 - bit if a in flipped else bit)
            else:
                out.append(slice(None))
        return tuple(out)

    def copies(self, env, stage):
        for i, (pat, (ss, rs)) in enumerate(zip(self.patterns[stage], self.sems[stage])):
            yield pltpu.make_async_remote_copy(
                src_ref=env.ref["G" + self.chunk.name].at[
                    self.index(env, stage, pat) + (self.rows, self.cols)
                ],
                dst_ref=env.ref[f"R{self.name}_{stage}"].at[i],
                send_sem=env.sems.at[ss],
                recv_sem=env.sems.at[rs],
                device_id=env.partner(pat),
                device_id_type=MESH,
            )

    def finish(self, env, stage):
        for c in self.copies(env, stage):
            c.wait()
        own = self.index(env, stage, ())
        g = env.ref["G" + self.chunk.name]
        got = env.ref[f"R{self.name}_{stage}"]
        left = sum(isinstance(o, slice) for o in own)
        for at in np.ndindex(*[2] * left):
            piece = iter(at)
            here = tuple(next(piece) if isinstance(o, slice) else o for o in own)
            here = here + (self.rows, self.cols)
            total = g[here].astype(F32)
            for i in range(len(self.patterns[stage])):
                total = total + got[(i, *at)].astype(F32)
            g[here] = total.astype(BF)

    def step(self, env, at):
        if at > 0:
            self.finish(env, at - 1)
        if at < len(self.stages):
            for c in self.copies(env, at):
                c.start()


class Chunk:
    def __init__(self, plan, kind, layer):
        self.kind, self.layer, self.plan = kind, layer, plan
        self.name = f"{kind}{layer}"
        nb, r = plan.nb, plan.r
        rows, cols = {
            "U": (r, plan.FF),
            "O": (r, plan.D),
            "Q": (r, 3 * plan.D),
            "D": (plan.D // 4, plan.FF // plan.nd),
        }[kind]
        self.rows, self.cols = rows, cols
        plan.add("G" + self.name, [2] * (2 + nb) + [rows, cols], BF)
        out_shape = (cols, rows) if kind == "D" else (rows, cols)
        plan.add("P" + self.name, out_shape, BF)
        self.parts, start, shares = [], 0, SHARES[kind]
        for number, share in enumerate(shares):
            whole = rows if kind == "D" else cols
            stop = start + whole * share // sum(shares)
            span = slice(start, stop)
            if kind == "D":
                self.parts.append(Part(self, number, span, slice(0, cols)))
            else:
                self.parts.append(Part(self, number, slice(0, rows), span))
            start = stop
        self.last_sems = [(plan.sem(), plan.sem()) for _ in range(3)]
        self.local_sem = plan.sem()
        self.to_do = len(self.parts)

    def parts_done(self, env):
        own = tuple(env.bits[a] for a in axes_of(self.plan.nb))
        total = env.ref["G" + self.name][own]
        if self.kind == "D":
            total = total.astype(F32).T
        if self.kind == "Q":
            total = total.astype(F32)
            d = self.plan.D
            lo = lax.broadcasted_iota(jnp.int32, (self.rows, 128), 1) < 64
            tiles = []
            for p in range(HEADS // 2):
                q = total[:, 128 * p : 128 * p + 128]
                k0 = pltpu.roll(total[:, d + 256 * p : d + 256 * p + 128], 64, 1)
                k1 = pltpu.roll(total[:, d + 256 * p + 128 : d + 256 * p + 256], 64, 1)
                tiles += [jnp.where(lo, q, k0), jnp.where(lo, k0, q), k1]
            total = jnp.concatenate(tiles, axis=1)
        env.ref["P" + self.name][...] = total.astype(BF)
        for c in self.spread(env)[:3]:
            c.start()

    def place(self, env, quarter):
        out = env.out[self.kind]
        if self.kind == "D":
            cols = pl.ds(pl.multiple_of(quarter * self.rows, self.rows), self.rows)
            return out.at[self.layer, :, cols]
        return out.at[self.layer, quarter]

    def spread(self, env):
        core, x = ("head", 1), ("head", 2)
        src, here = env.ref["P" + self.name], self.place(env, env.head)
        there = self.place(env, env.partner([x])[1])
        copies = [pltpu.make_async_copy(src, here, env.sems.at[self.local_sem])]
        for (a, b, pat), (ss, rs) in zip(
            ((src, here, [x]), (src, here, [core]), (there, there, [core])), self.last_sems
        ):
            copies.append(
                pltpu.make_async_remote_copy(
                    src_ref=a,
                    dst_ref=b,
                    send_sem=env.sems.at[ss],
                    recv_sem=env.sems.at[rs],
                    device_id=env.partner(pat),
                    device_id_type=MESH,
                )
            )
        return copies

    def pass_on(self, env):
        copies = self.spread(env)
        copies[1].wait_recv()
        copies[3].start()

    def complete(self, env):
        copies = self.spread(env)
        copies[0].wait()
        copies[1].wait_send()
        copies[2].wait()
        copies[3].wait()


def schedule(plan):
    layers = sorted({l for _, l in plan.chunks}, reverse=True)
    ready = {DOWN: "D", UP: "U", OUT: "O", QKV: "Q"}
    todo = {}

    def advance(acts, ch, number):
        part = ch.parts[number]
        if part.at > len(part.stages):
            return
        acts.append((part.step, part.at))
        part.at += 1
        if part.at > len(part.stages):
            ch.to_do -= 1
            if ch.to_do == 0:
                acts.append((ch.parts_done,))

    for point in [(n, l) for l in layers for n in range(GN2 + 1)] + [TAIL]:
        acts = todo.setdefault(point, [])
        ch = plan.chunks.get((ready.get(point[0]), point[1]))
        if ch is not None:
            for i in range(len(ch.parts)):
                advance(acts, ch, i)
        for c in EVENTS.get(point, ()):
            ch = plan.chunks.get(("DUOQ"[c // 100], c // 10 % 10))
            if ch is None:
                continue
            advance(acts, ch, c % 10)
    for ch in plan.chunks.values():
        for i, part in enumerate(ch.parts):
            while part.at <= len(part.stages):
                advance(acts, ch, i)
    for ch in plan.chunks.values():
        acts.append((ch.pass_on,))
    return todo


def make_plan(layers, tl, width, ff, nd):
    plan = Plan(layers, tl, width, ff, nd)
    t, n = plan.T, HEADS
    add = plan.add
    add("x", (t, width), F32)
    add("dual", (t, width), F32)
    add("cot", (2, tl, width), BF)
    add("E", (4 * tl, 128), BF)
    add("EQ", (t, 128), BF)
    add("wq", (layers, width, width), BF)
    add("wkv", (layers, width, 2 * width), BF)
    add("wo", (layers, n // 2, 2, 64, width), BF)
    add("wup", (width, ff), BF)
    add("wdown", (ff, width), BF)
    add("low_in", (layers, 2, tl, width), BF)
    add("KV", (layers, n, 4 * tl, 128), BF)
    add("Q", (layers, n // 2, t, 128), BF)
    add("QX", (layers, t, 128), BF)
    add("att", (layers, t, width), BF)
    add("n_attn", (layers, t, width), BF)
    add("RS", (t, 128), F32)
    add("low_mid", (layers, t, width), BF)
    add("n_ffn", (layers, t, width), BF)
    add("act", (t, ff), BF)
    add("gp", (t, ff), BF)
    add("gb", (t, width), BF)
    add("ksend", (n, t, 128), BF)
    add("krecv", (n, t, 128), BF)
    add("GB", (16, width), F32)
    nbits = 2 + plan.nb
    add("GBR", (nbits, 16, width), F32)
    plan.chunks = {}
    for layer in reversed(range(layers)):
        for kind in "DUOQ":
            plan.chunks[kind, layer] = Chunk(plan, kind, layer)
    plan.misc = {}
    for name in (
        ["tok_l", "cot_l", "res_l", "gtok_l", "act_s", "gp_s", "act_b", "gp_b", "gb_out"]
        + [f"{w}{l}{i}" for l in range(layers) for w in ("wqkv", "wo0", "wo1", "wup", "wdown") for i in "ab"]
    ):
        plan.misc[name] = plan.sem()
    for name in (
        ["tok_r", "cot_r", "res_r", "gtok_r"]
        + [f"kv{l}{i}" for l in range(layers) for i in range(2)]
        + [f"dkv{l}{h}" for l in range(layers) for h in range(n)]
        + [f"GB{i}" for i in range(nbits)]
    ):
        plan.misc[name] = (plan.sem(), plan.sem())
    return plan


def kernel(plan, names, *refs):
    (tokens, counts, lengths, wqkv, wo, wup, wdown, gain, bias, cot) = refs[:10]
    (o_res, o_gtok, o_q, o_o, o_u, o_d, o_gb, s_act, s_gp) = refs[10:19]
    ref = dict(zip(names, refs[19:-1]))
    sems = refs[-1]
    r = SimpleNamespace(**{k: v for k, v in ref.items()})
    L, T, TL, D, FF, nb = plan.L, plan.T, plan.TL, plan.D, plan.FF, plan.nb
    n_heads = HEADS
    dp, head = lax.axis_index("dp"), lax.axis_index("head")
    core, xc = head % 2, head // 2
    bits = {("head", 1): core, ("head", 2): xc}
    for b in range(nb):
        bits["dp", 1 << b] = (dp // (1 << b)) % 2

    def partner(pat):
        d, h = dp, head
        for axis, bit in pat:
            v = bits[axis, bit]
            if axis == "dp":
                d = d + bit * (1 - 2 * v)
            else:
                h = h + bit * (1 - 2 * v)
        return (d, h)

    env = SimpleNamespace(
        ref=ref,
        sems=sems,
        bits=bits,
        partner=partner,
        head=head,
        out={"Q": o_q, "O": o_o, "U": o_u, "D": o_d},
    )
    CORE, XP = [("head", 1)], [("head", 2)]

    greet = [CORE, XP]
    for ch in plan.chunks.values():
        for part in ch.parts:
            for pats in part.patterns:
                for pat in pats:
                    if set(pat) not in [set(g) for g in greet]:
                        greet.append(pat)
    for b in range(nb):
        if [("dp", 1 << b)] not in greet:
            greet.append([("dp", 1 << b)])
    barrier = pltpu.get_barrier_semaphore()
    for pat in greet:
        pl.semaphore_signal(barrier, inc=1, device_id=partner(pat), device_id_type=MESH)

    def local(src, dst, name):
        return pltpu.make_async_copy(src, dst, sems.at[plan.misc[name]])

    def remote(src, dst, name, pat):
        ss, rs = plan.misc[name]
        return pltpu.make_async_remote_copy(
            src_ref=src,
            dst_ref=dst,
            send_sem=sems.at[ss],
            recv_sem=sems.at[rs],
            device_id=partner(pat),
            device_id_type=MESH,
        )

    stage_ref = [r.act, r.gp]
    raw = [
        local(wqkv.at[l], stage_ref[l].at[:, pl.ds(0, 3 * D)], f"wqkv{l}a") for l in range(L)
    ]
    raw[0].start()
    tok_l = local(tokens.at[xc], r.low_in.at[0, xc], "tok_l")
    tok_l.start()
    cot_l = local(cot.at[xc], r.cot.at[xc], "cot_l")
    wos = []
    for l in range(L):
        wos.append(
            [
                local(wo.at[l, :, e], r.wo.at[l, :, 1 - e], f"wo{e}{l}a")
                for e in range(2)
            ]
        )
    ups = [[local(wup.at[l], r.wup, f"wup{l}{i}") for i in "ab"[: L - l]] for l in range(L)]
    downs = [[local(wdown.at[l], r.wdown, f"wdown{l}{i}") for i in "ab"[: L - l]] for l in range(L)]
    pl.semaphore_wait(barrier, len(greet))
    tok_r = remote(tokens.at[1 - xc], r.low_in.at[0, xc], "tok_r", XP)
    tok_r.start()
    for c in raw[1:] + wos[0] + [ups[0][0], downs[0][0]] + sum(wos[1:], []) + [cot_l]:
        c.start()
    cot_r = remote(cot.at[1 - xc], r.cot.at[xc], "cot_r", XP)

    lane = lax.broadcasted_iota(jnp.int32, (TL, 128), 1)
    row = lax.broadcasted_iota(jnp.int32, (TL, 128), 0)
    count = counts[xc]
    several = count == 4
    for j in range(4):
        quarter = core + 2 * j if j < 2 else (1 - core) + 2 * (j - 2)
        limit_one = lengths[xc, 0] - TL * quarter
        limit = jnp.where(several, lengths[xc, quarter], limit_one)
        usable = row < limit
        same = jnp.logical_or(lane == quarter, jnp.logical_not(several))
        ok = jnp.logical_and(usable, same)
        tile = jnp.where(lane < 4, jnp.where(ok, 0.0, NEG), jnp.where(lane < 32, 1.0, 0.0))
        r.E[pl.ds(TL * j, TL), :] = tile.astype(BF)
    for b in range(2):
        tile = jnp.where(lane == core + 2 * b, 1.0, 0.0).astype(BF)
        r.EQ[pl.ds(TL * b, TL), :] = tile
        for l in range(L):
            r.QX[l, pl.ds(TL * b, TL), :] = tile

    low_half = lax.broadcasted_iota(jnp.int32, (D, 128), 1) < 64
    for l in range(L):
        raw[l].wait()

        def sort_pair(p, _, l=l):
            cols = lambda i: pl.ds(pl.multiple_of(p * 384 + 128 * i, 128), 128)
            t0 = stage_ref[l][:, cols(0)].astype(F32)
            t1 = stage_ref[l][:, cols(1)].astype(F32)
            t2 = stage_ref[l][:, cols(2)].astype(F32)
            r0, r1, r2 = (pltpu.roll(t, 64, 1) for t in (t0, t1, t2))
            r.wq[l, :, pl.ds(pl.multiple_of(p * 128, 128), 128)] = jnp.where(low_half, t0, t1).astype(BF)
            r.wkv[l, :, pl.ds(pl.multiple_of(p * 256, 128), 128)] = jnp.where(low_half, r0, r1).astype(BF)
            r.wkv[l, :, pl.ds(pl.multiple_of(p * 256 + 128, 128), 128)] = r2.astype(BF)
            return 0

        lax.fori_loop(0, n_heads // 2, sort_pair, 0)

    lane1 = lax.broadcasted_iota(jnp.int32, (1, 128), 1)
    m_lo = jnp.where(lane1 < 64, 1.0, 0.0).astype(BF)
    m_hi = jnp.where(lane1 < 64, 0.0, 1.0).astype(BF)
    m_of = [m_lo, m_hi]
    CH = T

    def rows_of(i):
        return pl.ds(i * CH, CH)

    def normalise(v):
        mu = jnp.mean(v, axis=1, keepdims=True)
        cen = v - mu
        var = jnp.mean(cen * cen, axis=1, keepdims=True)
        rs = lax.rsqrt(var + EPS)
        return cen * rs, rs

    def norm_back(g, n, rs, gain_row):
        h = g * gain_row
        return rs * (
            h - jnp.mean(h, axis=1, keepdims=True) - n * jnp.mean(h * n, axis=1, keepdims=True)
        )

    def keep_rs(col, rows, rs):
        lanes = lax.broadcasted_iota(jnp.int32, (CH, 128), 1)
        r.RS[rows, :] = jnp.where(lanes == col, rs, r.RS[rows, :])

    def fold(v):
        return jnp.sum(v.reshape(v.shape[0] // 8, 8, D), axis=0)

    r.RS[...] = jnp.zeros((T, 128), F32)
    tok_l.wait()
    tok_r.wait()
    cot_r.start()
    for b in range(2):
        v = r.low_in[0, b].astype(F32)
        r.x[pl.ds(TL * b, TL), :] = v
        r.dual[pl.ds(TL * b, TL), :] = v

    hold = {}

    def forward(l):
        if l > 0:
            r.low_in[l] = r.x[...].astype(BF).reshape(2, TL, D)
        low = r.low_in[l].reshape(T, D)
        sends = []
        hh = n_heads // 2
        for half in range(2):
            kv = dot(low, r.wkv[l, :, D * half : D * half + D]).astype(BF)
            for i in range(hh):
                r.KV[l, half * hh + i, 0:T, :] = kv[:, 128 * i : 128 * i + 128]
            c = remote(
                r.KV.at[l, pl.ds(half * hh, hh), pl.ds(0, T)],
                r.KV.at[l, pl.ds(half * hh, hh), pl.ds(T, T)],
                f"kv{l}{half}",
                CORE,
            )
            c.start()
            sends.append(c)
        q = (dot(low, r.wq[l]) * (LOG2E / 8.0)).astype(BF)
        for p in range(n_heads // 2):
            r.Q[l, p] = q[:, 128 * p : 128 * p + 128]
        lane_t = lax.broadcasted_iota(jnp.int32, (TL, 128), 1)

        pairs = 1
        tasks = [(u, e, b) for u in range(pairs) for e in range(2) for b in range(2)]

        def scores(p, e, b):
            rows = pl.ds(TL * b, TL)
            kve = jnp.concatenate([r.KV[l, 2 * p + e], r.E[...]], axis=1)
            qe = jnp.concatenate([r.Q[l, p, rows, :] * m_of[e], r.EQ[rows, :]], axis=1)
            return dot_t(qe, kve)

        def attend(i, _):
            outs, lses = {}, {}
            first = i * pairs
            ahead = scores(first, *tasks[0][1:])
            for k, (u, e, b) in enumerate(tasks):
                p, s, ahead = first + u, ahead, None
                if k + 1 < len(tasks):
                    ahead = scores(first + tasks[k + 1][0], *tasks[k + 1][1:])
                top = jnp.max(s, axis=1, keepdims=True)
                pe = jnp.exp2(s - top)
                total = jnp.sum(pe, axis=1, keepdims=True)
                o = dot(pe.astype(BF), r.KV[l, 2 * p + e])
                outs[e, b] = o * (1.0 / total)
                lses[e, b] = top + jnp.log(total) * LOG2E
                if e == 1:
                    rows = pl.ds(TL * b, TL)
                    tile = r.QX[l, rows, :].astype(F32)
                    for e2 in range(2):
                        hi, mid, lo = split3(-lses[e2, b])
                        at = lane_t - (8 + 3 * (2 * p + e2))
                        tile = jnp.where(at == 0, hi, jnp.where(at == 1, mid, jnp.where(at == 2, lo, tile)))
                    r.QX[l, rows, :] = tile.astype(BF)
                    both = jnp.where(lane_t < 64, outs[1, b], outs[0, b])
                    r.att[l, rows, pl.ds(pl.multiple_of(p * 128, 128), 128)] = both.astype(BF)
            return 0

        steps = n_heads // 4 // pairs
        for half in range(2):
            sends[half].wait()
            lax.fori_loop(half * steps, half * steps + steps, attend, 0)
        if l == 0:
            for l2 in range(L):
                for c in wos[l2]:
                    c.wait()
        branch = dot(r.att[l], r.wo[l].reshape(D, D))

        def after_attn(i, _):
            rows = rows_of(i)
            br = branch
            r.dual[rows, :] = r.dual[rows, :] + br
            n, rs = normalise(r.x[rows, :] + br)
            r.n_attn[l, rows, :] = n.astype(BF)
            keep_rs(2 * l, rows, rs)
            y = n * gain[2 * l : 2 * l + 1, :] + bias[2 * l : 2 * l + 1, :]
            r.x[rows, :] = y
            r.low_mid[l, rows, :] = y.astype(BF)
            return 0

        after_attn(0, 0)
        ups[l][0].wait()
        downs[l][0].wait()
        if l > 0:
            hold["act_s"].wait()
            hold["gp_s"].wait()
        fb = 512

        def ffn_cols(j, _):
            cols = pl.ds(pl.multiple_of(j * fb, fb), fb)
            a, gp = gelu_parts(dot(r.low_mid[l], r.wup[:, cols]))
            r.act[:, cols] = a.astype(BF)
            r.gp[:, cols] = gp.astype(BF)
            return 0

        lax.fori_loop(0, FF // fb, ffn_cols, 0)
        branch = dot(r.act[...], r.wdown[...])
        if l < L - 1:
            hold["act_s"] = local(r.act, s_act.at[l], "act_s")
            hold["gp_s"] = local(r.gp, s_gp.at[l], "gp_s")
            hold["act_s"].start()
            hold["gp_s"].start()
            ups[l + 1][0].start()
            downs[l + 1][0].start()

        def after_ffn(i, _):
            rows = rows_of(i)
            br = branch
            r.dual[rows, :] = r.dual[rows, :] + br
            n, rs = normalise(r.x[rows, :] + br)
            r.n_ffn[l, rows, :] = n.astype(BF)
            keep_rs(2 * l + 1, rows, rs)
            r.x[rows, :] = n * gain[2 * l + 1 : 2 * l + 2, :] + bias[2 * l + 1 : 2 * l + 2, :]
            return 0

        after_ffn(0, 0)

    for l in range(L):
        forward(l)

    cot_l.wait()
    cot_r.wait()
    k = 2 * L
    zero = jnp.zeros((8, D), F32)
    r.GB[...] = jnp.zeros((16, D), F32)

    def put_gb(row, acc):
        r.GB[row : row + 1, :] = jnp.sum(acc[0], axis=0, keepdims=True)
        r.GB[8 + row : 9 + row, :] = jnp.sum(acc[1], axis=0, keepdims=True)

    for b in range(2):

        def ending(i, acc, b=b):
            rows = pl.ds(TL * b, TL)
            part = pl.ds(0, TL)
            n, rs = normalise(r.dual[rows, :])
            res = r.x[rows, :] + n * gain[k : k + 1, :] + bias[k : k + 1, :]
            g = r.cot[b, part, :].astype(F32)
            r.cot[b, part, :] = res.astype(BF)
            r.x[rows, :] = g
            r.dual[rows, :] = norm_back(g, n, rs, gain[k : k + 1, :])
            return acc[0] + fold(g * n), acc[1] + fold(g)

        acc = ending(0, (zero, zero) if b == 0 else acc)
    put_gb(k, acc)
    res_l = local(r.cot.at[xc], o_res.at[xc], "res_l")
    res_r = remote(r.cot.at[1 - xc], o_res.at[xc], "res_r", XP)
    res_l.start()
    res_r.start()

    def norm_pull(row, n_ref, l):
        def step(i, acc):
            rows = rows_of(i)
            g, n = r.x[rows, :], n_ref[l, rows, :].astype(F32)
            pre = norm_back(g, n, r.RS[rows, row : row + 1], gain[row : row + 1, :])
            r.x[rows, :] = pre
            r.gb[rows, :] = (pre + r.dual[rows, :]).astype(BF)
            return acc[0] + fold(g * n), acc[1] + fold(g)

        put_gb(row, step(0, (zero, zero)))

    def store_rows(ch, res, cols, swap=False):
        g = ref["G" + ch.name]
        rr = plan.r
        piece = min(rr, 64)
        for d in range(plan.nd):
            for q in range(4):
                for s in range(0, rr, piece):
                    src = (4 * d + q) * rr + s
                    if swap:
                        src = src ^ 64
                    idx = (q % 2, q // 2) + tuple((d >> b) & 1 for b in reversed(range(nb)))
                    g[idx + (slice(s, s + piece), cols)] = res[src : src + piece].astype(BF)

    def exchange_gb(i):
        pat = ([CORE, XP] + [[("dp", 1 << b)] for b in range(nb)])[i]
        return remote(r.GB, r.GBR.at[i], f"GB{i}", pat)

    order = list(plan.chunks.values())

    todo = schedule(plan)

    def step_chunks(point, l):
        for act, *at in todo.get((point, l), ()):
            act(env, *at)
        if (point, l) in GB_STEPS:
            i = GB_STEPS.index((point, l))
            if 0 < i <= 2 + nb:
                exchange_gb(i - 1).wait()
                r.GB[...] = r.GB[...] + r.GBR[i - 1]
            if i < 2 + nb:
                exchange_gb(i).start()

    def backward_ffn(l):
        norm_pull(2 * l + 1, r.n_ffn, l)
        if l < L - 1:
            for c in (hold["act_b"], hold["gp_b"], ups[l][1], downs[l][1]):
                c.wait()
        ch = plan.chunks["D", l]
        gbt = r.gb[...].astype(F32).T.astype(BF)
        dcols = ch.cols
        g = ref["G" + ch.name]
        for d in range(plan.nd):
            idx = tuple((d >> b) & 1 for b in reversed(range(nb)))
            step = min(dcols, 512)
            for s in range(0, dcols, step):
                res = dot(gbt, r.act[:, d * dcols + s : d * dcols + s + step])
                for q in range(4):
                    g[(q % 2, q // 2) + idx + (slice(None), slice(s, s + step))] = res[
                        q * ch.rows : (q + 1) * ch.rows
                    ].astype(BF)
        step_chunks(DOWN, l)
        fb = 512

        def hidden_cols(j, _):
            cols = pl.ds(pl.multiple_of(j * fb, fb), fb)
            gact = dot_t(r.gb[...], r.wdown[cols, :])
            r.gp[:, cols] = (gact * r.gp[:, cols].astype(F32)).astype(BF)
            return 0

        lax.fori_loop(0, FF // fb, hidden_cols, 0)
        step_chunks(HID, l)
        ch = plan.chunks["U", l]
        lmt = r.low_mid[l].astype(F32).T.astype(BF)
        for j in range(FF // fb):
            res = dot(lmt, r.gp[:, j * fb : (j + 1) * fb])
            store_rows(ch, res, slice(j * fb, (j + 1) * fb))
        step_chunks(UP, l)
        r.x[...] = r.x[...] + dot_t(r.gp[...], r.wup[...])
        step_chunks(GN, l)
        if l > 0:
            hold["act_b"] = local(s_act.at[l - 1], r.act, "act_b")
            hold["gp_b"] = local(s_gp.at[l - 1], r.gp, "gp_b")
            for c in (hold["gp_b"], ups[l - 1][1], downs[l - 1][1]):
                c.start()

    def backward_attn(l):
        norm_pull(2 * l, r.n_attn, l)
        step_chunks(NORM_A, l)
        ch = plan.chunks["O", l]
        res = dot(r.att[l].astype(F32).T.astype(BF), r.gb[...])
        store_rows(ch, res, slice(None), swap=True)
        step_chunks(OUT, l)
        r.gb[...] = dot_t(r.gb[...], r.wo[l].reshape(D, D)).astype(BF)
        lane_t = lax.broadcasted_iota(jnp.int32, (T, 128), 1)
        scale = [
            jnp.where(lane1 < 64, 1.0 / LOG2E, 1.0),
            jnp.where(lane1 < 64, 1.0, 1.0 / LOG2E),
        ]

        def dkv_copy(h, name_h):
            ss, rs = plan.misc[f"dkv{l}0"]
            return pltpu.make_async_remote_copy(
                src_ref=r.ksend.at[h],
                dst_ref=r.krecv.at[h],
                send_sem=sems.at[ss + 2 * h],
                recv_sem=sems.at[rs + 2 * h],
                device_id=partner(CORE),
                device_id_type=MESH,
            )

        def pair(p, _):
            tile = pl.ds(pl.multiple_of(p * 128, 128), 128)
            att = r.att[l, :, tile].astype(F32)
            given = []
            for e in range(2):
                h = 2 * p + e
                q = r.Q[l, p] * m_of[e]
                at = lane1 - (8 + 3 * h)
                mine = jnp.where(
                    jnp.logical_or(lane1 < 4, jnp.logical_and(at >= 0, at < 3)), 1.0, 0.0
                ).astype(BF)
                do = r.gb[:, tile] * m_of[1 - e]
                centre = jnp.sum(att * do.astype(F32), axis=1, keepdims=True)
                hi, mid, lo = split3(-centre)
                ed = jnp.where(
                    lane_t == 4, hi, jnp.where(lane_t == 5, mid, jnp.where(lane_t == 6, lo, 0.0))
                ).astype(BF)
                qd = jnp.concatenate(
                    [
                        jnp.concatenate([q, r.QX[l] * mine], axis=1),
                        jnp.concatenate([do, ed], axis=1),
                    ],
                    axis=0,
                )
                given.append((h, qd, jnp.concatenate([do, q], axis=0)))

            def scores(e, j):
                h, qd, _ = given[e]
                rows = pl.ds(T * j, T)
                return dot_t(jnp.concatenate([r.KV[l, h, rows, :], r.E[rows, :]], axis=1), qd)

            dqts = [0.0, 0.0]

            def products(e, j, pr, ds):
                h, _, dq_in = given[e]
                dkv = dot(jnp.concatenate([pr, ds], axis=1), dq_in) * scale[e]
                dqts[e] = dqts[e] + dot_lt(r.KV[l, h, pl.ds(T * j, T), :], ds)
                if j == 1:
                    r.ksend[h] = dkv.astype(BF)
                    dkv_copy(h, None).start()
                else:
                    r.act[:, pl.ds(pl.multiple_of(D + h * 128, 128), 128)] = dkv.astype(BF)
                    for at in range(n_heads // 2):
                        point = HEAD + 2 * at + e
                        if todo.get((point, l)) or (point, l) in GB_STEPS:

                            @pl.when(p == at)
                            def _(point=point):
                                step_chunks(point, l)

            tasks = [(e, j) for e in range(2) for j in (1, 0)]
            ahead, behind = scores(*tasks[0]), None
            for k, (e, j) in enumerate(tasks):
                ss, ahead = ahead, scores(*tasks[k + 1]) if k + 1 < len(tasks) else None
                pr = jnp.exp2(ss[:, :T])
                ds = (pr * ss[:, T:]).astype(BF)
                if behind is not None:
                    products(*behind)
                behind = (e, j, pr.astype(BF), ds)
            products(*behind)
            dq = jnp.concatenate([dqts[0][:64], dqts[1][64:]], axis=0).T * (1.0 / 8.0)
            r.act[:, tile] = dq.astype(BF)
            return 0

        lax.fori_loop(0, n_heads // 2, pair, 0)
        for h in range(n_heads):
            dkv_copy(h, None).wait()
            cols = slice(D + 128 * h, D + 128 * h + 128)
            r.act[:, cols] = (r.act[:, cols].astype(F32) + r.krecv[h].astype(F32)).astype(BF)
        ch = plan.chunks["Q", l]
        lit = r.low_in[l].reshape(T, D).astype(F32).T.astype(BF)
        for j in range(3):
            cols = slice(j * D, (j + 1) * D)
            store_rows(ch, dot(lit, r.act[:, cols]), cols)
        step_chunks(QKV, l)
        back = dot_t(r.act[:, :D], r.wq[l]) + dot_t(r.act[:, D : 3 * D], r.wkv[l])
        r.x[...] = r.x[...] + back
        step_chunks(GN2, l)
        if l > 0:
            hold["act_b"].start()

    for l in reversed(range(L)):
        backward_ffn(l)
        backward_attn(l)

    res_l.wait()
    res_r.wait()
    for b in range(2):
        rows = pl.ds(TL * b, TL)
        r.cot[b] = (r.x[rows, :] + r.dual[rows, :]).astype(BF)
    gt_l = local(r.cot.at[xc], o_gtok.at[xc], "gtok_l")
    gt_r = remote(r.cot.at[1 - xc], o_gtok.at[xc], "gtok_r", XP)
    gt_l.start()
    gt_r.start()
    for i in range(2 + nb):
        if i + 1 >= len(GB_STEPS):
            exchange_gb(i).start()
            exchange_gb(i).wait()
            r.GB[...] = r.GB[...] + r.GBR[i]
    gb_out = local(r.GB, o_gb, "gb_out")
    gb_out.start()
    step_chunks(*TAIL)
    for ch in order:
        ch.complete(env)
    gb_out.wait()
    gt_l.wait()
    gt_r.wait()


def body(nd, tokens, counts, lengths, wqkv, wo, wup, wdown, gain, bias, cot):
    layers, width = wo.shape[0], wo.shape[2]
    ff = wup.shape[2]
    tl = tokens.shape[1]
    plan = make_plan(layers, tl, width, ff, nd)
    names = list(plan.scratch)
    any_spec = pl.BlockSpec(memory_space=pl.ANY)
    vmem = pl.BlockSpec(memory_space=pltpu.VMEM)
    smem = pl.BlockSpec(memory_space=pltpu.SMEM)
    rr = plan.r
    sd = jax.ShapeDtypeStruct
    outs = pl.pallas_call(
        partial(kernel, plan, names),
        out_shape=(
            sd(tokens.shape, BF),
            sd(tokens.shape, BF),
            sd((layers, 4, rr, 3 * width), BF),
            sd((layers, 4, rr, width), BF),
            sd((layers, 4, rr, ff), BF),
            sd((layers, ff // nd, width), BF),
            sd((16, width), F32),
            sd((max(layers - 1, 1), 2 * tl, ff), BF),
            sd((max(layers - 1, 1), 2 * tl, ff), BF),
        ),
        in_specs=[any_spec, smem, smem, any_spec, any_spec, any_spec, any_spec, vmem, vmem, any_spec],
        out_specs=[any_spec] * 9,
        scratch_shapes=[plan.scratch[k] for k in names] + [pltpu.SemaphoreType.DMA((plan.n_sem,))],
        compiler_params=pltpu.CompilerParams(
            collective_id=0, has_side_effects=True, vmem_limit_bytes=60 * 2**20
        ),
    )(
        tokens,
        counts,
        lengths,
        wqkv,
        wo.reshape(layers, HEADS // 2, 2, 64, width),
        wup,
        wdown,
        gain,
        bias,
        cot,
    )
    wide = list(outs[:6])
    for i, cols in ((2, 3 * width), (3, width), (4, ff)):
        wide[i] = wide[i].reshape(layers, 4 * rr, cols)
    norms = gain.shape[0]
    size = lax.axis_size("dp")
    piece = width // size
    summed_here = nd == size

    def widen(*refs):
        src, dst, narrow, full = refs[:7], refs[7:15], refs[15:22], refs[22:28]
        sems = refs[28]
        into = [pltpu.make_async_copy(a, b, sems.at[i]) for i, (a, b) in enumerate(zip(src, narrow))]
        away = [pltpu.make_async_copy(a, b, sems.at[7 + i]) for i, (a, b) in enumerate(zip(full, dst))]
        for c in into:
            c.start()
        for i in range(6):
            into[i].wait()
            full[i][...] = narrow[i][...].astype(F32)
            away[i].start()
        into[6].wait()
        gb = narrow[6][...]
        if summed_here:
            start = lax.axis_index("dp") * piece
            gb = pltpu.roll(gb, lax.rem(width - start, width), 1)[:, :piece]
        dst[6][...] = gb[:norms]
        dst[7][...] = gb[8 : 8 + norms]
        for c in away:
            c.wait()

    gcols = piece if summed_here else width
    result, grad_tokens, *grads, gain_rows, bias_rows = pl.pallas_call(
        widen,
        out_shape=[sd(w.shape, F32) for w in wide] + [sd((norms, gcols), F32)] * 2,
        in_specs=[any_spec] * 7,
        out_specs=[any_spec] * 6 + [vmem] * 2,
        scratch_shapes=[pltpu.VMEM(w.shape, BF) for w in wide]
        + [pltpu.VMEM(outs[6].shape, F32)]
        + [pltpu.VMEM(w.shape, F32) for w in wide]
        + [pltpu.SemaphoreType.DMA((13,))],
        compiler_params=pltpu.CompilerParams(vmem_limit_bytes=56 * 2**20),
    )(*wide, outs[6])
    gains = [gain_rows, bias_rows]
    if not summed_here:
        grads = [lax.psum_scatter(g, "dp", scatter_dimension=1, tiled=True) for g in grads]
        gains = [lax.psum_scatter(g, "dp", scatter_dimension=1, tiled=True) for g in gains]
    return (result, grad_tokens, *grads, *gains)


def solution(mesh):
    dp = mesh.shape["dp"]
    nd = dp if dp & (dp - 1) == 0 and 512 % (64 * dp) == 0 else 1
    return jax.shard_map(
        partial(body, nd),
        mesh=mesh,
        in_specs=(
            P("dp", "head", None),
            P("dp"),
            P("dp", None),
            P(),
            P(),
            P(),
            P(),
            P(),
            P(),
            P("dp", "head", None),
        ),
        out_specs=(
            P("dp", "head", None),
            P("dp", "head", None),
            P(None, "dp", None),
            P(None, "dp", None),
            P(None, "dp", None),
            P(None, "dp", None),
            P(None, "dp"),
            P(None, "dp"),
        ),
        check_vma=False,
    )
```
